32 devices in a mesh: slab: 4 (over y, x), row: 4 (over z), col: 2 (over core).
Axes of the slice: x: 2, y: 2, z: 4, core: 2. Of those that a mesh axis runs over, the one named last changes fastest.
Arguments:
- wave: float32 [16, 32, 32, 256], P(None, 'slab', 'row', 'col')
- potential: float32 [32, 32, 256], P('slab', 'row', 'col'), may hold values from -1 to 1
- positions: int32 [3, 256], P(None, ('slab', 'row', 'col')), may hold values from 0 to 255, as said below
- species: int32 [256], P(('slab', 'row', 'col')), may hold values from 0 to 3
- counts: int32 [32], P(('slab', 'row', 'col')), may hold values from 1 to 8, as said below
- offsets: int32 [4, 3, 384], replicated, may hold values from -5 to 5, as said below
- beta: float32 [4, 384], replicated, may hold values from -0.3125 to 0.3125
- coupling: float32 [4], replicated, may hold values from 0.5 to 4
Outputs:
- filtered: float32 [16, 32, 32, 256], P(None, 'slab', 'row', 'col')
- gram: float32 [16, 16], replicated
The draws below stay inside these ranges and needn't reach their ends.
Inputs may be any that keep to these rules, and one draw needn't show every extreme that they name: `positions`: slot j belongs to block j // 8, blocks numbered with the first dimension slowest and the third fastest; its position lies inside that block of 8 x 8 x 128 cells; the first slot sits at the grid's first cell and the last slot at its last cell. `counts`: some block has all 8 slots live. `offsets`: each species' points are distinct lattice points at distance 5 or less from the anchor, and include the six points at distance 5 along the axes.
All inputs are finite; a program needn't handle non-finite values.
Results may differ from the reference program's by a relative error of at most 0.000086.
Values sent between devices are 32-bit elements; how exact they have to be, the bound alone decides.
A program may use at most 192 MiB of HBM per device.

```python
import math
import jax
import jax.numpy as jnp
import numpy as np
from jax import lax

BANDS = 16
SPECIES = 4
POINTS = 384
CX = 8
CY = 8
CZ = 128
ACAP = 8
NX = 32
NY = 32
NZ = 256
ATOMS = 256


ball_reach = 5


def ball_table():
    axis_points = []
    other_points = []
    for step_x in range(-ball_reach, ball_reach + 1):
        for step_y in range(-ball_reach, ball_reach + 1):
            for step_z in range(-ball_reach, ball_reach + 1):
                radius_sq = step_x * step_x + step_y * step_y + step_z * step_z
                if radius_sq <= ball_reach * ball_reach:
                    if radius_sq == ball_reach * ball_reach and (abs(step_x) == ball_reach or abs(step_y) == ball_reach or abs(step_z) == ball_reach):
                        axis_points.append((step_x, step_y, step_z))
                    else:
                        other_points.append((step_x, step_y, step_z))
    return np.array(axis_points + other_points, dtype=np.int32)


def draw_wave(key, part):
    key = jax.random.fold_in(key, 11)
    noise_key = jax.random.fold_in(key, 0)
    noise = jax.random.normal(noise_key, (BANDS, NX, NY, NZ), jnp.float32)
    depth = jnp.arange(NX, dtype=jnp.float32) / (NX - 1)
    envelope = (1.0 + 2.0 * depth)[None, :, None, None]
    return noise * envelope


def draw_positions(key, part):
    key = jax.random.fold_in(key, 12)
    blocks = NX // CX * (NY // CY) * (NZ // CZ)
    total = ACAP * blocks
    slots = jnp.arange(total, dtype=jnp.int32)
    owner = slots // ACAP
    columns = NZ // CZ
    rows = NY // CY
    block_x = owner // (rows * columns)
    block_y = owner // columns % rows
    block_z = owner % columns
    key_x, key_y, key_z = jax.random.split(key, 3)
    place_x = block_x * CX + jax.random.randint(key_x, (total,), 0, CX)
    place_y = block_y * CY + jax.random.randint(key_y, (total,), 0, CY)
    place_z = block_z * CZ + jax.random.randint(key_z, (total,), 0, CZ)
    placed = jnp.stack([place_x, place_y, place_z]).astype(jnp.int32)
    placed = placed.at[:, 0].set(jnp.zeros((3,), jnp.int32))
    placed = placed.at[:, total - 1].set(jnp.array([NX - 1, NY - 1, NZ - 1], dtype=jnp.int32))
    return placed.astype(jnp.int32)


def draw_counts(key, part):
    key = jax.random.fold_in(key, 13)
    blocks = NX // CX * (NY // CY) * (NZ // CZ)
    first_key, second_key = jax.random.split(key)
    drawn = jax.random.randint(first_key, (blocks,), 1, ACAP + 1)
    chosen = jax.random.randint(second_key, (), 0, blocks)
    return drawn.at[chosen].set(ACAP).astype(jnp.int32)


def draw_offsets(key, part):
    key = jax.random.fold_in(key, 14)
    table = jnp.asarray(ball_table())
    remaining = table.shape[0] - 6
    stacked = []
    for kind in range(SPECIES):
        order = jax.random.permutation(jax.random.fold_in(key, kind), remaining)[:POINTS - 6] + 6
        chosen = jnp.concatenate([jnp.arange(6, dtype=jnp.int32), order.astype(jnp.int32)])
        stacked.append(table[chosen].T)
    return jnp.stack(stacked).astype(jnp.int32)


def plant(values, own_key, low, top_value):
    index_at = [jax.random.randint(jax.random.fold_in(own_key, axis), (), 0, length) for axis, length in enumerate(values.shape)]
    main_axis = values.shape.index(max(values.shape))
    next_to = index_at[:main_axis] + [(index_at[main_axis] + 1) % values.shape[main_axis]] + index_at[main_axis + 1:]
    return values.at[tuple(index_at)].set(low).at[tuple(next_to)].set(top_value)


def levels(own_key, shape, cuts, low, top_value):
    loudness = 1.0
    for position, parts in cuts:
        draws = jax.random.uniform(jax.random.fold_in(jax.random.fold_in(own_key, 6), position), (parts,), jnp.float32, low / len(cuts), top_value / len(cuts))
        loudness = loudness * jnp.repeat(jnp.exp(draws), shape[position] // parts).reshape((-1,) + (1,) * (len(shape) - 1 - position))
    return loudness


def bell_draw(own_key, shape, scale, most, kind=jnp.bfloat16):
    values = scale * jax.random.normal(own_key, shape, jnp.float32)
    return jnp.clip(values, min=-most, max=most).astype(kind)


def setup_inputs(seed: int = 0) -> dict:
    streams_of = jax.random.split(jax.random.key(seed), 9)
    return {
        "wave": draw_wave(jax.random.fold_in(streams_of[8], 71), 0),
        "potential": jnp.clip(jax.random.uniform(streams_of[1], (NX, NY, NZ), jnp.float32, -1.0, 1.0) * levels(streams_of[1], (NX, NY, NZ), ((0, 4), (1, 4), (2, 2)), -0.4, 0.0), -1.0, 1.0),
        "positions": draw_positions(jax.random.fold_in(streams_of[8], 71), 0),
        "species": plant(jax.random.randint(streams_of[3], (ATOMS,), 0, SPECIES), jax.random.fold_in(streams_of[3], 1), 0, SPECIES - 1).astype(jnp.int32),
        "counts": draw_counts(jax.random.fold_in(streams_of[8], 71), 0),
        "offsets": draw_offsets(jax.random.fold_in(streams_of[8], 71), 0),
        "beta": bell_draw(streams_of[6], (SPECIES, POINTS), POINTS ** -0.5, 0.3125, jnp.float32),
        "coupling": jnp.clip(jnp.exp(jax.random.uniform(streams_of[7], (SPECIES,), jnp.float32, math.log(0.5), math.log(4.0))), 0.5, 4.0),
    }


stencil_weights = (-5369.0 / 1800.0, 12.0 / 7.0, -15.0 / 56.0, 10.0 / 189.0, -1.0 / 112.0, 2.0 / 1925.0, -1.0 / 16632.0)
lower_edge = 3.0
upper_edge = 17.0


def stencil(padded, extent):
    size_x, size_y, size_z = extent

    def window(shift_x, shift_y, shift_z):
        return padded[:, 6 + shift_x:6 + shift_x + size_x, 6 + shift_y:6 + shift_y + size_y, 6 + shift_z:6 + shift_z + size_z]

    total = (3.0 * stencil_weights[0]) * window(0, 0, 0)
    for reach in range(1, 7):
        paired = window(reach, 0, 0) + window(-reach, 0, 0) + window(0, reach, 0) + window(0, -reach, 0) + window(0, 0, reach) + window(0, 0, -reach)
        total = total + stencil_weights[reach] * paired
    return total


def nonlocal_term(field, positions, species, counts, offsets, beta, coupling):
    bands = field.shape[0]
    atoms = positions.shape[1]
    slots = jnp.arange(atoms, dtype=jnp.int32)
    active = (slots % ACAP < counts[slots // ACAP]).astype(jnp.float32)
    points = positions.T[:, :, None] + offsets[species]
    limits = jnp.array([NX, NY, NZ], dtype=jnp.int32)[None, :, None]
    inside = jnp.all((points >= 0) & (points < limits), axis=1)
    flat_index = (points[:, 0] * NY + points[:, 1]) * NZ + points[:, 2]
    flat_index = jnp.where(inside, flat_index, NX * NY * NZ).astype(jnp.int32).reshape(-1)
    values = field.reshape(bands, -1)
    picked = jnp.take(values, flat_index, axis=1, mode="fill", fill_value=0.0).reshape(bands, atoms, -1)
    shapes = beta[species]
    projected = jnp.sum(picked * shapes[None], axis=2)
    scaled = projected * (coupling[species] * active)[None]
    spread = (scaled[:, :, None] * shapes[None]).reshape(bands, -1)
    result = jnp.zeros_like(values).at[:, flat_index].add(spread, mode="drop")
    return result.reshape(field.shape)


def reference(wave, potential, positions, species, counts, offsets, beta, coupling):
    centre = 0.5 * (upper_edge + lower_edge)
    half_width = 0.5 * (upper_edge - lower_edge)

    def filter_step(field):
        padded = jnp.pad(field, ((0, 0), (6, 6), (6, 6), (6, 6)))
        applied = -0.5 * stencil(padded, field.shape[1:]) + potential[None] * field
        applied = applied + nonlocal_term(field, positions, species, counts, offsets, beta, coupling)
        return (applied - centre * field) / half_width

    first = filter_step(wave)
    second = 2.0 * filter_step(first) - wave
    third = 2.0 * filter_step(second) - first
    flattened = third.reshape(third.shape[0], -1)
    gram = jnp.dot(flattened, flattened.T, precision=lax.Precision.HIGHEST) / (NX * NY * NZ)
    return third, gram
```

```python
import jax
import jax.numpy as jnp
import ml_dtypes
import numpy as np
from jax import lax
from jax.experimental import pallas as pl
from jax.experimental.pallas import tpu as pltpu
from jax.sharding import PartitionSpec as P

stencil_weights = (
    -5369.0 / 1800.0,
    12.0 / 7.0,
    -15.0 / 56.0,
    10.0 / 189.0,
    -1.0 / 112.0,
    2.0 / 1925.0,
    -1.0 / 16632.0,
)
lower_edge = 3.0
upper_edge = 17.0


def padded_2(block, sides, width):
    for axis, dim in sides:
        count = lax.axis_size(axis)
        forward = [(i, i + 1) for i in range(count - 1)]
        backward = [(target, source) for source, target in forward]
        low = lax.ppermute(
            lax.slice_in_dim(block, block.shape[dim] - width, None, axis=dim), axis, forward
        )
        high = lax.ppermute(lax.slice_in_dim(block, 0, width, axis=dim), axis, backward)
        block = jnp.concatenate([low, block, high], axis=dim)
    return block


def stencil(padded, extent):
    size_x, size_y, size_z = extent

    def window(shift_x, shift_y, shift_z):
        return padded[
            :,
            6 + shift_x : 6 + shift_x + size_x,
            6 + shift_y : 6 + shift_y + size_y,
            6 + shift_z : 6 + shift_z + size_z,
        ]

    total = 3.0 * stencil_weights[0] * window(0, 0, 0)
    for reach in range(1, 7):
        paired = (
            window(reach, 0, 0)
            + window(-reach, 0, 0)
            + window(0, reach, 0)
            + window(0, -reach, 0)
            + window(0, 0, reach)
            + window(0, 0, -reach)
        )
        total = total + stencil_weights[reach] * paired
    return total


def atom_tables(species, offsets, beta, coupling):
    matches = species[:, None] == jnp.arange(beta.shape[0], dtype=jnp.int32)[None]
    onehot = matches.astype(jnp.float32)
    shapes = jnp.dot(onehot, beta, precision=lax.Precision.HIGHEST)
    gains = jnp.sum(onehot * coupling[None], axis=1)
    offset_rows = jnp.sum(jnp.where(matches[:, :, None, None], offsets[None], 0), axis=1)
    return (shapes, offset_rows, gains)


def add_rims(accumulated, received, axis_dim):
    length = accumulated.shape[axis_dim]
    inner = lax.slice_in_dim(accumulated, 6, length - 6, axis=axis_dim)
    lower_part = lax.slice_in_dim(received, 0, 6, axis=axis_dim)
    upper_part = lax.slice_in_dim(received, 18, 24, axis=axis_dim)
    leading = [slice(None)] * 4
    leading[axis_dim] = slice(0, 6)
    inner = inner.at[tuple(leading)].add(lower_part)
    trailing = [slice(None)] * 4
    trailing[axis_dim] = slice(length - 18, length - 12)
    return inner.at[tuple(trailing)].add(upper_part)


def shards(wave, potential, positions, species, counts, offsets, beta, coupling):
    bands, size_x, size_y, size_z = wave.shape
    extent = (size_x, size_y, size_z)
    wide_x, wide_y, wide_z = (size_x + 12, size_y + 12, size_z + 12)
    anchor = jnp.stack(
        [
            lax.axis_index("slab") * size_x,
            lax.axis_index("row") * size_y,
            lax.axis_index("col") * size_z,
        ]
    )
    slot_count = positions.shape[1]
    own_shapes, own_offsets, own_gains = atom_tables(species, offsets, beta, coupling)
    active = (jnp.arange(slot_count, dtype=jnp.int32) < counts[0]).astype(jnp.float32)
    own_weights = own_gains * active
    local = positions.T[:, :, None] - anchor[None, :, None] + own_offsets + 6
    ext_index = ((local[:, 0] * wide_y + local[:, 1]) * wide_z + local[:, 2]).reshape(-1)
    centre = 0.5 * (upper_edge + lower_edge)
    half_width = 0.5 * (upper_edge - lower_edge)

    def spread_rims(scaled):
        contributions = (scaled[:, :, None] * own_shapes[None]).reshape(bands, -1)
        accumulated = (
            jnp.zeros((bands, wide_x * wide_y * wide_z), jnp.float32)
            .at[:, ext_index]
            .add(contributions)
        )
        accumulated = accumulated.reshape(bands, wide_x, wide_y, wide_z)
        rims = jnp.concatenate([accumulated[:, :6], accumulated[:, -6:]], axis=1)
        received = padded_2(rims, (("slab", 1),), 6)
        accumulated = add_rims(accumulated, received, 1)
        rims = jnp.concatenate([accumulated[:, :, :6], accumulated[:, :, -6:]], axis=2)
        received = padded_2(rims, (("row", 2),), 6)
        accumulated = add_rims(accumulated, received, 2)
        rims = jnp.concatenate([accumulated[:, :, :, :6], accumulated[:, :, :, -6:]], axis=3)
        received = padded_2(rims, (("col", 3),), 6)
        return add_rims(accumulated, received, 3)

    def filter_step(field):
        padded = padded_2(field, (("slab", 1), ("row", 2), ("col", 3)), 6)
        picked = jnp.take(padded.reshape(bands, -1), ext_index, axis=1).reshape(
            bands, slot_count, -1
        )
        projected = jnp.sum(picked * own_shapes[None], axis=2)
        scaled = projected * own_weights[None]
        projector_part = spread_rims(scaled)
        applied = -0.5 * stencil(padded, extent) + potential[None] * field + projector_part
        return (applied - centre * field) / half_width

    first = filter_step(wave)
    second = 2.0 * filter_step(first) - wave
    third = 2.0 * filter_step(second) - first
    flattened = third.reshape(bands, -1)
    partial_gram = jnp.dot(flattened, flattened.T, precision=lax.Precision.HIGHEST)
    summed_gram = lax.psum(partial_gram, ("slab", "row", "col"))
    cells_total = (
        size_x
        * size_y
        * size_z
        * lax.axis_size("slab")
        * lax.axis_size("row")
        * lax.axis_size("col")
    )
    return (third, summed_gram / cells_total)


side = 32
lanes = 128
per_group = lanes // side
groups = side // per_group
margin = 32
low_groups = 2
low_rows = 16
box = 16
unroll = 8
centre = 0.5 * (upper_edge + lower_edge)
half_width = 0.5 * (upper_edge - lower_edge)
MESH = pl.DeviceIdType.MESH


def plane_matrices():
    span = 2 * per_group
    full = np.zeros((2 * span * side, 2 * span * side), np.float64)
    index = np.arange(2 * span * side)
    x, y = index // side, index % side
    dx = np.abs(x[:, None] - x[None])
    dy = np.abs(y[:, None] - y[None])
    for reach in range(1, 7):
        near = ((dx == reach) & (dy == 0)) | ((dx == 0) & (dy == reach))
        full[near] = -0.5 / half_width * stencil_weights[reach]
    cut = span * side
    parts = []
    for part in (full[:cut, :cut], full[:cut, cut:], full[cut:, :cut]):
        high = part.astype(ml_dtypes.bfloat16)
        parts += [high, (part - high.astype(np.float64)).astype(ml_dtypes.bfloat16)]
    return np.stack(parts)


def spread_kernel(
    rows, wave, potential, info, field_out, potential_out, atoms_out,
    got, own, halo, listed, local_sem, send_sem, recv_sem, pair_send, pair_recv,
):
    bands = wave.shape[0]
    slab, row, col = (lax.axis_index(name) for name in ("slab", "row", "col"))
    me = slab * rows + row
    other = (slab, row, 1 - col)

    def partner(step):
        target = lax.rem(me + step, bands)
        return target, (target // rows, lax.rem(target, rows), col)

    barrier = pltpu.get_barrier_semaphore()
    for step in range(1, bands):
        pl.semaphore_signal(barrier, inc=1, device_id=partner(step)[1], device_id_type=MESH)
    pl.semaphore_signal(barrier, inc=1, device_id=other, device_id_type=MESH)
    pl.semaphore_wait(barrier, bands)

    copies = [
        pltpu.make_async_copy(wave.at[me], got.at[0, me], local_sem.at[0]),
        pltpu.make_async_copy(potential, got.at[1, me], local_sem.at[1]),
        pltpu.make_async_copy(info, listed.at[col, me], local_sem.at[2]),
    ]
    for step in range(1, bands):
        target, device = partner(step)
        pairs = ((wave.at[target], got.at[0, me]), (potential, got.at[1, me]), (info, listed.at[col, me]))
        for kind, (source, place) in enumerate(pairs):
            copies.append(
                pltpu.make_async_remote_copy(
                    src_ref=source,
                    dst_ref=place,
                    send_sem=send_sem.at[kind, step],
                    recv_sem=recv_sem.at[kind, step],
                    device_id=device,
                    device_id_type=MESH,
                )
            )
    for copy in copies:
        copy.start()
    for copy in copies:
        copy.wait()

    for kind in range(2):
        for group in range(groups):
            tiles = [
                got[kind, group // 2 * rows + r, group % 2 * per_group + x]
                for x in range(per_group)
                for r in range(rows)
            ]
            own[kind, group] = jnp.concatenate(tiles, axis=0).T

    start = pl.multiple_of((1 - col) * (own.shape[2] - margin), margin)
    pairs = ((own.at[:, :, pl.ds(start, margin)], halo), (listed.at[col], listed.at[col]))
    copies = []
    for kind, (source, place) in enumerate(pairs):
        copies.append(
            pltpu.make_async_remote_copy(
                src_ref=source,
                dst_ref=place,
                send_sem=pair_send.at[kind],
                recv_sem=pair_recv.at[kind],
                device_id=other,
                device_id_type=MESH,
            )
        )
    for copy in copies:
        copy.start()
    own_at = pl.multiple_of(col * margin, margin)
    halo_at = pl.multiple_of((1 - col) * own.shape[2], margin)
    outs = (field_out, potential_out)
    for kind in range(2):
        outs[kind][:, pl.ds(own_at, own.shape[2]), :] = own[kind]
    for copy in copies:
        copy.wait()
    for kind in range(2):
        outs[kind][:, pl.ds(halo_at, margin), :] = halo[kind]
    atoms_out[...] = listed[...]


def filter_kernel(
    rows, atoms, coupling, field, potential, offsets, beta, matrices, out,
    ping, pong, plane, high, low, tables, shapes, found, weights,
):
    window = field.shape[1]
    depth = out.shape[3]
    slots = 8
    col = lax.axis_index("col")
    window_start = col * (depth - margin)
    inner = pl.ds(low_rows, window)

    def clear_rims(ref):
        ref[:low_groups] = jnp.zeros((low_groups,) + ref.shape[1:], jnp.float32)
        ref[low_groups + groups :] = jnp.zeros((low_groups,) + ref.shape[1:], jnp.float32)
        middle = pl.ds(low_groups, groups)
        ref[middle, :low_rows] = jnp.zeros((groups, low_rows, lanes), jnp.float32)
        ref[middle, low_rows + window :] = jnp.zeros((groups, low_rows, lanes), jnp.float32)

    clear_rims(ping)
    ping[pl.ds(low_groups, groups), inner] = field[...]

    for kind in range(beta.shape[0]):
        points = beta.shape[1]
        dx = offsets[kind, 0:1, :] + 5
        dy = offsets[kind, 1:2, :] + 5
        dz = offsets[kind, 2:3, :] + 5
        value = beta[kind : kind + 1, :]
        first = value.astype(jnp.bfloat16).astype(jnp.float32)
        second = (value - first).astype(jnp.bfloat16).astype(jnp.float32)
        third = value - first - second
        for phase in range(per_group):
            moved = dx + phase
            place = (moved // per_group) * box + dz
            lane = (moved % per_group) * side + dy
            hit = lax.broadcasted_iota(jnp.int32, (4 * box, points), 0) == place
            left = jnp.concatenate([jnp.where(hit, part, 0.0) for part in (first, second, third)], axis=0)
            right = (lax.broadcasted_iota(jnp.int32, (lanes, points), 0) == lane).astype(jnp.float32)
            dense = lax.dot_general(
                left.astype(jnp.bfloat16),
                right.astype(jnp.bfloat16),
                (((1,), (1,)), ((), ())),
                preferred_element_type=jnp.float32,
            )
            tables[kind * per_group + phase] = (
                dense[: 4 * box] + dense[4 * box : 8 * box] + dense[8 * box :]
            )

    lane_y = lax.broadcasted_iota(jnp.int32, (4 * box, lanes), 1) % side

    def find(slot, count):
        block, place = slot // slots, lax.rem(slot, slots)
        x, y, z, kind, live = (atoms[block, 0, word * slots + place] for word in range(5))
        local = z - window_start
        wanted = (live > 0) & (local >= -5) & (local <= window + 4)

        @pl.when(wanted)
        def _():
            found[0, count] = (x + 3) // per_group
            found[1, count] = local - 5 + low_rows
            weights[count] = coupling[kind] / half_width
            table = tables[kind * per_group + lax.rem(x + 3, per_group)]
            start = y - 5
            rolled = pltpu.roll(table, lax.rem(start + lanes, lanes), 1)
            shapes[count] = jnp.where((lane_y >= start) & (lane_y <= start + 10), rolled, 0.0)

        return count + wanted.astype(jnp.int32)

    count = lax.fori_loop(0, atoms.shape[0] * slots, find, jnp.int32(0))
    for extra in range(unroll):
        found[0, count + extra] = 0
        found[1, count + extra] = 0
        weights[count + extra] = 0.0
        shapes[count + extra] = jnp.zeros((4 * box, lanes), jnp.float32)
    batches = (count + unroll - 1) // unroll

    def step(source, target, scale, keep):
        for tile in range(groups // 2):
            wide = jnp.concatenate(
                [source[low_groups + 2 * tile, inner], source[low_groups + 2 * tile + 1, inner]], axis=1
            )
            big = wide.astype(jnp.bfloat16)
            high[pl.ds(tile * window, window)] = big
            low[pl.ds(tile * window, window)] = (wide - big.astype(jnp.float32)).astype(jnp.bfloat16)
        total = groups // 2 * window

        def product(part, which, begin, end):
            return jnp.dot(part[begin:end], matrices[which], preferred_element_type=jnp.float32)

        def triple(which, begin, end):
            return (
                product(high, which, begin, end)
                + product(low, which, begin, end)
                + product(high, which + 1, begin, end)
            )

        plane[...] = triple(0, 0, total)
        plane[window:] += triple(2, 0, total - window)
        plane[: total - window] += triple(4, window, total)

        for group in range(groups):
            padded = low_groups + group
            diagonal = (potential[group] - (centre + 1.5 * stencil_weights[0])) / half_width
            value = diagonal * source[padded, inner]
            for reach in range(1, 7):
                value = value + (-0.5 / half_width * stencil_weights[reach]) * (
                    source[padded, pl.ds(low_rows + reach, window)]
                    + source[padded, pl.ds(low_rows - reach, window)]
                )
            half = group % 2 * lanes
            value = value + plane[pl.ds(group // 2 * window, window), half : half + lanes]
            if keep:
                value = scale * value - target[padded, inner]
            target[padded, inner] = value

        def batch(index, carry):
            base = index * unroll
            gains = []
            for extra in range(unroll):
                atom = base + extra
                group, at = found[0, atom], found[1, atom]
                total = jnp.zeros((box, lanes), jnp.float32)
                for part in range(4):
                    total = total + source[group + part, pl.ds(at, box)] * shapes[atom, pl.ds(part * box, box)]
                summed = jnp.sum(jnp.sum(total, axis=0, keepdims=True), axis=1, keepdims=True)
                gains.append(summed * (weights[atom] * scale))
            for extra in range(unroll):
                atom = base + extra
                group, at = found[0, atom], found[1, atom]
                for part in range(4):
                    target[group + part, pl.ds(at, box)] += gains[extra] * shapes[atom, pl.ds(part * box, box)]
            return carry

        lax.fori_loop(0, batches, batch, 0)
        clear_rims(target)

    step(ping, pong, 1.0, False)
    step(pong, ping, 2.0, True)
    step(ping, pong, 2.0, True)

    begin = pl.multiple_of(low_rows + col * margin, 16)
    for group in range(groups):
        turned = pong[low_groups + group, pl.ds(begin, depth), :].T
        for x in range(per_group):
            for r in range(rows):
                at = (x * rows + r) * 8
                out[group // 2 * rows + r, group % 2 * per_group + x] = turned[at : at + 8]


def collect_kernel(
    shape, cells, pieces, block, gram, partial, sums, local_sem, send_sem, recv_sem, sum_send, sum_recv
):
    slabs, rows, cols = shape
    bands = pieces.shape[0]
    devices = slabs * rows * cols
    slab, row, col = (lax.axis_index(name) for name in ("slab", "row", "col"))
    me = slab * rows + row
    mine = me * cols + col

    def partner(step):
        target = lax.rem(mine + step, devices)
        return (target // (rows * cols), lax.rem(target // cols, rows), lax.rem(target, cols))

    barrier = pltpu.get_barrier_semaphore()
    for step in range(1, devices):
        pl.semaphore_signal(barrier, inc=1, device_id=partner(step), device_id_type=MESH)
    pl.semaphore_wait(barrier, devices - 1)

    copies = [pltpu.make_async_copy(pieces.at[me], block.at[me], local_sem)]
    for step in range(1, bands):
        target = lax.rem(me + step, bands)
        copies.append(
            pltpu.make_async_remote_copy(
                src_ref=pieces.at[target],
                dst_ref=block.at[me],
                send_sem=send_sem.at[step],
                recv_sem=recv_sem.at[step],
                device_id=(target // rows, lax.rem(target, rows), col),
                device_id_type=MESH,
            )
        )
    for copy in copies:
        copy.start()
    for copy in copies:
        copy.wait()

    size_x, size_y, depth = block.shape[1:]
    flat = bands * size_y
    product = jnp.zeros((flat, flat), jnp.float32)
    for x in range(size_x):
        part = block[:, x].reshape(flat, depth)
        product = product + lax.dot_general(
            part,
            part,
            (((1,), (1,)), ((), ())),
            precision=lax.Precision.HIGHEST,
            preferred_element_type=jnp.float32,
        )
    one = lax.broadcasted_iota(jnp.int32, (flat, flat), 0)
    two = lax.broadcasted_iota(jnp.int32, (flat, flat), 1)
    product = jnp.where(one % size_y == two % size_y, product, 0.0)
    pick = (
        lax.broadcasted_iota(jnp.int32, (bands, flat), 0)
        == lax.broadcasted_iota(jnp.int32, (bands, flat), 1) // size_y
    ).astype(jnp.float32)
    pick_back = (one // size_y == two).astype(jnp.float32)
    folded = jnp.dot(pick, product, precision=lax.Precision.HIGHEST, preferred_element_type=jnp.float32)
    folded = jnp.dot(folded, pick_back, precision=lax.Precision.HIGHEST, preferred_element_type=jnp.float32)
    partial[...] = folded
    sums[mine] = folded
    copies = []
    for step in range(1, devices):
        copies.append(
            pltpu.make_async_remote_copy(
                src_ref=partial,
                dst_ref=sums.at[mine],
                send_sem=sum_send.at[step],
                recv_sem=sum_recv.at[step],
                device_id=partner(step),
                device_id_type=MESH,
            )
        )
    for copy in copies:
        copy.start()
    for copy in copies:
        copy.wait()
    gram[...] = jnp.sum(sums[...], axis=0) * (1.0 / cells)


def band_shards(shape, wave, potential, positions, species, counts, offsets, beta, coupling):
    slabs, rows, cols = shape
    bands, size_x, size_y, size_z = wave.shape
    slots = positions.shape[1]
    window = size_z + margin
    vmem = pl.BlockSpec(memory_space=pltpu.VMEM)
    smem = pl.BlockSpec(memory_space=pltpu.SMEM)
    live = (jnp.arange(slots, dtype=jnp.int32) < counts[0]).astype(jnp.int32)
    info = jnp.concatenate([positions.reshape(-1), species, live])
    info = jnp.pad(info, (0, lanes - info.shape[0])).reshape(1, lanes)
    dma = pltpu.SemaphoreType.DMA
    field, wide_potential, atoms = pl.pallas_call(
        lambda *refs: spread_kernel(rows, *refs),
        out_shape=(
            jax.ShapeDtypeStruct((groups, window, lanes), jnp.float32),
            jax.ShapeDtypeStruct((groups, window, lanes), jnp.float32),
            jax.ShapeDtypeStruct((cols, bands, 1, lanes), jnp.int32),
        ),
        in_specs=[vmem] * 3,
        out_specs=[vmem] * 3,
        scratch_shapes=[
            pltpu.VMEM((2, bands, size_x, size_y, size_z), jnp.float32),
            pltpu.VMEM((2, groups, size_z, lanes), jnp.float32),
            pltpu.VMEM((2, groups, margin, lanes), jnp.float32),
            pltpu.VMEM((cols, bands, 1, lanes), jnp.int32),
            dma((3,)),
            dma((3, bands)),
            dma((3, bands)),
            dma((2,)),
            dma((2,)),
        ],
        compiler_params=pltpu.CompilerParams(
            collective_id=0, has_side_effects=True, vmem_limit_bytes=32 * 2**20
        ),
        name="spread",
    )(wave, potential, info)

    most = bands * cols * slots + unroll
    pieces = pl.pallas_call(
        lambda *refs: filter_kernel(rows, *refs),
        out_shape=jax.ShapeDtypeStruct(wave.shape, jnp.float32),
        in_specs=[smem, smem] + [vmem] * 5,
        out_specs=vmem,
        scratch_shapes=[
            pltpu.VMEM((groups + 2 * low_groups, window + 2 * low_rows, lanes), jnp.float32),
            pltpu.VMEM((groups + 2 * low_groups, window + 2 * low_rows, lanes), jnp.float32),
            pltpu.VMEM((groups // 2 * window, 2 * lanes), jnp.float32),
            pltpu.VMEM((groups // 2 * window, 2 * lanes), jnp.bfloat16),
            pltpu.VMEM((groups // 2 * window, 2 * lanes), jnp.bfloat16),
            pltpu.VMEM((beta.shape[0] * per_group, 4 * box, lanes), jnp.float32),
            pltpu.VMEM((most, 4 * box, lanes), jnp.float32),
            pltpu.SMEM((2, most), jnp.int32),
            pltpu.SMEM((most,), jnp.float32),
        ],
        compiler_params=pltpu.CompilerParams(vmem_limit_bytes=40 * 2**20),
        name="chebyshev",
    )(
        atoms.reshape(cols * bands, 1, lanes),
        coupling,
        field,
        wide_potential,
        offsets,
        beta,
        jnp.asarray(plane_matrices()),
    )

    devices = slabs * rows * cols
    cells = devices * size_x * size_y * size_z
    filtered, gram = pl.pallas_call(
        lambda *refs: collect_kernel(shape, cells, *refs),
        out_shape=(
            jax.ShapeDtypeStruct(wave.shape, jnp.float32),
            jax.ShapeDtypeStruct((bands, lanes), jnp.float32),
        ),
        in_specs=[vmem],
        out_specs=[vmem] * 2,
        scratch_shapes=[
            pltpu.VMEM((bands, lanes), jnp.float32),
            pltpu.VMEM((devices, bands, lanes), jnp.float32),
            dma,
            dma((bands,)),
            dma((bands,)),
            dma((devices,)),
            dma((devices,)),
        ],
        compiler_params=pltpu.CompilerParams(
            collective_id=1, has_side_effects=True, vmem_limit_bytes=32 * 2**20
        ),
        name="collect",
    )(pieces)
    return filtered, gram[:, :bands]


def solution(mesh):
    in_specs = (
        P(None, "slab", "row", "col"),
        P("slab", "row", "col"),
        P(None, ("slab", "row", "col")),
        P(("slab", "row", "col")),
        P(("slab", "row", "col")),
        P(),
        P(),
        P(),
    )
    out_specs = (P(None, "slab", "row", "col"), P())
    shape = tuple(mesh.shape[name] for name in ("slab", "row", "col"))

    def run(*arrays):
        bands, size_x, size_y, size_z = arrays[0].shape
        one_band_a_chip = (
            shape[0] * shape[1] == bands
            and shape[2] == 2
            and (size_x, size_y, size_z) == (shape[0] * 8, shape[1] * 8, 2 * lanes)
            and (size_x, size_y) == (side, side)
            and arrays[2].shape[1] == 8 * mesh.size
        )
        body = (lambda *blocks: band_shards(shape, *blocks)) if one_band_a_chip else shards
        return jax.shard_map(
            body, mesh=mesh, in_specs=in_specs, out_specs=out_specs, check_vma=False
        )(*arrays)

    return run
```

```python
import jax
import jax.numpy as jnp
import ml_dtypes
import numpy as np
from jax import lax
from jax.experimental import pallas as pl
from jax.experimental.pallas import tpu as pltpu
from jax.sharding import PartitionSpec as P

stencil_weights = (
    -5369.0 / 1800.0,
    12.0 / 7.0,
    -15.0 / 56.0,
    10.0 / 189.0,
    -1.0 / 112.0,
    2.0 / 1925.0,
    -1.0 / 16632.0,
)
lower_edge = 3.0
upper_edge = 17.0


def padded_2(block, sides, width):
    for axis, dim in sides:
        count = lax.axis_size(axis)
        forward = [(i, i + 1) for i in range(count - 1)]
        backward = [(target, source) for source, target in forward]
        low = lax.ppermute(
            lax.slice_in_dim(block, block.shape[dim] - width, None, axis=dim), axis, forward
        )
        high = lax.ppermute(lax.slice_in_dim(block, 0, width, axis=dim), axis, backward)
        block = jnp.concatenate([low, block, high], axis=dim)
    return block


def stencil(padded, extent):
    size_x, size_y, size_z = extent

    def window(shift_x, shift_y, shift_z):
        return padded[
            :,
            6 + shift_x : 6 + shift_x + size_x,
            6 + shift_y : 6 + shift_y + size_y,
            6 + shift_z : 6 + shift_z + size_z,
        ]

    total = 3.0 * stencil_weights[0] * window(0, 0, 0)
    for reach in range(1, 7):
        paired = (
            window(reach, 0, 0)
            + window(-reach, 0, 0)
            + window(0, reach, 0)
            + window(0, -reach, 0)
            + window(0, 0, reach)
            + window(0, 0, -reach)
        )
        total = total + stencil_weights[reach] * paired
    return total


def atom_tables(species, offsets, beta, coupling):
    matches = species[:, None] == jnp.arange(beta.shape[0], dtype=jnp.int32)[None]
    onehot = matches.astype(jnp.float32)
    shapes = jnp.dot(onehot, beta, precision=lax.Precision.HIGHEST)
    gains = jnp.sum(onehot * coupling[None], axis=1)
    offset_rows = jnp.sum(jnp.where(matches[:, :, None, None], offsets[None], 0), axis=1)
    return (shapes, offset_rows, gains)


def add_rims(accumulated, received, axis_dim):
    length = accumulated.shape[axis_dim]
    inner = lax.slice_in_dim(accumulated, 6, length - 6, axis=axis_dim)
    lower_part = lax.slice_in_dim(received, 0, 6, axis=axis_dim)
    upper_part = lax.slice_in_dim(received, 18, 24, axis=axis_dim)
    leading = [slice(None)] * 4
    leading[axis_dim] = slice(0, 6)
    inner = inner.at[tuple(leading)].add(lower_part)
    trailing = [slice(None)] * 4
    trailing[axis_dim] = slice(length - 18, length - 12)
    return inner.at[tuple(trailing)].add(upper_part)


def shards(wave, potential, positions, species, counts, offsets, beta, coupling):
    bands, size_x, size_y, size_z = wave.shape
    extent = (size_x, size_y, size_z)
    wide_x, wide_y, wide_z = (size_x + 12, size_y + 12, size_z + 12)
    anchor = jnp.stack(
        [
            lax.axis_index("slab") * size_x,
            lax.axis_index("row") * size_y,
            lax.axis_index("col") * size_z,
        ]
    )
    slot_count = positions.shape[1]
    own_shapes, own_offsets, own_gains = atom_tables(species, offsets, beta, coupling)
    active = (jnp.arange(slot_count, dtype=jnp.int32) < counts[0]).astype(jnp.float32)
    own_weights = own_gains * active
    local = positions.T[:, :, None] - anchor[None, :, None] + own_offsets + 6
    ext_index = ((local[:, 0] * wide_y + local[:, 1]) * wide_z + local[:, 2]).reshape(-1)
    centre = 0.5 * (upper_edge + lower_edge)
    half_width = 0.5 * (upper_edge - lower_edge)

    def spread_rims(scaled):
        contributions = (scaled[:, :, None] * own_shapes[None]).reshape(bands, -1)
        accumulated = (
            jnp.zeros((bands, wide_x * wide_y * wide_z), jnp.float32)
            .at[:, ext_index]
            .add(contributions)
        )
        accumulated = accumulated.reshape(bands, wide_x, wide_y, wide_z)
        rims = jnp.concatenate([accumulated[:, :6], accumulated[:, -6:]], axis=1)
        received = padded_2(rims, (("slab", 1),), 6)
        accumulated = add_rims(accumulated, received, 1)
        rims = jnp.concatenate([accumulated[:, :, :6], accumulated[:, :, -6:]], axis=2)
        received = padded_2(rims, (("row", 2),), 6)
        accumulated = add_rims(accumulated, received, 2)
        rims = jnp.concatenate([accumulated[:, :, :, :6], accumulated[:, :, :, -6:]], axis=3)
        received = padded_2(rims, (("col", 3),), 6)
        return add_rims(accumulated, received, 3)

    def filter_step(field):
        padded = padded_2(field, (("slab", 1), ("row", 2), ("col", 3)), 6)
        picked = jnp.take(padded.reshape(bands, -1), ext_index, axis=1).reshape(
            bands, slot_count, -1
        )
        projected = jnp.sum(picked * own_shapes[None], axis=2)
        scaled = projected * own_weights[None]
        projector_part = spread_rims(scaled)
        applied = -0.5 * stencil(padded, extent) + potential[None] * field + projector_part
        return (applied - centre * field) / half_width

    first = filter_step(wave)
    second = 2.0 * filter_step(first) - wave
    third = 2.0 * filter_step(second) - first
    flattened = third.reshape(bands, -1)
    partial_gram = jnp.dot(flattened, flattened.T, precision=lax.Precision.HIGHEST)
    summed_gram = lax.psum(partial_gram, ("slab", "row", "col"))
    cells_total = (
        size_x
        * size_y
        * size_z
        * lax.axis_size("slab")
        * lax.axis_size("row")
        * lax.axis_size("col")
    )
    return (third, summed_gram / cells_total)


side = 32
lanes = 128
per_group = lanes // side
groups = side // per_group
margin = 32
low_groups = 2
low_rows = 16
box = 16
unroll = 8
centre = 0.5 * (upper_edge + lower_edge)
half_width = 0.5 * (upper_edge - lower_edge)
MESH = pl.DeviceIdType.MESH


def plane_matrices():
    span = 2 * per_group
    full = np.zeros((2 * span * side, 2 * span * side), np.float64)
    index = np.arange(2 * span * side)
    x, y = index // side, index % side
    dx = np.abs(x[:, None] - x[None])
    dy = np.abs(y[:, None] - y[None])
    for reach in range(1, 7):
        near = ((dx == reach) & (dy == 0)) | ((dx == 0) & (dy == reach))
        full[near] = -0.5 / half_width * stencil_weights[reach]
    cut = span * side
    parts = []
    for part in (full[:cut, :cut], full[:cut, cut:], full[cut:, :cut]):
        high = part.astype(ml_dtypes.bfloat16)
        parts += [high, (part - high.astype(np.float64)).astype(ml_dtypes.bfloat16)]
    return np.stack(parts)


def split_three(value):
    first = value.astype(jnp.bfloat16).astype(jnp.float32)
    second = (value - first).astype(jnp.bfloat16).astype(jnp.float32)
    return (first, second, value - first - second)


def build_tables(offsets, beta, tables):
    points = beta.shape[1]
    for kind in range(beta.shape[0]):
        dx = offsets[kind, 0:1, :] + 5
        dy = offsets[kind, 1:2, :] + 5
        dz = offsets[kind, 2:3, :] + 5
        parts = split_three(beta[kind : kind + 1, :])
        for phase in range(per_group):
            moved = dx + phase
            place = (moved // per_group) * box + dz
            lane = (moved % per_group) * side + dy
            hit = lax.broadcasted_iota(jnp.int32, (4 * box, points), 0) == place
            left = jnp.concatenate([jnp.where(hit, part, 0.0) for part in parts], axis=0)
            right = (lax.broadcasted_iota(jnp.int32, (lanes, points), 0) == lane).astype(jnp.float32)
            dense = lax.dot_general(
                left.astype(jnp.bfloat16),
                right.astype(jnp.bfloat16),
                (((1,), (1,)), ((), ())),
                preferred_element_type=jnp.float32,
            )
            tables[kind * per_group + phase] = (
                dense[: 4 * box] + dense[4 * box : 8 * box] + dense[8 * box :]
            )


def spread_kernel(
    shape, wave, potential, positions, species, counts, offsets, beta, field_out, potential_out, atoms_out, tables,
    got, info, local_sem, send_sem, recv_sem, part_send, part_recv, pair_send, pair_recv,
):
    slabs, rows, _ = shape
    depth = wave.shape[3]
    slab, row, col = (lax.axis_index(name) for name in ("slab", "row", "col"))
    me = slab * rows + row
    other = (slab, row, 1 - col)
    shifts = [(s, r) for s in (1, 2, 3, 0) for r in range(rows)]

    def partner(shift):
        return (lax.rem(slab + shift[0], slabs), lax.rem(row + shift[1], rows), col)

    barrier = pltpu.get_barrier_semaphore()
    for shift in shifts:
        if shift != (0, 0):
            pl.semaphore_signal(barrier, inc=1, device_id=partner(shift), device_id_type=MESH)
    pl.semaphore_signal(barrier, inc=1, device_id=other, device_id_type=MESH)

    slots = positions.shape[1]
    live = (lax.broadcasted_iota(jnp.int32, (1, slots), 1) < counts[0]).astype(jnp.int32)
    words = [positions[0:1, :], positions[1:2, :], positions[2:3, :], species[...].reshape(1, slots), live]
    words.append(jnp.zeros((1, lanes - 5 * slots), jnp.int32))
    info[...] = jnp.concatenate(words, axis=1)
    pl.semaphore_wait(barrier, slabs * rows)

    def remote(source, place, send, recv, device):
        copy = pltpu.make_async_remote_copy(
            src_ref=source,
            dst_ref=place,
            send_sem=send,
            recv_sem=recv,
            device_id=device,
            device_id_type=MESH,
        )
        copy.start()
        return copy

    def local(source, place, sem):
        copy = pltpu.make_async_copy(source, place, sem)
        copy.start()
        return copy

    first = [
        local(potential, got.at[1, me], local_sem.at[1]),
        local(info, atoms_out.at[col, me], local_sem.at[2]),
    ]
    for r in range(1, rows):
        device = partner((0, r))
        first.append(remote(potential, got.at[1, me], part_send.at[0, r], part_recv.at[0, r], device))
        first.append(remote(info, atoms_out.at[col, me], part_send.at[1, r], part_recv.at[1, r], device))
    moves = {}
    for index, shift in enumerate(shifts):
        if shift == (0, 0):
            moves[shift] = local(wave.at[me], got.at[0, me], local_sem.at[0])
        else:
            device = partner(shift)
            target = device[0] * rows + device[1]
            moves[shift] = remote(wave.at[target], got.at[0, me], send_sem.at[index], recv_sem.at[index], device)
    for copy in first:
        copy.wait()
    run = pl.ds(slab * rows, rows)
    second = []
    for s in range(1, slabs):
        device = partner((s, 0))
        second.append(remote(got.at[1, run], got.at[1, run], part_send.at[2, s], part_recv.at[2, s], device))
        second.append(
            remote(atoms_out.at[col, run], atoms_out.at[col, run], part_send.at[3, s], part_recv.at[3, s], device)
        )
    build_tables(offsets, beta, tables)
    for copy in second:
        copy.wait()

    own_at = pl.multiple_of(col * margin, margin)
    from_at = pl.multiple_of(col * margin + (1 - col) * (depth - margin), margin)
    to_at = pl.multiple_of(col * depth, margin)

    def turn(kind, out, part):
        for half in range(2):
            tiles = [
                got[kind, part * rows + r, half * per_group + x] for x in range(per_group) for r in range(rows)
            ]
            out[part * 2 + half, pl.ds(own_at, depth), :] = jnp.concatenate(tiles, axis=0).T

    def pass_on(out, part, size, index):
        source = out.at[pl.ds(part * 2, size), pl.ds(from_at, margin), :]
        place = out.at[pl.ds(part * 2, size), pl.ds(to_at, margin), :]
        return remote(source, place, pair_send.at[index], pair_recv.at[index], other)

    last = [remote(atoms_out.at[col], atoms_out.at[col], pair_send.at[0], pair_recv.at[0], other)]
    for part in range(slabs):
        turn(1, potential_out, part)
    last.append(pass_on(potential_out, 0, groups, 1))
    for order, s in enumerate((1, 2, 3, 0)):
        for r in range(rows):
            moves[(s, r)].wait()
        part = lax.rem(slab + (slabs - s), slabs)
        turn(0, field_out, part)
        last.append(pass_on(field_out, part, 2, 2 + order))
    for copy in last:
        copy.wait()


def filter_kernel(
    rows, atoms, coupling, field, potential, tables, matrices_in, out,
    ping, pong, plane, high, low, matrices, shapes, listed, found, weights, matrix_sem,
):
    window = field.shape[1]
    depth = out.shape[3]
    slots = 8
    col = lax.axis_index("col")
    window_start = col * (depth - margin)
    inner = pl.ds(low_rows, window)
    matrix_copy = pltpu.make_async_copy(matrices_in, matrices, matrix_sem)
    matrix_copy.start()

    def clear_rims(ref):
        ref[:low_groups] = jnp.zeros((low_groups,) + ref.shape[1:], jnp.float32)
        ref[low_groups + groups :] = jnp.zeros((low_groups,) + ref.shape[1:], jnp.float32)
        middle = pl.ds(low_groups, groups)
        ref[middle, :low_rows] = jnp.zeros((groups, low_rows, lanes), jnp.float32)
        ref[middle, low_rows + window :] = jnp.zeros((groups, low_rows, lanes), jnp.float32)

    clear_rims(ping)
    ping[pl.ds(low_groups, groups), inner] = field[...]

    lane_y = lax.broadcasted_iota(jnp.int32, (4 * box, lanes), 1) % side

    def find(block, count):
        for place in range(slots):
            local = atoms[block, 0, 2 * slots + place] - window_start
            live = atoms[block, 0, 4 * slots + place]
            listed[count] = block * slots + place
            count = count + jnp.where((local >= -5) & (local <= window + 4), live, 0)
        return count

    count = lax.fori_loop(0, atoms.shape[0], find, jnp.int32(0))
    for extra in range(unroll):
        listed[count + extra] = 0
    batches = (count + unroll - 1) // unroll

    def shape_batch(index, carry):
        for extra in range(unroll):
            atom = index * unroll + extra
            slot = listed[atom]
            block, place = slot // slots, lax.rem(slot, slots)
            x, y, z, kind = (atoms[block, 0, word * slots + place] for word in range(4))
            found[0, atom] = (x + 3) // per_group
            found[1, atom] = jnp.clip(z - window_start, -5, window + 4) - 5 + low_rows
            weights[atom] = jnp.where(atom < count, coupling[kind] / half_width, 0.0)
            start = y - 5
            table = tables[kind * per_group + lax.rem(x + 3, per_group)]
            rolled = pltpu.roll(table, lax.rem(start + lanes, lanes), 1)
            shapes[atom] = jnp.where((lane_y >= start) & (lane_y <= start + 10), rolled, 0.0)
        return carry

    lax.fori_loop(0, batches, shape_batch, 0)
    matrix_copy.wait()

    def step(source, target, scale, keep):
        for tile in range(groups // 2):
            wide = jnp.concatenate(
                [source[low_groups + 2 * tile, inner], source[low_groups + 2 * tile + 1, inner]], axis=1
            )
            big = wide.astype(jnp.bfloat16)
            high[pl.ds(tile * window, window)] = big
            low[pl.ds(tile * window, window)] = (wide - big.astype(jnp.float32)).astype(jnp.bfloat16)
        total = groups // 2 * window

        def product(part, which, begin, end):
            return jnp.dot(part[begin:end], matrices[which], preferred_element_type=jnp.float32)

        def triple(which, begin, end):
            return (
                product(high, which, begin, end)
                + product(low, which, begin, end)
                + product(high, which + 1, begin, end)
            )

        plane[...] = triple(0, 0, total)
        plane[window:] += triple(2, 0, total - window)
        plane[: total - window] += triple(4, window, total)

        for group in range(groups):
            padded = low_groups + group
            diagonal = (potential[group] - (centre + 1.5 * stencil_weights[0])) / half_width
            value = diagonal * source[padded, inner]
            for reach in range(1, 7):
                value = value + (-0.5 / half_width * stencil_weights[reach]) * (
                    source[padded, pl.ds(low_rows + reach, window)]
                    + source[padded, pl.ds(low_rows - reach, window)]
                )
            half = group % 2 * lanes
            value = value + plane[pl.ds(group // 2 * window, window), half : half + lanes]
            if keep:
                value = scale * value - target[padded, inner]
            target[padded, inner] = value

        def batch(index, carry):
            base = index * unroll
            gains = []
            for extra in range(unroll):
                atom = base + extra
                group, at = found[0, atom], found[1, atom]
                total = jnp.zeros((box, lanes), jnp.float32)
                for part in range(4):
                    total = total + source[group + part, pl.ds(at, box)] * shapes[atom, pl.ds(part * box, box)]
                summed = jnp.sum(jnp.sum(total, axis=0, keepdims=True), axis=1, keepdims=True)
                gains.append(summed * (weights[atom] * scale))
            for extra in range(unroll):
                atom = base + extra
                group, at = found[0, atom], found[1, atom]
                for part in range(4):
                    target[group + part, pl.ds(at, box)] += gains[extra] * shapes[atom, pl.ds(part * box, box)]
            return carry

        lax.fori_loop(0, batches, batch, 0)
        clear_rims(target)

    step(ping, pong, 1.0, False)
    step(pong, ping, 2.0, True)
    step(ping, pong, 2.0, True)

    begin = pl.multiple_of(low_rows + col * margin, 16)
    for group in range(groups):
        turned = pong[low_groups + group, pl.ds(begin, depth), :].T
        for x in range(per_group):
            for r in range(rows):
                at = (x * rows + r) * 8
                out[group // 2 * rows + r, group % 2 * per_group + x] = turned[at : at + 8]


def collect_kernel(
    shape, cells, pieces, block, gram, partial, sums, local_sem, send_sem, recv_sem, sum_send, sum_recv
):
    slabs, rows, cols = shape
    bands = pieces.shape[0]
    devices = slabs * rows * cols
    slab, row, col = (lax.axis_index(name) for name in ("slab", "row", "col"))
    me = slab * rows + row
    mine = me * cols + col

    def partner(step):
        target = lax.rem(mine + step, devices)
        return (target // (rows * cols), lax.rem(target // cols, rows), lax.rem(target, cols))

    barrier = pltpu.get_barrier_semaphore()
    for step in range(1, devices):
        pl.semaphore_signal(barrier, inc=1, device_id=partner(step), device_id_type=MESH)
    pl.semaphore_wait(barrier, devices - 1)

    copies = [pltpu.make_async_copy(pieces.at[me], block.at[me], local_sem)]
    for step in range(1, bands):
        target = lax.rem(me + step, bands)
        copies.append(
            pltpu.make_async_remote_copy(
                src_ref=pieces.at[target],
                dst_ref=block.at[me],
                send_sem=send_sem.at[step],
                recv_sem=recv_sem.at[step],
                device_id=(target // rows, lax.rem(target, rows), col),
                device_id_type=MESH,
            )
        )
    for copy in copies:
        copy.start()
    for copy in copies:
        copy.wait()

    size_x, size_y = block.shape[1:3]
    flat = bands * size_y
    wide = jnp.concatenate([block[:, x].reshape(flat, lanes) for x in range(size_x)], axis=1)
    high = wide.astype(jnp.bfloat16)
    low = (wide - high.astype(jnp.float32)).astype(jnp.bfloat16)
    product = lax.dot_general(
        high,
        jnp.concatenate([high, low], axis=0),
        (((1,), (1,)), ((), ())),
        preferred_element_type=jnp.float32,
    )
    cross = product[:, flat:]
    product = product[:, :flat] + cross + cross.T
    one = lax.broadcasted_iota(jnp.int32, (flat, flat), 0)
    two = lax.broadcasted_iota(jnp.int32, (flat, flat), 1)
    product = jnp.where(one % size_y == two % size_y, product, 0.0)
    product = jnp.sum(product.reshape(bands, size_y, flat), axis=1)

    def times(value, picks):
        parts = jnp.concatenate(split_three(value), axis=0).astype(jnp.bfloat16)
        result = jnp.dot(parts, picks.astype(jnp.bfloat16), preferred_element_type=jnp.float32)
        return result[:bands] + result[bands : 2 * bands] + result[2 * bands :]

    folded = times(product, (one // size_y == two % bands).astype(jnp.float32))
    packed = (2, bands // 2, lanes)
    keep = lax.broadcasted_iota(jnp.int32, packed, 1) == lax.broadcasted_iota(jnp.int32, packed, 2) // bands
    partial[...] = jnp.sum(jnp.where(keep, folded.reshape(packed), 0.0), axis=1)
    sums[mine] = partial[...]
    copies = []
    for step in range(1, devices):
        copies.append(
            pltpu.make_async_remote_copy(
                src_ref=partial,
                dst_ref=sums.at[mine],
                send_sem=sum_send.at[step],
                recv_sem=sum_recv.at[step],
                device_id=partner(step),
                device_id_type=MESH,
            )
        )
    for copy in copies:
        copy.start()
    for copy in copies:
        copy.wait()
    total = jnp.sum(sums[...], axis=0) * (1.0 / cells)
    total = jnp.where(keep, jnp.broadcast_to(total[:, None, :], packed), 0.0).reshape(bands, lanes)
    gram[...] = times(total, (one % bands == two).astype(jnp.float32))[:, :bands]


def band_shards(shape, wave, potential, positions, species, counts, offsets, beta, coupling):
    slabs, rows, cols = shape
    bands, size_x, size_y, size_z = wave.shape
    slots = positions.shape[1]
    window = size_z + margin
    vmem = pl.BlockSpec(memory_space=pltpu.VMEM)
    smem = pl.BlockSpec(memory_space=pltpu.SMEM)
    hbm = pl.BlockSpec(memory_space=pltpu.HBM)
    dma = pltpu.SemaphoreType.DMA
    table_count = beta.shape[0] * per_group
    field, wide_potential, atoms, tables = pl.pallas_call(
        lambda *refs: spread_kernel(shape, *refs),
        out_shape=(
            jax.ShapeDtypeStruct((groups, window, lanes), jnp.float32),
            jax.ShapeDtypeStruct((groups, window, lanes), jnp.float32),
            jax.ShapeDtypeStruct((cols, bands, 1, lanes), jnp.int32),
            jax.ShapeDtypeStruct((table_count, 4 * box, lanes), jnp.float32),
        ),
        in_specs=[hbm, hbm, vmem, vmem, smem, vmem, vmem],
        out_specs=[vmem] * 4,
        scratch_shapes=[
            pltpu.VMEM((2, bands, size_x, size_y, size_z), jnp.float32),
            pltpu.VMEM((1, lanes), jnp.int32),
            dma((3,)),
            dma((bands,)),
            dma((bands,)),
            dma((4, 4)),
            dma((4, 4)),
            dma((6,)),
            dma((6,)),
        ],
        compiler_params=pltpu.CompilerParams(
            collective_id=0, has_side_effects=True, vmem_limit_bytes=32 * 2**20
        ),
        name="spread",
    )(wave, potential, positions, species, counts, offsets, beta)

    most = bands * cols * slots + unroll
    pieces = pl.pallas_call(
        lambda *refs: filter_kernel(rows, *refs),
        out_shape=jax.ShapeDtypeStruct(wave.shape, jnp.float32),
        in_specs=[smem, smem, vmem, vmem, vmem, hbm],
        out_specs=vmem,
        scratch_shapes=[
            pltpu.VMEM((groups + 2 * low_groups, window + 2 * low_rows, lanes), jnp.float32),
            pltpu.VMEM((groups + 2 * low_groups, window + 2 * low_rows, lanes), jnp.float32),
            pltpu.VMEM((groups // 2 * window, 2 * lanes), jnp.float32),
            pltpu.VMEM((groups // 2 * window, 2 * lanes), jnp.bfloat16),
            pltpu.VMEM((groups // 2 * window, 2 * lanes), jnp.bfloat16),
            pltpu.VMEM((6, 2 * lanes, 2 * lanes), jnp.bfloat16),
            pltpu.VMEM((most, 4 * box, lanes), jnp.float32),
            pltpu.SMEM((most,), jnp.int32),
            pltpu.SMEM((2, most), jnp.int32),
            pltpu.SMEM((most,), jnp.float32),
            dma,
        ],
        compiler_params=pltpu.CompilerParams(vmem_limit_bytes=40 * 2**20),
        name="chebyshev",
    )(
        atoms.reshape(cols * bands, 1, lanes),
        coupling,
        field,
        wide_potential,
        tables,
        jnp.asarray(plane_matrices()),
    )

    devices = slabs * rows * cols
    cells = devices * size_x * size_y * size_z
    filtered, gram = pl.pallas_call(
        lambda *refs: collect_kernel(shape, cells, *refs),
        out_shape=(
            jax.ShapeDtypeStruct(wave.shape, jnp.float32),
            jax.ShapeDtypeStruct((bands, bands), jnp.float32),
        ),
        in_specs=[vmem],
        out_specs=[vmem] * 2,
        scratch_shapes=[
            pltpu.VMEM((2, lanes), jnp.float32),
            pltpu.VMEM((devices, 2, lanes), jnp.float32),
            dma,
            dma((bands,)),
            dma((bands,)),
            dma((devices,)),
            dma((devices,)),
        ],
        compiler_params=pltpu.CompilerParams(
            collective_id=1, has_side_effects=True, vmem_limit_bytes=32 * 2**20
        ),
        name="collect",
    )(pieces)
    return filtered, gram


def solution(mesh):
    in_specs = (
        P(None, "slab", "row", "col"),
        P("slab", "row", "col"),
        P(None, ("slab", "row", "col")),
        P(("slab", "row", "col")),
        P(("slab", "row", "col")),
        P(),
        P(),
        P(),
    )
    out_specs = (P(None, "slab", "row", "col"), P())
    shape = tuple(mesh.shape[name] for name in ("slab", "row", "col"))

    def run(*arrays):
        bands, size_x, size_y, size_z = arrays[0].shape
        one_band_a_chip = (
            shape[0] * shape[1] == bands
            and shape[2] == 2
            and (size_x, size_y, size_z) == (shape[0] * 8, shape[1] * 8, 2 * lanes)
            and (size_x, size_y) == (side, side)
            and arrays[2].shape[1] == 8 * mesh.size
        )
        body = (lambda *blocks: band_shards(shape, *blocks)) if one_band_a_chip else shards
        return jax.shard_map(
            body, mesh=mesh, in_specs=in_specs, out_specs=out_specs, check_vma=False
        )(*arrays)

    return run
```

```python
import jax
import jax.numpy as jnp
import ml_dtypes
import numpy as np
from jax import lax
from jax.experimental import pallas as pl
from jax.experimental.pallas import tpu as pltpu
from jax.sharding import PartitionSpec as P

stencil_weights = (
    -5369.0 / 1800.0,
    12.0 / 7.0,
    -15.0 / 56.0,
    10.0 / 189.0,
    -1.0 / 112.0,
    2.0 / 1925.0,
    -1.0 / 16632.0,
)
lower_edge = 3.0
upper_edge = 17.0


def padded_2(block, sides, width):
    for axis, dim in sides:
        count = lax.axis_size(axis)
        forward = [(i, i + 1) for i in range(count - 1)]
        backward = [(target, source) for source, target in forward]
        low = lax.ppermute(
            lax.slice_in_dim(block, block.shape[dim] - width, None, axis=dim), axis, forward
        )
        high = lax.ppermute(lax.slice_in_dim(block, 0, width, axis=dim), axis, backward)
        block = jnp.concatenate([low, block, high], axis=dim)
    return block


def stencil(padded, extent):
    size_x, size_y, size_z = extent

    def window(shift_x, shift_y, shift_z):
        return padded[
            :,
            6 + shift_x : 6 + shift_x + size_x,
            6 + shift_y : 6 + shift_y + size_y,
            6 + shift_z : 6 + shift_z + size_z,
        ]

    total = 3.0 * stencil_weights[0] * window(0, 0, 0)
    for reach in range(1, 7):
        paired = (
            window(reach, 0, 0)
            + window(-reach, 0, 0)
            + window(0, reach, 0)
            + window(0, -reach, 0)
            + window(0, 0, reach)
            + window(0, 0, -reach)
        )
        total = total + stencil_weights[reach] * paired
    return total


def atom_tables(species, offsets, beta, coupling):
    matches = species[:, None] == jnp.arange(beta.shape[0], dtype=jnp.int32)[None]
    onehot = matches.astype(jnp.float32)
    shapes = jnp.dot(onehot, beta, precision=lax.Precision.HIGHEST)
    gains = jnp.sum(onehot * coupling[None], axis=1)
    offset_rows = jnp.sum(jnp.where(matches[:, :, None, None], offsets[None], 0), axis=1)
    return (shapes, offset_rows, gains)


def add_rims(accumulated, received, axis_dim):
    length = accumulated.shape[axis_dim]
    inner = lax.slice_in_dim(accumulated, 6, length - 6, axis=axis_dim)
    lower_part = lax.slice_in_dim(received, 0, 6, axis=axis_dim)
    upper_part = lax.slice_in_dim(received, 18, 24, axis=axis_dim)
    leading = [slice(None)] * 4
    leading[axis_dim] = slice(0, 6)
    inner = inner.at[tuple(leading)].add(lower_part)
    trailing = [slice(None)] * 4
    trailing[axis_dim] = slice(length - 18, length - 12)
    return inner.at[tuple(trailing)].add(upper_part)


def shards(wave, potential, positions, species, counts, offsets, beta, coupling):
    bands, size_x, size_y, size_z = wave.shape
    extent = (size_x, size_y, size_z)
    wide_x, wide_y, wide_z = (size_x + 12, size_y + 12, size_z + 12)
    anchor = jnp.stack(
        [
            lax.axis_index("slab") * size_x,
            lax.axis_index("row") * size_y,
            lax.axis_index("col") * size_z,
        ]
    )
    slot_count = positions.shape[1]
    own_shapes, own_offsets, own_gains = atom_tables(species, offsets, beta, coupling)
    active = (jnp.arange(slot_count, dtype=jnp.int32) < counts[0]).astype(jnp.float32)
    own_weights = own_gains * active
    local = positions.T[:, :, None] - anchor[None, :, None] + own_offsets + 6
    ext_index = ((local[:, 0] * wide_y + local[:, 1]) * wide_z + local[:, 2]).reshape(-1)
    centre = 0.5 * (upper_edge + lower_edge)
    half_width = 0.5 * (upper_edge - lower_edge)

    def spread_rims(scaled):
        contributions = (scaled[:, :, None] * own_shapes[None]).reshape(bands, -1)
        accumulated = (
            jnp.zeros((bands, wide_x * wide_y * wide_z), jnp.float32)
            .at[:, ext_index]
            .add(contributions)
        )
        accumulated = accumulated.reshape(bands, wide_x, wide_y, wide_z)
        rims = jnp.concatenate([accumulated[:, :6], accumulated[:, -6:]], axis=1)
        received = padded_2(rims, (("slab", 1),), 6)
        accumulated = add_rims(accumulated, received, 1)
        rims = jnp.concatenate([accumulated[:, :, :6], accumulated[:, :, -6:]], axis=2)
        received = padded_2(rims, (("row", 2),), 6)
        accumulated = add_rims(accumulated, received, 2)
        rims = jnp.concatenate([accumulated[:, :, :, :6], accumulated[:, :, :, -6:]], axis=3)
        received = padded_2(rims, (("col", 3),), 6)
        return add_rims(accumulated, received, 3)

    def filter_step(field):
        padded = padded_2(field, (("slab", 1), ("row", 2), ("col", 3)), 6)
        picked = jnp.take(padded.reshape(bands, -1), ext_index, axis=1).reshape(
            bands, slot_count, -1
        )
        projected = jnp.sum(picked * own_shapes[None], axis=2)
        scaled = projected * own_weights[None]
        projector_part = spread_rims(scaled)
        applied = -0.5 * stencil(padded, extent) + potential[None] * field + projector_part
        return (applied - centre * field) / half_width

    first = filter_step(wave)
    second = 2.0 * filter_step(first) - wave
    third = 2.0 * filter_step(second) - first
    flattened = third.reshape(bands, -1)
    partial_gram = jnp.dot(flattened, flattened.T, precision=lax.Precision.HIGHEST)
    summed_gram = lax.psum(partial_gram, ("slab", "row", "col"))
    cells_total = (
        size_x
        * size_y
        * size_z
        * lax.axis_size("slab")
        * lax.axis_size("row")
        * lax.axis_size("col")
    )
    return (third, summed_gram / cells_total)


side = 32
lanes = 128
per_group = lanes // side
groups = side // per_group
margin = 32
low_groups = 2
low_rows = 16
box = 16
unroll = 8
centre = 0.5 * (upper_edge + lower_edge)
half_width = 0.5 * (upper_edge - lower_edge)
MESH = pl.DeviceIdType.MESH


def build_matrices(matrices):
    span = 2 * per_group
    size = span * side
    one = lax.broadcasted_iota(jnp.int32, (size, size), 0)
    two = lax.broadcasted_iota(jnp.int32, (size, size), 1)
    dy = jnp.abs(one % side - two % side)
    for which, shift in enumerate((0, span, -span)):
        dx = jnp.abs(one // side - two // side - shift)
        distance = jnp.where(dy == 0, dx, jnp.where(dx == 0, dy, 0))
        high = jnp.zeros((size, size), jnp.float32)
        low = jnp.zeros((size, size), jnp.float32)
        for reach in range(1, 7):
            weight = -0.5 / half_width * stencil_weights[reach]
            top = float(np.float32(ml_dtypes.bfloat16(weight)))
            high = jnp.where(distance == reach, top, high)
            low = jnp.where(distance == reach, weight - top, low)
        matrices[2 * which] = high.astype(jnp.bfloat16)
        matrices[2 * which + 1] = low.astype(jnp.bfloat16)


def split_three(value):
    first = value.astype(jnp.bfloat16).astype(jnp.float32)
    second = (value - first).astype(jnp.bfloat16).astype(jnp.float32)
    return (first, second, value - first - second)


def build_tables(offsets, beta, tables):
    points = beta.shape[1]
    for kind in range(beta.shape[0]):
        dx, dy, dz = (offsets[axis, kind : kind + 1, :] + 5 for axis in range(3))
        parts = split_three(beta[kind : kind + 1, :])
        for phase in range(per_group):
            moved = dx + phase
            place = (moved // per_group) * box + dz
            lane = (moved % per_group) * side + dy
            hit = lax.broadcasted_iota(jnp.int32, (4 * box, points), 0) == place
            left = jnp.concatenate([jnp.where(hit, part, 0.0) for part in parts], axis=0)
            right = (lax.broadcasted_iota(jnp.int32, (lanes, points), 0) == lane).astype(jnp.float32)
            dense = lax.dot_general(
                left.astype(jnp.bfloat16),
                right.astype(jnp.bfloat16),
                (((1,), (1,)), ((), ())),
                preferred_element_type=jnp.float32,
            )
            tables[kind * per_group + phase] = (
                dense[: 4 * box] + dense[4 * box : 8 * box] + dense[8 * box :]
            )


def spread_kernel(
    shape, wave, potential, positions, species, counts, offsets, beta, coupling,
    field_out, potential_out, atoms_out, tables, matrices, strengths, got, info, local_sem, send_sem, recv_sem, part_send, part_recv, pair_send, pair_recv,
):
    slabs, rows, _ = shape
    depth = wave.shape[3]
    slab, row, col = (lax.axis_index(name) for name in ("slab", "row", "col"))
    me = slab * rows + row
    other = (slab, row, 1 - col)
    shifts = [(s, r) for s in (1, 2, 3, 0) for r in range(rows)]

    def partner(shift):
        return (lax.rem(slab + shift[0], slabs), lax.rem(row + shift[1], rows), col)

    barrier = pltpu.get_barrier_semaphore()
    for shift in shifts:
        if shift != (0, 0):
            pl.semaphore_signal(barrier, inc=1, device_id=partner(shift), device_id_type=MESH)
    pl.semaphore_signal(barrier, inc=1, device_id=other, device_id_type=MESH)

    slots = positions.shape[1]
    live = (lax.broadcasted_iota(jnp.int32, (1, slots), 1) < counts[0]).astype(jnp.int32)
    words = [positions[0:1, :], positions[1:2, :], positions[2:3, :], species[...].reshape(1, slots), live]
    words.append(jnp.zeros((1, lanes - 5 * slots), jnp.int32))
    info[...] = jnp.concatenate(words, axis=1)
    pl.semaphore_wait(barrier, slabs * rows)

    def remote(source, place, send, recv, device):
        copy = pltpu.make_async_remote_copy(
            src_ref=source,
            dst_ref=place,
            send_sem=send,
            recv_sem=recv,
            device_id=device,
            device_id_type=MESH,
        )
        copy.start()
        return copy

    def local(source, place, sem):
        copy = pltpu.make_async_copy(source, place, sem)
        copy.start()
        return copy

    first = [
        local(potential, got.at[1, me], local_sem.at[1]),
        local(info, atoms_out.at[col, me], local_sem.at[2]),
    ]
    for r in range(1, rows):
        device = partner((0, r))
        first.append(remote(potential, got.at[1, me], part_send.at[0, r], part_recv.at[0, r], device))
        first.append(remote(info, atoms_out.at[col, me], part_send.at[1, r], part_recv.at[1, r], device))
    moves = {}
    for index, shift in enumerate(shifts):
        if shift == (0, 0):
            moves[shift] = local(wave.at[me], got.at[0, me], local_sem.at[0])
        else:
            device = partner(shift)
            target = device[0] * rows + device[1]
            moves[shift] = remote(wave.at[target], got.at[0, me], send_sem.at[index], recv_sem.at[index], device)
    for copy in first:
        copy.wait()
    run = pl.ds(slab * rows, rows)
    second = []
    for s in range(1, slabs):
        device = partner((s, 0))
        second.append(remote(got.at[1, run], got.at[1, run], part_send.at[2, s], part_recv.at[2, s], device))
        second.append(
            remote(atoms_out.at[col, run], atoms_out.at[col, run], part_send.at[3, s], part_recv.at[3, s], device)
        )
    build_tables(offsets, beta, tables)
    build_matrices(matrices)
    kinds = beta.shape[0]
    for kind in range(kinds):
        strengths[kind] = jnp.full((1, lanes), 1.0 / half_width, jnp.float32) * coupling[kind]
    strengths[kinds] = jnp.zeros((1, lanes), jnp.float32)
    for copy in second:
        copy.wait()

    own_at = pl.multiple_of(col * margin, margin)
    from_at = pl.multiple_of(col * margin + (1 - col) * (depth - margin), margin)
    to_at = pl.multiple_of(col * depth, margin)

    def turn(kind, out, part):
        for half in range(2):
            tiles = [
                got[kind, part * rows + r, half * per_group + x] for x in range(per_group) for r in range(rows)
            ]
            out[part * 2 + half, pl.ds(own_at, depth), :] = jnp.concatenate(tiles, axis=0).T

    def pass_on(out, part, size, index):
        source = out.at[pl.ds(part * 2, size), pl.ds(from_at, margin), :]
        place = out.at[pl.ds(part * 2, size), pl.ds(to_at, margin), :]
        return remote(source, place, pair_send.at[index], pair_recv.at[index], other)

    last = [remote(atoms_out.at[col], atoms_out.at[col], pair_send.at[0], pair_recv.at[0], other)]
    for part in range(slabs):
        turn(1, potential_out, part)
    last.append(pass_on(potential_out, 0, groups, 1))
    for order, s in enumerate((1, 2, 3, 0)):
        for r in range(rows):
            moves[(s, r)].wait()
        part = lax.rem(slab + (slabs - s), slabs)
        turn(0, field_out, part)
        last.append(pass_on(field_out, part, 2, 2 + order))
    for copy in last:
        copy.wait()


def plane_part(source, matrices, plane, high, low, window):
    inner = pl.ds(low_rows, window)
    for tile in range(groups // 2):
        wide = jnp.concatenate(
            [source[low_groups + 2 * tile, inner], source[low_groups + 2 * tile + 1, inner]], axis=1
        )
        big = wide.astype(jnp.bfloat16)
        high[pl.ds(tile * window, window)] = big
        low[pl.ds(tile * window, window)] = (wide - big.astype(jnp.float32)).astype(jnp.bfloat16)
    total = groups // 2 * window

    def product(part, which, begin, end):
        return jnp.dot(part[begin:end], matrices[which], preferred_element_type=jnp.float32)

    def triple(which, begin, end):
        return (
            product(high, which, begin, end)
            + product(low, which, begin, end)
            + product(high, which + 1, begin, end)
        )

    plane[...] = triple(0, 0, total)
    plane[window:] += triple(2, 0, total - window)
    plane[: total - window] += triple(4, window, total)


def local_part(source, potential, plane, part, half, window):
    group = 2 * part + half
    padded = low_groups + group
    diagonal = (potential[group] - (centre + 1.5 * stencil_weights[0])) / half_width
    value = diagonal * source[padded, pl.ds(low_rows, window)]
    for reach in range(1, 7):
        value = value + (-0.5 / half_width * stencil_weights[reach]) * (
            source[padded, pl.ds(low_rows + reach, window)] + source[padded, pl.ds(low_rows - reach, window)]
        )
    at = part * window
    if not isinstance(part, int):
        at = pl.multiple_of(at, 32)
    return value + plane[pl.ds(at, window), half * lanes : (half + 1) * lanes]


def filter_kernel(
    depth, atoms, field, potential, tables, matrices, strengths, ping, pong,
    plane, high, low, shapes, listed, found,
):
    window = field.shape[1]
    slots = 8
    col = lax.axis_index("col")
    window_start = col * (depth - margin)
    inner = pl.ds(low_rows, window)

    def clear_rims(ref):
        ref[:low_groups] = jnp.zeros((low_groups,) + ref.shape[1:], jnp.float32)
        ref[low_groups + groups :] = jnp.zeros((low_groups,) + ref.shape[1:], jnp.float32)
        middle = pl.ds(low_groups, groups)
        ref[middle, :low_rows] = jnp.zeros((groups, low_rows, lanes), jnp.float32)
        ref[middle, low_rows + window :] = jnp.zeros((groups, low_rows, lanes), jnp.float32)

    clear_rims(ping)
    ping[pl.ds(low_groups, groups), inner] = field[...]

    lane_y = lax.broadcasted_iota(jnp.int32, (4 * box, lanes), 1) % side

    def find(block, count):
        for place in range(slots):
            local = atoms[block, 0, 2 * slots + place] - window_start
            live = atoms[block, 0, 4 * slots + place]
            listed[count] = block * slots + place
            count = count + jnp.where((local >= -5) & (local <= window + 4), live, 0)
        return count

    count = lax.fori_loop(0, atoms.shape[0], find, jnp.int32(0))
    for extra in range(unroll):
        listed[count + extra] = 0
    batches = jnp.maximum((count + unroll - 1) // unroll, 1)

    def shape_batch(index, carry):
        for extra in range(unroll):
            atom = index * unroll + extra
            slot = listed[atom]
            block, place = slot // slots, lax.rem(slot, slots)
            x, y, z, kind = (atoms[block, 0, word * slots + place] for word in range(4))
            found[0, atom] = (x + 3) // per_group
            found[1, atom] = jnp.clip(z - window_start, -5, window + 4) - 5 + low_rows
            found[2, atom] = jnp.where(atom < count, kind, strengths.shape[0] - 1)
            start = y - 5
            table = tables[kind * per_group + lax.rem(x + 3, per_group)]
            rolled = pltpu.roll(table, lax.rem(start + lanes, lanes), 1)
            shapes[atom] = jnp.where((lane_y >= start) & (lane_y <= start + 10), rolled, 0.0)
        return carry

    lax.fori_loop(0, batches, shape_batch, 0)

    def gather(source, index, scale):
        gains = []
        for extra in range(unroll):
            atom = index * unroll + extra
            group, at = found[0, atom], found[1, atom]
            total = jnp.zeros((box, lanes), jnp.float32)
            for part in range(4):
                total = total + source[group + part, pl.ds(at, box)] * shapes[atom, pl.ds(part * box, box)]
            summed = jnp.sum(jnp.sum(total, axis=0, keepdims=True), axis=1, keepdims=True)
            gains.append(summed * (strengths[found[2, atom]] * scale))
        return tuple(gains)

    def scatter(target, index, gains):
        for extra in range(unroll):
            atom = index * unroll + extra
            group, at = found[0, atom], found[1, atom]
            for part in range(4):
                target[group + part, pl.ds(at, box)] += gains[extra] * shapes[atom, pl.ds(part * box, box)]

    def project(source, target, scale):
        def batch(index, gains):
            later = gather(source, index, scale)
            scatter(target, index - 1, gains)
            return later

        gains = lax.fori_loop(1, batches, batch, gather(source, 0, scale))
        scatter(target, batches - 1, gains)

    def step(source, target, scale, keep):
        plane_part(source, matrices, plane, high, low, window)
        for part in range(groups // 2):
            for half in range(2):
                padded = low_groups + 2 * part + half
                value = local_part(source, potential, plane, part, half, window)
                if keep:
                    value = scale * value - target[padded, inner]
                target[padded, inner] = value
        project(source, target, scale)
        clear_rims(target)

    step(ping, pong, 1.0, False)
    step(pong, ping, 2.0, True)
    middle = pl.ds(low_groups, groups)
    pong[middle, inner] = -pong[middle, inner]
    project(ping, pong, 2.0)


def collect_kernel(
    shape, cells, source, rest, potential, matrices, block, gram,
    plane, high, low, turning, pieces, partial, sums, local_sem, send_sem, recv_sem, sum_send, sum_recv,
):
    slabs, rows, cols = shape
    bands, _, _, depth = block.shape
    window = potential.shape[1]
    devices = slabs * rows * cols
    slab, row, col = (lax.axis_index(name) for name in ("slab", "row", "col"))
    me = slab * rows + row
    mine = me * cols + col

    def partner(step):
        target = lax.rem(mine + step, devices)
        return (target // (rows * cols), lax.rem(target // cols, rows), lax.rem(target, cols))

    barrier = pltpu.get_barrier_semaphore()
    for step in range(1, devices):
        pl.semaphore_signal(barrier, inc=1, device_id=partner(step), device_id_type=MESH)
    plane_part(source, matrices, plane, high, low, window)
    begin = pl.multiple_of(col * margin, margin)
    copies = []
    for order, s in enumerate((1, 2, 3, 0)):
        part = lax.rem(slab + s, slabs)
        for half in range(2):
            padded = low_groups + 2 * part + half
            value = local_part(source, potential, plane, part, half, window)
            turning[half] = 2.0 * value + rest[padded, pl.ds(low_rows, window)]
            turned = turning[half, pl.ds(begin, depth), :].T
            for x in range(per_group):
                for r in range(rows):
                    at = (x * rows + r) * 8
                    pieces[part * rows + r, half * per_group + x] = turned[at : at + 8]
        if order == 0:
            pl.semaphore_wait(barrier, devices - 1)
        for r in range(rows):
            to_row = lax.rem(row + r, rows)
            target = part * rows + to_row
            if s == 0 and r == 0:
                copies.append(pltpu.make_async_copy(pieces.at[me], block.at[me], local_sem))
            else:
                copies.append(
                    pltpu.make_async_remote_copy(
                        src_ref=pieces.at[target],
                        dst_ref=block.at[me],
                        send_sem=send_sem.at[order * rows + r],
                        recv_sem=recv_sem.at[order * rows + r],
                        device_id=(part, to_row, col),
                        device_id_type=MESH,
                    )
                )
            copies[-1].start()
    for copy in copies:
        copy.wait()

    size_x, size_y = block.shape[1:3]
    flat = bands * size_y
    wide = jnp.concatenate([block[:, x].reshape(flat, lanes) for x in range(size_x)], axis=1)
    high = wide.astype(jnp.bfloat16)
    low = (wide - high.astype(jnp.float32)).astype(jnp.bfloat16)
    product = lax.dot_general(
        high,
        jnp.concatenate([high, low], axis=0),
        (((1,), (1,)), ((), ())),
        preferred_element_type=jnp.float32,
    )
    cross = product[:, flat:]
    product = product[:, :flat] + cross + cross.T
    one = lax.broadcasted_iota(jnp.int32, (flat, flat), 0)
    two = lax.broadcasted_iota(jnp.int32, (flat, flat), 1)
    product = jnp.where(one % size_y == two % size_y, product, 0.0)
    product = jnp.sum(product.reshape(bands, size_y, flat), axis=1)

    def times(value, picks):
        parts = jnp.concatenate(split_three(value), axis=0).astype(jnp.bfloat16)
        result = jnp.dot(parts, picks.astype(jnp.bfloat16), preferred_element_type=jnp.float32)
        return result[:bands] + result[bands : 2 * bands] + result[2 * bands :]

    folded = times(product, (one // size_y == two % bands).astype(jnp.float32))
    packed = (2, bands // 2, lanes)
    keep = lax.broadcasted_iota(jnp.int32, packed, 1) == lax.broadcasted_iota(jnp.int32, packed, 2) // bands
    partial[...] = jnp.sum(jnp.where(keep, folded.reshape(packed), 0.0), axis=1)
    sums[mine] = partial[...]
    copies = []
    for step in range(1, devices):
        copies.append(
            pltpu.make_async_remote_copy(
                src_ref=partial,
                dst_ref=sums.at[mine],
                send_sem=sum_send.at[step],
                recv_sem=sum_recv.at[step],
                device_id=partner(step),
                device_id_type=MESH,
            )
        )
    for copy in copies:
        copy.start()
    for copy in copies:
        copy.wait()
    total = jnp.sum(sums[...], axis=0) * (1.0 / cells)
    total = jnp.where(keep, jnp.broadcast_to(total[:, None, :], packed), 0.0).reshape(bands, lanes)
    gram[...] = times(total, (one % bands == two).astype(jnp.float32))[:, :bands]


def band_shards(shape, wave, potential, positions, species, counts, offsets, beta, coupling):
    slabs, rows, cols = shape
    bands, size_x, size_y, size_z = wave.shape
    slots = positions.shape[1]
    window = size_z + margin
    vmem = pl.BlockSpec(memory_space=pltpu.VMEM)
    smem = pl.BlockSpec(memory_space=pltpu.SMEM)
    hbm = pl.BlockSpec(memory_space=pltpu.HBM)
    dma = pltpu.SemaphoreType.DMA
    table_count = beta.shape[0] * per_group
    matrices_shape = jax.ShapeDtypeStruct((6, 2 * lanes, 2 * lanes), jnp.bfloat16)
    field, wide_potential, atoms, tables, matrices, strengths = pl.pallas_call(
        lambda *refs: spread_kernel(shape, *refs),
        out_shape=(
            jax.ShapeDtypeStruct((groups, window, lanes), jnp.float32),
            jax.ShapeDtypeStruct((groups, window, lanes), jnp.float32),
            jax.ShapeDtypeStruct((cols, bands, 1, lanes), jnp.int32),
            jax.ShapeDtypeStruct((table_count, 4 * box, lanes), jnp.float32),
            matrices_shape,
            jax.ShapeDtypeStruct((beta.shape[0] + 1, 1, lanes), jnp.float32),
        ),
        in_specs=[hbm, hbm, vmem, vmem, smem, vmem, vmem, smem],
        out_specs=[vmem] * 6,
        scratch_shapes=[
            pltpu.VMEM((2, bands, size_x, size_y, size_z), jnp.float32),
            pltpu.VMEM((1, lanes), jnp.int32),
            dma((3,)),
            dma((bands,)),
            dma((bands,)),
            dma((4, 4)),
            dma((4, 4)),
            dma((6,)),
            dma((6,)),
        ],
        compiler_params=pltpu.CompilerParams(
            collective_id=0, has_side_effects=True, vmem_limit_bytes=32 * 2**20
        ),
        name="spread",
    )(wave, potential, positions, species, counts, offsets.transpose(1, 0, 2), beta, coupling)

    most = bands * cols * slots + unroll
    padded = jax.ShapeDtypeStruct((groups + 2 * low_groups, window + 2 * low_rows, lanes), jnp.float32)
    plane_scratch = [
        pltpu.VMEM((groups // 2 * window, 2 * lanes), jnp.float32),
        pltpu.VMEM((groups // 2 * window, 2 * lanes), jnp.bfloat16),
        pltpu.VMEM((groups // 2 * window, 2 * lanes), jnp.bfloat16),
    ]
    second, rest = pl.pallas_call(
        lambda *refs: filter_kernel(size_z, *refs),
        out_shape=(padded, padded),
        in_specs=[smem] + [vmem] * 5,
        out_specs=[vmem] * 2,
        scratch_shapes=plane_scratch
        + [
            pltpu.VMEM((most, 4 * box, lanes), jnp.float32),
            pltpu.SMEM((most,), jnp.int32),
            pltpu.SMEM((3, most), jnp.int32),
        ],
        compiler_params=pltpu.CompilerParams(vmem_limit_bytes=40 * 2**20),
        name="chebyshev",
    )(atoms.reshape(cols * bands, 1, lanes), field, wide_potential, tables, matrices, strengths)

    devices = slabs * rows * cols
    cells = devices * size_x * size_y * size_z
    filtered, gram = pl.pallas_call(
        lambda *refs: collect_kernel(shape, cells, *refs),
        out_shape=(
            jax.ShapeDtypeStruct(wave.shape, jnp.float32),
            jax.ShapeDtypeStruct((bands, bands), jnp.float32),
        ),
        in_specs=[vmem] * 4,
        out_specs=[vmem] * 2,
        scratch_shapes=plane_scratch
        + [
            pltpu.VMEM((2, window, lanes), jnp.float32),
            pltpu.VMEM(wave.shape, jnp.float32),
            pltpu.VMEM((2, lanes), jnp.float32),
            pltpu.VMEM((devices, 2, lanes), jnp.float32),
            dma,
            dma((bands,)),
            dma((bands,)),
            dma((devices,)),
            dma((devices,)),
        ],
        compiler_params=pltpu.CompilerParams(
            collective_id=1, has_side_effects=True, vmem_limit_bytes=32 * 2**20
        ),
        name="collect",
    )(second, rest, wide_potential, matrices)
    return filtered, gram


def solution(mesh):
    in_specs = (
        P(None, "slab", "row", "col"),
        P("slab", "row", "col"),
        P(None, ("slab", "row", "col")),
        P(("slab", "row", "col")),
        P(("slab", "row", "col")),
        P(),
        P(),
        P(),
    )
    out_specs = (P(None, "slab", "row", "col"), P())
    shape = tuple(mesh.shape[name] for name in ("slab", "row", "col"))

    def run(*arrays):
        bands, size_x, size_y, size_z = arrays[0].shape
        one_band_a_chip = (
            shape[0] * shape[1] == bands
            and shape[2] == 2
            and (size_x, size_y, size_z) == (shape[0] * 8, shape[1] * 8, 2 * lanes)
            and (size_x, size_y) == (side, side)
            and arrays[2].shape[1] == 8 * mesh.size
        )
        body = (lambda *blocks: band_shards(shape, *blocks)) if one_band_a_chip else shards
        return jax.shard_map(
            body, mesh=mesh, in_specs=in_specs, out_specs=out_specs, check_vma=False
        )(*arrays)

    return run
```

```python
import jax
import jax.numpy as jnp
import ml_dtypes
import numpy as np
from jax import lax
from jax.experimental import pallas as pl
from jax.experimental.pallas import tpu as pltpu
from jax.sharding import PartitionSpec as P

stencil_weights = (
    -5369.0 / 1800.0,
    12.0 / 7.0,
    -15.0 / 56.0,
    10.0 / 189.0,
    -1.0 / 112.0,
    2.0 / 1925.0,
    -1.0 / 16632.0,
)
lower_edge = 3.0
upper_edge = 17.0


def padded_2(block, sides, width):
    for axis, dim in sides:
        count = lax.axis_size(axis)
        forward = [(i, i + 1) for i in range(count - 1)]
        backward = [(target, source) for source, target in forward]
        low = lax.ppermute(
            lax.slice_in_dim(block, block.shape[dim] - width, None, axis=dim), axis, forward
        )
        high = lax.ppermute(lax.slice_in_dim(block, 0, width, axis=dim), axis, backward)
        block = jnp.concatenate([low, block, high], axis=dim)
    return block


def stencil(padded, extent):
    size_x, size_y, size_z = extent

    def window(shift_x, shift_y, shift_z):
        return padded[
            :,
            6 + shift_x : 6 + shift_x + size_x,
            6 + shift_y : 6 + shift_y + size_y,
            6 + shift_z : 6 + shift_z + size_z,
        ]

    total = 3.0 * stencil_weights[0] * window(0, 0, 0)
    for reach in range(1, 7):
        paired = (
            window(reach, 0, 0)
            + window(-reach, 0, 0)
            + window(0, reach, 0)
            + window(0, -reach, 0)
            + window(0, 0, reach)
            + window(0, 0, -reach)
        )
        total = total + stencil_weights[reach] * paired
    return total


def atom_tables(species, offsets, beta, coupling):
    matches = species[:, None] == jnp.arange(beta.shape[0], dtype=jnp.int32)[None]
    onehot = matches.astype(jnp.float32)
    shapes = jnp.dot(onehot, beta, precision=lax.Precision.HIGHEST)
    gains = jnp.sum(onehot * coupling[None], axis=1)
    offset_rows = jnp.sum(jnp.where(matches[:, :, None, None], offsets[None], 0), axis=1)
    return (shapes, offset_rows, gains)


def add_rims(accumulated, received, axis_dim):
    length = accumulated.shape[axis_dim]
    inner = lax.slice_in_dim(accumulated, 6, length - 6, axis=axis_dim)
    lower_part = lax.slice_in_dim(received, 0, 6, axis=axis_dim)
    upper_part = lax.slice_in_dim(received, 18, 24, axis=axis_dim)
    leading = [slice(None)] * 4
    leading[axis_dim] = slice(0, 6)
    inner = inner.at[tuple(leading)].add(lower_part)
    trailing = [slice(None)] * 4
    trailing[axis_dim] = slice(length - 18, length - 12)
    return inner.at[tuple(trailing)].add(upper_part)


def shards(wave, potential, positions, species, counts, offsets, beta, coupling):
    bands, size_x, size_y, size_z = wave.shape
    extent = (size_x, size_y, size_z)
    wide_x, wide_y, wide_z = (size_x + 12, size_y + 12, size_z + 12)
    anchor = jnp.stack(
        [
            lax.axis_index("slab") * size_x,
            lax.axis_index("row") * size_y,
            lax.axis_index("col") * size_z,
        ]
    )
    slot_count = positions.shape[1]
    own_shapes, own_offsets, own_gains = atom_tables(species, offsets, beta, coupling)
    active = (jnp.arange(slot_count, dtype=jnp.int32) < counts[0]).astype(jnp.float32)
    own_weights = own_gains * active
    local = positions.T[:, :, None] - anchor[None, :, None] + own_offsets + 6
    ext_index = ((local[:, 0] * wide_y + local[:, 1]) * wide_z + local[:, 2]).reshape(-1)
    centre = 0.5 * (upper_edge + lower_edge)
    half_width = 0.5 * (upper_edge - lower_edge)

    def spread_rims(scaled):
        contributions = (scaled[:, :, None] * own_shapes[None]).reshape(bands, -1)
        accumulated = (
            jnp.zeros((bands, wide_x * wide_y * wide_z), jnp.float32)
            .at[:, ext_index]
            .add(contributions)
        )
        accumulated = accumulated.reshape(bands, wide_x, wide_y, wide_z)
        rims = jnp.concatenate([accumulated[:, :6], accumulated[:, -6:]], axis=1)
        received = padded_2(rims, (("slab", 1),), 6)
        accumulated = add_rims(accumulated, received, 1)
        rims = jnp.concatenate([accumulated[:, :, :6], accumulated[:, :, -6:]], axis=2)
        received = padded_2(rims, (("row", 2),), 6)
        accumulated = add_rims(accumulated, received, 2)
        rims = jnp.concatenate([accumulated[:, :, :, :6], accumulated[:, :, :, -6:]], axis=3)
        received = padded_2(rims, (("col", 3),), 6)
        return add_rims(accumulated, received, 3)

    def filter_step(field):
        padded = padded_2(field, (("slab", 1), ("row", 2), ("col", 3)), 6)
        picked = jnp.take(padded.reshape(bands, -1), ext_index, axis=1).reshape(
            bands, slot_count, -1
        )
        projected = jnp.sum(picked * own_shapes[None], axis=2)
        scaled = projected * own_weights[None]
        projector_part = spread_rims(scaled)
        applied = -0.5 * stencil(padded, extent) + potential[None] * field + projector_part
        return (applied - centre * field) / half_width

    first = filter_step(wave)
    second = 2.0 * filter_step(first) - wave
    third = 2.0 * filter_step(second) - first
    flattened = third.reshape(bands, -1)
    partial_gram = jnp.dot(flattened, flattened.T, precision=lax.Precision.HIGHEST)
    summed_gram = lax.psum(partial_gram, ("slab", "row", "col"))
    cells_total = (
        size_x
        * size_y
        * size_z
        * lax.axis_size("slab")
        * lax.axis_size("row")
        * lax.axis_size("col")
    )
    return (third, summed_gram / cells_total)


side = 32
lanes = 128
per_group = lanes // side
groups = side // per_group
margin = 32
low_groups = 2
low_rows = 16
box = 16
unroll = 8
centre = 0.5 * (upper_edge + lower_edge)
half_width = 0.5 * (upper_edge - lower_edge)
MESH = pl.DeviceIdType.MESH


def build_matrices(matrices):
    span = 2 * per_group
    size = span * side
    one = lax.broadcasted_iota(jnp.int32, (size, size), 0)
    two = lax.broadcasted_iota(jnp.int32, (size, size), 1)
    dy = jnp.abs(one % side - two % side)
    for which, shift in enumerate((0, span, -span)):
        dx = jnp.abs(one // side - two // side - shift)
        distance = jnp.where(dy == 0, dx, jnp.where(dx == 0, dy, 0))
        high = jnp.zeros((size, size), jnp.float32)
        low = jnp.zeros((size, size), jnp.float32)
        for reach in range(1, 7):
            weight = -0.5 / half_width * stencil_weights[reach]
            top = float(np.float32(ml_dtypes.bfloat16(weight)))
            high = jnp.where(distance == reach, top, high)
            low = jnp.where(distance == reach, weight - top, low)
        for place, part in enumerate((high, high, low)):
            matrices[which, pl.ds(place * size, size)] = part.astype(jnp.bfloat16)


def split_three(value):
    first = value.astype(jnp.bfloat16).astype(jnp.float32)
    second = (value - first).astype(jnp.bfloat16).astype(jnp.float32)
    return (first, second, value - first - second)


def build_tables(offsets, beta, tables):
    points = beta.shape[1]
    for kind in range(beta.shape[0]):
        dx, dy, dz = (offsets[kind, axis : axis + 1, :] + 5 for axis in range(3))
        parts = split_three(beta[kind : kind + 1, :])
        for phase in range(per_group):
            moved = dx + phase
            place = (moved // per_group) * box + dz
            lane = (moved % per_group) * side + dy
            hit = lax.broadcasted_iota(jnp.int32, (4 * box, points), 0) == place
            left = jnp.concatenate([jnp.where(hit, part, 0.0) for part in parts], axis=0)
            right = (lax.broadcasted_iota(jnp.int32, (lanes, points), 0) == lane).astype(jnp.float32)
            dense = lax.dot_general(
                left.astype(jnp.bfloat16),
                right.astype(jnp.bfloat16),
                (((1,), (1,)), ((), ())),
                preferred_element_type=jnp.float32,
            )
            tables[kind * per_group + phase] = (
                dense[: 4 * box] + dense[4 * box : 8 * box] + dense[8 * box :]
            )


def spread_kernel(
    shape, wave, potential, positions, species, counts, offsets, beta, coupling,
    field_out, potential_out, atoms_out, tables, matrices, strengths, got, info, local_sem, send_sem, recv_sem, part_send, part_recv, pair_send, pair_recv,
):
    slabs, rows, _ = shape
    depth = wave.shape[3]
    slab, row, col = (lax.axis_index(name) for name in ("slab", "row", "col"))
    me = slab * rows + row
    other = (slab, row, 1 - col)
    shifts = [(s, r) for s in (1, 2, 3, 0) for r in range(rows)]

    def partner(shift):
        return (lax.rem(slab + shift[0], slabs), lax.rem(row + shift[1], rows), col)

    barrier = pltpu.get_barrier_semaphore()
    for shift in shifts:
        if shift != (0, 0):
            pl.semaphore_signal(barrier, inc=1, device_id=partner(shift), device_id_type=MESH)
    pl.semaphore_signal(barrier, inc=1, device_id=other, device_id_type=MESH)

    slots = positions.shape[1]
    live = (lax.broadcasted_iota(jnp.int32, (1, slots), 1) < counts[0]).astype(jnp.int32)
    words = [positions[0:1, :], positions[1:2, :], positions[2:3, :], species[...].reshape(1, slots), live]
    words.append(jnp.zeros((1, lanes - 5 * slots), jnp.int32))
    info[...] = jnp.concatenate(words, axis=1)
    pl.semaphore_wait(barrier, slabs * rows)

    def remote(source, place, send, recv, device):
        copy = pltpu.make_async_remote_copy(
            src_ref=source,
            dst_ref=place,
            send_sem=send,
            recv_sem=recv,
            device_id=device,
            device_id_type=MESH,
        )
        copy.start()
        return copy

    def local(source, place, sem):
        copy = pltpu.make_async_copy(source, place, sem)
        copy.start()
        return copy

    first = [
        local(potential, got.at[1, me], local_sem.at[1]),
        local(info, atoms_out.at[col, me], local_sem.at[2]),
    ]
    for r in range(1, rows):
        device = partner((0, r))
        first.append(remote(potential, got.at[1, me], part_send.at[0, r], part_recv.at[0, r], device))
        first.append(remote(info, atoms_out.at[col, me], part_send.at[1, r], part_recv.at[1, r], device))
    moves = {}
    for index, shift in enumerate(shifts):
        if shift == (0, 0):
            moves[shift] = local(wave.at[me], got.at[0, me], local_sem.at[0])
        else:
            device = partner(shift)
            target = device[0] * rows + device[1]
            moves[shift] = remote(wave.at[target], got.at[0, me], send_sem.at[index], recv_sem.at[index], device)
    for copy in first:
        copy.wait()
    run = pl.ds(slab * rows, rows)
    second = []
    for s in range(1, slabs):
        device = partner((s, 0))
        second.append(remote(got.at[1, run], got.at[1, run], part_send.at[2, s], part_recv.at[2, s], device))
        second.append(
            remote(atoms_out.at[col, run], atoms_out.at[col, run], part_send.at[3, s], part_recv.at[3, s], device)
        )
    build_tables(offsets, beta, tables)
    build_matrices(matrices)
    kinds = beta.shape[0]
    for kind in range(kinds):
        strengths[kind] = jnp.full((1, lanes), 1.0 / half_width, jnp.float32) * coupling[kind]
    strengths[kinds] = jnp.zeros((1, lanes), jnp.float32)
    for copy in second:
        copy.wait()

    own_at = pl.multiple_of(col * margin, margin)
    from_at = pl.multiple_of(col * margin + (1 - col) * (depth - margin), margin)
    to_at = pl.multiple_of(col * depth, margin)

    def turn(kind, out, part):
        for half in range(2):
            tiles = [
                got[kind, part * rows + r, half * per_group + x] for x in range(per_group) for r in range(rows)
            ]
            out[part * 2 + half, pl.ds(own_at, depth), :] = jnp.concatenate(tiles, axis=0).T

    def pass_on(out, part, size, index):
        source = out.at[pl.ds(part * 2, size), pl.ds(from_at, margin), :]
        place = out.at[pl.ds(part * 2, size), pl.ds(to_at, margin), :]
        return remote(source, place, pair_send.at[index], pair_recv.at[index], other)

    last = [remote(atoms_out.at[col], atoms_out.at[col], pair_send.at[0], pair_recv.at[0], other)]
    for part in range(slabs):
        turn(1, potential_out, part)
    last.append(pass_on(potential_out, 0, groups, 1))
    for order, s in enumerate((1, 2, 3, 0)):
        for r in range(rows):
            moves[(s, r)].wait()
        part = lax.rem(slab + (slabs - s), slabs)
        turn(0, field_out, part)
        last.append(pass_on(field_out, part, 2, 2 + order))
    for copy in last:
        copy.wait()


def plane_part(source, matrices, plane, split, window):
    inner = pl.ds(low_rows, window)
    for tile in range(groups // 2):
        wide = jnp.concatenate(
            [source[low_groups + 2 * tile, inner], source[low_groups + 2 * tile + 1, inner]], axis=1
        )
        big = wide.astype(jnp.bfloat16)
        rows = pl.ds(tile * window, window)
        split[rows, : 2 * lanes] = big
        split[rows, 2 * lanes : 4 * lanes] = (wide - big.astype(jnp.float32)).astype(jnp.bfloat16)
        split[rows, 4 * lanes :] = big
    total = groups // 2 * window

    def product(which, begin, end):
        return jnp.dot(split[begin:end], matrices[which], preferred_element_type=jnp.float32)

    plane[...] = product(0, 0, total)
    plane[window:] += product(1, 0, total - window)
    plane[: total - window] += product(2, window, total)


def local_part(source, potential, plane, part, half, window):
    group = 2 * part + half
    padded = low_groups + group
    diagonal = (potential[group] - (centre + 1.5 * stencil_weights[0])) / half_width
    value = diagonal * source[padded, pl.ds(low_rows, window)]
    for reach in range(1, 7):
        value = value + (-0.5 / half_width * stencil_weights[reach]) * (
            source[padded, pl.ds(low_rows + reach, window)] + source[padded, pl.ds(low_rows - reach, window)]
        )
    at = part * window
    if not isinstance(part, int):
        at = pl.multiple_of(at, 32)
    return value + plane[pl.ds(at, window), half * lanes : (half + 1) * lanes]


def filter_kernel(
    depth, atoms, field, potential, tables, matrices, strengths, ping, pong,
    plane, split, shapes, listed, found,
):
    window = field.shape[1]
    slots = 8
    col = lax.axis_index("col")
    window_start = col * (depth - margin)
    inner = pl.ds(low_rows, window)

    def clear_rims(ref):
        ref[:low_groups] = jnp.zeros((low_groups,) + ref.shape[1:], jnp.float32)
        ref[low_groups + groups :] = jnp.zeros((low_groups,) + ref.shape[1:], jnp.float32)
        middle = pl.ds(low_groups, groups)
        ref[middle, :low_rows] = jnp.zeros((groups, low_rows, lanes), jnp.float32)
        ref[middle, low_rows + window :] = jnp.zeros((groups, low_rows, lanes), jnp.float32)

    clear_rims(ping)
    ping[pl.ds(low_groups, groups), inner] = field[...]

    lane_y = lax.broadcasted_iota(jnp.int32, (4 * box, lanes), 1) % side

    def find(block, count):
        for place in range(slots):
            local = atoms[block, 0, 2 * slots + place] - window_start
            live = atoms[block, 0, 4 * slots + place]
            listed[count] = block * slots + place
            count = count + jnp.where((local >= -5) & (local <= window + 4), live, 0)
        return count

    count = lax.fori_loop(0, atoms.shape[0], find, jnp.int32(0))
    for extra in range(unroll):
        listed[count + extra] = 0
    batches = jnp.maximum((count + unroll - 1) // unroll, 1)

    def shape_batch(index, carry):
        for extra in range(unroll):
            atom = index * unroll + extra
            slot = listed[atom]
            block, place = slot // slots, lax.rem(slot, slots)
            x, y, z, kind = (atoms[block, 0, word * slots + place] for word in range(4))
            found[0, atom] = (x + 3) // per_group
            found[1, atom] = jnp.clip(z - window_start, -5, window + 4) - 5 + low_rows
            found[2, atom] = jnp.where(atom < count, kind, strengths.shape[0] - 1)
            start = y - 5
            table = tables[kind * per_group + lax.rem(x + 3, per_group)]
            rolled = pltpu.roll(table, lax.rem(start + lanes, lanes), 1)
            shapes[atom] = jnp.where((lane_y >= start) & (lane_y <= start + 10), rolled, 0.0)
        return carry

    lax.fori_loop(0, batches, shape_batch, 0)

    def gather(source, index, scale):
        gains = []
        for extra in range(unroll):
            atom = index * unroll + extra
            group, at = found[0, atom], found[1, atom]
            total = jnp.zeros((box, lanes), jnp.float32)
            for part in range(4):
                total = total + source[group + part, pl.ds(at, box)] * shapes[atom, pl.ds(part * box, box)]
            summed = jnp.sum(jnp.sum(total, axis=0, keepdims=True), axis=1, keepdims=True)
            gains.append(summed * (strengths[found[2, atom]] * scale))
        return tuple(gains)

    def scatter(target, index, gains):
        for extra in range(unroll):
            atom = index * unroll + extra
            group, at = found[0, atom], found[1, atom]
            for part in range(4):
                target[group + part, pl.ds(at, box)] += gains[extra] * shapes[atom, pl.ds(part * box, box)]

    def project(source, target, scale):
        def batch(index, gains):
            later = gather(source, index, scale)
            scatter(target, index - 1, gains)
            return later

        gains = lax.fori_loop(1, batches, batch, gather(source, 0, scale))
        scatter(target, batches - 1, gains)

    def step(source, target, scale, keep):
        plane_part(source, matrices, plane, split, window)
        for part in range(groups // 2):
            for half in range(2):
                padded = low_groups + 2 * part + half
                value = local_part(source, potential, plane, part, half, window)
                if keep:
                    value = scale * value - target[padded, inner]
                target[padded, inner] = value
        project(source, target, scale)
        clear_rims(target)

    step(ping, pong, 1.0, False)
    step(pong, ping, 2.0, True)
    middle = pl.ds(low_groups, groups)
    pong[middle, inner] = -pong[middle, inner]
    project(ping, pong, 2.0)


def collect_kernel(
    shape, cells, source, rest, potential, matrices, block, gram,
    plane, split, turning, pieces, partial, sums, local_sem, send_sem, recv_sem, sum_send, sum_recv,
):
    slabs, rows, cols = shape
    bands, _, _, depth = block.shape
    window = potential.shape[1]
    devices = slabs * rows * cols
    slab, row, col = (lax.axis_index(name) for name in ("slab", "row", "col"))
    me = slab * rows + row
    mine = me * cols + col

    def partner(step):
        target = lax.rem(mine + step, devices)
        return (target // (rows * cols), lax.rem(target // cols, rows), lax.rem(target, cols))

    barrier = pltpu.get_barrier_semaphore()
    for step in range(1, devices):
        pl.semaphore_signal(barrier, inc=1, device_id=partner(step), device_id_type=MESH)
    plane_part(source, matrices, plane, split, window)
    begin = pl.multiple_of(col * margin, margin)
    copies = []
    for order, s in enumerate((1, 2, 3, 0)):
        part = lax.rem(slab + s, slabs)
        for half in range(2):
            padded = low_groups + 2 * part + half
            value = local_part(source, potential, plane, part, half, window)
            turning[half] = 2.0 * value + rest[padded, pl.ds(low_rows, window)]
            turned = turning[half, pl.ds(begin, depth), :].T
            for x in range(per_group):
                for r in range(rows):
                    at = (x * rows + r) * 8
                    pieces[part * rows + r, half * per_group + x] = turned[at : at + 8]
        if order == 0:
            pl.semaphore_wait(barrier, devices - 1)
        for r in range(rows):
            to_row = lax.rem(row + r, rows)
            target = part * rows + to_row
            if s == 0 and r == 0:
                copies.append(pltpu.make_async_copy(pieces.at[me], block.at[me], local_sem))
            else:
                copies.append(
                    pltpu.make_async_remote_copy(
                        src_ref=pieces.at[target],
                        dst_ref=block.at[me],
                        send_sem=send_sem.at[order * rows + r],
                        recv_sem=recv_sem.at[order * rows + r],
                        device_id=(part, to_row, col),
                        device_id_type=MESH,
                    )
                )
            copies[-1].start()
    for copy in copies:
        copy.wait()

    size_x, size_y = block.shape[1:3]
    flat = bands * size_y
    wide = jnp.concatenate([block[:, x].reshape(flat, lanes) for x in range(size_x)], axis=1)
    high = wide.astype(jnp.bfloat16)
    low = (wide - high.astype(jnp.float32)).astype(jnp.bfloat16)
    product = lax.dot_general(
        high,
        jnp.concatenate([high, low], axis=0),
        (((1,), (1,)), ((), ())),
        preferred_element_type=jnp.float32,
    )
    cross = product[:, flat:]
    product = product[:, :flat] + cross + cross.T
    one = lax.broadcasted_iota(jnp.int32, (flat, flat), 0)
    two = lax.broadcasted_iota(jnp.int32, (flat, flat), 1)
    product = jnp.where(one % size_y == two % size_y, product, 0.0)
    product = jnp.sum(product.reshape(bands, size_y, flat), axis=1)

    def times(value, picks):
        parts = jnp.concatenate(split_three(value), axis=0).astype(jnp.bfloat16)
        result = jnp.dot(parts, picks.astype(jnp.bfloat16), preferred_element_type=jnp.float32)
        return result[:bands] + result[bands : 2 * bands] + result[2 * bands :]

    folded = times(product, (one // size_y == two % bands).astype(jnp.float32))
    packed = (2, bands // 2, lanes)
    keep = lax.broadcasted_iota(jnp.int32, packed, 1) == lax.broadcasted_iota(jnp.int32, packed, 2) // bands
    partial[...] = jnp.sum(jnp.where(keep, folded.reshape(packed), 0.0), axis=1)
    sums[mine] = partial[...]
    copies = []
    for step in range(1, devices):
        copies.append(
            pltpu.make_async_remote_copy(
                src_ref=partial,
                dst_ref=sums.at[mine],
                send_sem=sum_send.at[step],
                recv_sem=sum_recv.at[step],
                device_id=partner(step),
                device_id_type=MESH,
            )
        )
    for copy in copies:
        copy.start()
    for copy in copies:
        copy.wait()
    total = jnp.sum(sums[...], axis=0) * (1.0 / cells)
    total = jnp.where(keep, jnp.broadcast_to(total[:, None, :], packed), 0.0).reshape(bands, lanes)
    gram[...] = times(total, (one % bands == two).astype(jnp.float32))[:, :bands]


def band_shards(shape, wave, potential, positions, species, counts, offsets, beta, coupling):
    slabs, rows, cols = shape
    bands, size_x, size_y, size_z = wave.shape
    slots = positions.shape[1]
    window = size_z + margin
    vmem = pl.BlockSpec(memory_space=pltpu.VMEM)
    smem = pl.BlockSpec(memory_space=pltpu.SMEM)
    hbm = pl.BlockSpec(memory_space=pltpu.HBM)
    dma = pltpu.SemaphoreType.DMA
    table_count = beta.shape[0] * per_group
    matrices_shape = jax.ShapeDtypeStruct((3, 6 * lanes, 2 * lanes), jnp.bfloat16)
    field, wide_potential, atoms, tables, matrices, strengths = pl.pallas_call(
        lambda *refs: spread_kernel(shape, *refs),
        out_shape=(
            jax.ShapeDtypeStruct((groups, window, lanes), jnp.float32),
            jax.ShapeDtypeStruct((groups, window, lanes), jnp.float32),
            jax.ShapeDtypeStruct((cols, bands, 1, lanes), jnp.int32),
            jax.ShapeDtypeStruct((table_count, 4 * box, lanes), jnp.float32),
            matrices_shape,
            jax.ShapeDtypeStruct((beta.shape[0] + 1, 1, lanes), jnp.float32),
        ),
        in_specs=[hbm, hbm, vmem, vmem, smem, vmem, vmem, smem],
        out_specs=[vmem] * 6,
        scratch_shapes=[
            pltpu.VMEM((2, bands, size_x, size_y, size_z), jnp.float32),
            pltpu.VMEM((1, lanes), jnp.int32),
            dma((3,)),
            dma((bands,)),
            dma((bands,)),
            dma((4, 4)),
            dma((4, 4)),
            dma((6,)),
            dma((6,)),
        ],
        compiler_params=pltpu.CompilerParams(
            collective_id=0, has_side_effects=True, vmem_limit_bytes=32 * 2**20
        ),
        name="spread",
    )(wave, potential, positions, species, counts, offsets, beta, coupling)

    most = bands * cols * slots + unroll
    padded = jax.ShapeDtypeStruct((groups + 2 * low_groups, window + 2 * low_rows, lanes), jnp.float32)
    plane_scratch = [
        pltpu.VMEM((groups // 2 * window, 2 * lanes), jnp.float32),
        pltpu.VMEM((groups // 2 * window, 6 * lanes), jnp.bfloat16),
    ]
    second, rest = pl.pallas_call(
        lambda *refs: filter_kernel(size_z, *refs),
        out_shape=(padded, padded),
        in_specs=[smem] + [vmem] * 5,
        out_specs=[vmem] * 2,
        scratch_shapes=plane_scratch
        + [
            pltpu.VMEM((most, 4 * box, lanes), jnp.float32),
            pltpu.SMEM((most,), jnp.int32),
            pltpu.SMEM((3, most), jnp.int32),
        ],
        compiler_params=pltpu.CompilerParams(vmem_limit_bytes=40 * 2**20),
        name="chebyshev",
    )(atoms.reshape(cols * bands, 1, lanes), field, wide_potential, tables, matrices, strengths)

    devices = slabs * rows * cols
    cells = devices * size_x * size_y * size_z
    filtered, gram = pl.pallas_call(
        lambda *refs: collect_kernel(shape, cells, *refs),
        out_shape=(
            jax.ShapeDtypeStruct(wave.shape, jnp.float32),
            jax.ShapeDtypeStruct((bands, bands), jnp.float32),
        ),
        in_specs=[vmem] * 4,
        out_specs=[vmem] * 2,
        scratch_shapes=plane_scratch
        + [
            pltpu.VMEM((2, window, lanes), jnp.float32),
            pltpu.VMEM(wave.shape, jnp.float32),
            pltpu.VMEM((2, lanes), jnp.float32),
            pltpu.VMEM((devices, 2, lanes), jnp.float32),
            dma,
            dma((bands,)),
            dma((bands,)),
            dma((devices,)),
            dma((devices,)),
        ],
        compiler_params=pltpu.CompilerParams(
            collective_id=1, has_side_effects=True, vmem_limit_bytes=32 * 2**20
        ),
        name="collect",
    )(second, rest, wide_potential, matrices)
    return filtered, gram


def solution(mesh):
    in_specs = (
        P(None, "slab", "row", "col"),
        P("slab", "row", "col"),
        P(None, ("slab", "row", "col")),
        P(("slab", "row", "col")),
        P(("slab", "row", "col")),
        P(),
        P(),
        P(),
    )
    out_specs = (P(None, "slab", "row", "col"), P())
    shape = tuple(mesh.shape[name] for name in ("slab", "row", "col"))

    def run(*arrays):
        bands, size_x, size_y, size_z = arrays[0].shape
        one_band_a_chip = (
            shape[0] * shape[1] == bands
            and shape[2] == 2
            and (size_x, size_y, size_z) == (shape[0] * 8, shape[1] * 8, 2 * lanes)
            and (size_x, size_y) == (side, side)
            and arrays[2].shape[1] == 8 * mesh.size
        )
        body = (lambda *blocks: band_shards(shape, *blocks)) if one_band_a_chip else shards
        return jax.shard_map(
            body, mesh=mesh, in_specs=in_specs, out_specs=out_specs, check_vma=False
        )(*arrays)

    return run
```

```python
import jax
import jax.numpy as jnp
import ml_dtypes
import numpy as np
from jax import lax
from jax.experimental import pallas as pl
from jax.experimental.pallas import tpu as pltpu
from jax.sharding import PartitionSpec as P

stencil_weights = (
    -5369.0 / 1800.0,
    12.0 / 7.0,
    -15.0 / 56.0,
    10.0 / 189.0,
    -1.0 / 112.0,
    2.0 / 1925.0,
    -1.0 / 16632.0,
)
lower_edge = 3.0
upper_edge = 17.0


def padded_2(block, sides, width):
    for axis, dim in sides:
        count = lax.axis_size(axis)
        forward = [(i, i + 1) for i in range(count - 1)]
        backward = [(target, source) for source, target in forward]
        low = lax.ppermute(
            lax.slice_in_dim(block, block.shape[dim] - width, None, axis=dim), axis, forward
        )
        high = lax.ppermute(lax.slice_in_dim(block, 0, width, axis=dim), axis, backward)
        block = jnp.concatenate([low, block, high], axis=dim)
    return block


def stencil(padded, extent):
    size_x, size_y, size_z = extent

    def window(shift_x, shift_y, shift_z):
        return padded[
            :,
            6 + shift_x : 6 + shift_x + size_x,
            6 + shift_y : 6 + shift_y + size_y,
            6 + shift_z : 6 + shift_z + size_z,
        ]

    total = 3.0 * stencil_weights[0] * window(0, 0, 0)
    for reach in range(1, 7):
        paired = (
            window(reach, 0, 0)
            + window(-reach, 0, 0)
            + window(0, reach, 0)
            + window(0, -reach, 0)
            + window(0, 0, reach)
            + window(0, 0, -reach)
        )
        total = total + stencil_weights[reach] * paired
    return total


def atom_tables(species, offsets, beta, coupling):
    matches = species[:, None] == jnp.arange(beta.shape[0], dtype=jnp.int32)[None]
    onehot = matches.astype(jnp.float32)
    shapes = jnp.dot(onehot, beta, precision=lax.Precision.HIGHEST)
    gains = jnp.sum(onehot * coupling[None], axis=1)
    offset_rows = jnp.sum(jnp.where(matches[:, :, None, None], offsets[None], 0), axis=1)
    return (shapes, offset_rows, gains)


def add_rims(accumulated, received, axis_dim):
    length = accumulated.shape[axis_dim]
    inner = lax.slice_in_dim(accumulated, 6, length - 6, axis=axis_dim)
    lower_part = lax.slice_in_dim(received, 0, 6, axis=axis_dim)
    upper_part = lax.slice_in_dim(received, 18, 24, axis=axis_dim)
    leading = [slice(None)] * 4
    leading[axis_dim] = slice(0, 6)
    inner = inner.at[tuple(leading)].add(lower_part)
    trailing = [slice(None)] * 4
    trailing[axis_dim] = slice(length - 18, length - 12)
    return inner.at[tuple(trailing)].add(upper_part)


def shards(wave, potential, positions, species, counts, offsets, beta, coupling):
    bands, size_x, size_y, size_z = wave.shape
    extent = (size_x, size_y, size_z)
    wide_x, wide_y, wide_z = (size_x + 12, size_y + 12, size_z + 12)
    anchor = jnp.stack(
        [
            lax.axis_index("slab") * size_x,
            lax.axis_index("row") * size_y,
            lax.axis_index("col") * size_z,
        ]
    )
    slot_count = positions.shape[1]
    own_shapes, own_offsets, own_gains = atom_tables(species, offsets, beta, coupling)
    active = (jnp.arange(slot_count, dtype=jnp.int32) < counts[0]).astype(jnp.float32)
    own_weights = own_gains * active
    local = positions.T[:, :, None] - anchor[None, :, None] + own_offsets + 6
    ext_index = ((local[:, 0] * wide_y + local[:, 1]) * wide_z + local[:, 2]).reshape(-1)
    centre = 0.5 * (upper_edge + lower_edge)
    half_width = 0.5 * (upper_edge - lower_edge)

    def spread_rims(scaled):
        contributions = (scaled[:, :, None] * own_shapes[None]).reshape(bands, -1)
        accumulated = (
            jnp.zeros((bands, wide_x * wide_y * wide_z), jnp.float32)
            .at[:, ext_index]
            .add(contributions)
        )
        accumulated = accumulated.reshape(bands, wide_x, wide_y, wide_z)
        rims = jnp.concatenate([accumulated[:, :6], accumulated[:, -6:]], axis=1)
        received = padded_2(rims, (("slab", 1),), 6)
        accumulated = add_rims(accumulated, received, 1)
        rims = jnp.concatenate([accumulated[:, :, :6], accumulated[:, :, -6:]], axis=2)
        received = padded_2(rims, (("row", 2),), 6)
        accumulated = add_rims(accumulated, received, 2)
        rims = jnp.concatenate([accumulated[:, :, :, :6], accumulated[:, :, :, -6:]], axis=3)
        received = padded_2(rims, (("col", 3),), 6)
        return add_rims(accumulated, received, 3)

    def filter_step(field):
        padded = padded_2(field, (("slab", 1), ("row", 2), ("col", 3)), 6)
        picked = jnp.take(padded.reshape(bands, -1), ext_index, axis=1).reshape(
            bands, slot_count, -1
        )
        projected = jnp.sum(picked * own_shapes[None], axis=2)
        scaled = projected * own_weights[None]
        projector_part = spread_rims(scaled)
        applied = -0.5 * stencil(padded, extent) + potential[None] * field + projector_part
        return (applied - centre * field) / half_width

    first = filter_step(wave)
    second = 2.0 * filter_step(first) - wave
    third = 2.0 * filter_step(second) - first
    flattened = third.reshape(bands, -1)
    partial_gram = jnp.dot(flattened, flattened.T, precision=lax.Precision.HIGHEST)
    summed_gram = lax.psum(partial_gram, ("slab", "row", "col"))
    cells_total = (
        size_x
        * size_y
        * size_z
        * lax.axis_size("slab")
        * lax.axis_size("row")
        * lax.axis_size("col")
    )
    return (third, summed_gram / cells_total)


side = 32
lanes = 128
per_group = lanes // side
groups = side // per_group
margin = 32
low_groups = 2
low_rows = 16
box = 16
unroll = 8
centre = 0.5 * (upper_edge + lower_edge)
half_width = 0.5 * (upper_edge - lower_edge)
MESH = pl.DeviceIdType.MESH


def build_matrices(matrices):
    span = 2 * per_group
    size = span * side
    one = lax.broadcasted_iota(jnp.int32, (size, size), 0)
    two = lax.broadcasted_iota(jnp.int32, (size, size), 1)
    dy = jnp.abs(one % side - two % side)
    for which, shift in enumerate((0, span, -span)):
        dx = jnp.abs(one // side - two // side - shift)
        distance = jnp.where(dy == 0, dx, jnp.where(dx == 0, dy, 0))
        high = jnp.zeros((size, size), jnp.float32)
        low = jnp.zeros((size, size), jnp.float32)
        for reach in range(1, 7):
            weight = -0.5 / half_width * stencil_weights[reach]
            top = float(np.float32(ml_dtypes.bfloat16(weight)))
            high = jnp.where(distance == reach, top, high)
            low = jnp.where(distance == reach, weight - top, low)
        matrices[2 * which] = high.astype(jnp.bfloat16)
        matrices[2 * which + 1] = low.astype(jnp.bfloat16)


def split_three(value):
    first = value.astype(jnp.bfloat16).astype(jnp.float32)
    second = (value - first).astype(jnp.bfloat16).astype(jnp.float32)
    return (first, second, value - first - second)


def build_tables(offsets, beta, tables):
    points = beta.shape[1]
    for kind in range(beta.shape[0]):
        dx, dy, dz = (offsets[axis, kind : kind + 1, :] + 5 for axis in range(3))
        parts = split_three(beta[kind : kind + 1, :])
        for phase in range(per_group):
            moved = dx + phase
            place = (moved // per_group) * box + dz
            lane = (moved % per_group) * side + dy
            hit = lax.broadcasted_iota(jnp.int32, (4 * box, points), 0) == place
            left = jnp.concatenate([jnp.where(hit, part, 0.0) for part in parts], axis=0)
            right = (lax.broadcasted_iota(jnp.int32, (lanes, points), 0) == lane).astype(jnp.float32)
            dense = lax.dot_general(
                left.astype(jnp.bfloat16),
                right.astype(jnp.bfloat16),
                (((1,), (1,)), ((), ())),
                preferred_element_type=jnp.float32,
            )
            tables[kind * per_group + phase] = (
                dense[: 4 * box] + dense[4 * box : 8 * box] + dense[8 * box :]
            )


def spread_kernel(
    shape, wave, potential, positions_in, species_in, counts, offsets_in, beta_in, coupling_in,
    field_out, potential_out, atoms_out, tables, matrices, strengths,
    positions, species, offsets, beta, coupling, small_sem, got, info, local_sem, send_sem, recv_sem, part_send, part_recv, pair_send, pair_recv,
):
    slabs, rows, _ = shape
    depth = wave.shape[3]
    slab, row, col = (lax.axis_index(name) for name in ("slab", "row", "col"))
    me = slab * rows + row
    other = (slab, row, 1 - col)
    shifts = [(s, r) for s in (1, 2, 3, 0) for r in range(rows)]

    def partner(shift):
        return (lax.rem(slab + shift[0], slabs), lax.rem(row + shift[1], rows), col)

    small = (
        (positions_in, positions),
        (species_in, species),
        (offsets_in, offsets),
        (beta_in, beta),
        (coupling_in, coupling),
    )
    small = [pltpu.make_async_copy(*pair, small_sem.at[index]) for index, pair in enumerate(small)]
    for copy in small:
        copy.start()
    barrier = pltpu.get_barrier_semaphore()
    for shift in shifts:
        if shift != (0, 0):
            pl.semaphore_signal(barrier, inc=1, device_id=partner(shift), device_id_type=MESH)
    pl.semaphore_signal(barrier, inc=1, device_id=other, device_id_type=MESH)

    for copy in small:
        copy.wait()
    slots = positions.shape[1]
    live = (lax.broadcasted_iota(jnp.int32, (1, slots), 1) < counts[0]).astype(jnp.int32)
    words = [positions[0:1, :], positions[1:2, :], positions[2:3, :], species[...].reshape(1, slots), live]
    words.append(jnp.zeros((1, lanes - 5 * slots), jnp.int32))
    info[...] = jnp.concatenate(words, axis=1)
    pl.semaphore_wait(barrier, slabs * rows)

    def remote(source, place, send, recv, device):
        copy = pltpu.make_async_remote_copy(
            src_ref=source,
            dst_ref=place,
            send_sem=send,
            recv_sem=recv,
            device_id=device,
            device_id_type=MESH,
        )
        copy.start()
        return copy

    def local(source, place, sem):
        copy = pltpu.make_async_copy(source, place, sem)
        copy.start()
        return copy

    first = [
        local(potential, got.at[1, me], local_sem.at[1]),
        local(info, atoms_out.at[col, me], local_sem.at[2]),
    ]
    for r in range(1, rows):
        device = partner((0, r))
        first.append(remote(potential, got.at[1, me], part_send.at[0, r], part_recv.at[0, r], device))
        first.append(remote(info, atoms_out.at[col, me], part_send.at[1, r], part_recv.at[1, r], device))
    moves = {}
    for index, shift in enumerate(shifts):
        if shift == (0, 0):
            moves[shift] = local(wave.at[me], got.at[0, me], local_sem.at[0])
        else:
            device = partner(shift)
            target = device[0] * rows + device[1]
            moves[shift] = remote(wave.at[target], got.at[0, me], send_sem.at[index], recv_sem.at[index], device)
    for copy in first:
        copy.wait()
    run = pl.ds(slab * rows, rows)
    second = []
    for s in range(1, slabs):
        device = partner((s, 0))
        second.append(remote(got.at[1, run], got.at[1, run], part_send.at[2, s], part_recv.at[2, s], device))
        second.append(
            remote(atoms_out.at[col, run], atoms_out.at[col, run], part_send.at[3, s], part_recv.at[3, s], device)
        )
    build_tables(offsets, beta, tables)
    build_matrices(matrices)
    kinds = beta.shape[0]
    for kind in range(kinds):
        strengths[kind] = jnp.full((1, lanes), 1.0 / half_width, jnp.float32) * coupling[kind]
    strengths[kinds] = jnp.zeros((1, lanes), jnp.float32)
    for copy in second:
        copy.wait()

    own_at = pl.multiple_of(col * margin, margin)
    from_at = pl.multiple_of(col * margin + (1 - col) * (depth - margin), margin)
    to_at = pl.multiple_of(col * depth, margin)

    def turn(kind, out, part):
        for half in range(2):
            tiles = [
                got[kind, part * rows + r, half * per_group + x] for x in range(per_group) for r in range(rows)
            ]
            out[part * 2 + half, pl.ds(own_at, depth), :] = jnp.concatenate(tiles, axis=0).T

    def pass_on(out, part, size, index):
        source = out.at[pl.ds(part * 2, size), pl.ds(from_at, margin), :]
        place = out.at[pl.ds(part * 2, size), pl.ds(to_at, margin), :]
        return remote(source, place, pair_send.at[index], pair_recv.at[index], other)

    last = [remote(atoms_out.at[col], atoms_out.at[col], pair_send.at[0], pair_recv.at[0], other)]
    for part in range(slabs):
        turn(1, potential_out, part)
    last.append(pass_on(potential_out, 0, groups, 1))
    for order, s in enumerate((1, 2, 3, 0)):
        for r in range(rows):
            moves[(s, r)].wait()
        part = lax.rem(slab + (slabs - s), slabs)
        turn(0, field_out, part)
        last.append(pass_on(field_out, part, 2, 2 + order))
    for copy in last:
        copy.wait()


def plane_part(source, matrices, plane, high, low, window):
    inner = pl.ds(low_rows, window)
    for tile in range(groups // 2):
        wide = jnp.concatenate(
            [source[low_groups + 2 * tile, inner], source[low_groups + 2 * tile + 1, inner]], axis=1
        )
        big = wide.astype(jnp.bfloat16)
        high[pl.ds(tile * window, window)] = big
        low[pl.ds(tile * window, window)] = (wide - big.astype(jnp.float32)).astype(jnp.bfloat16)
    total = groups // 2 * window

    def product(part, which, begin, end):
        return jnp.dot(part[begin:end], matrices[which], preferred_element_type=jnp.float32)

    def triple(which, begin, end):
        return (
            product(high, which, begin, end)
            + product(low, which, begin, end)
            + product(high, which + 1, begin, end)
        )

    plane[...] = triple(0, 0, total)
    plane[window:] += triple(2, 0, total - window)
    plane[: total - window] += triple(4, window, total)


def local_part(source, potential, plane, part, half, window):
    group = 2 * part + half
    padded = low_groups + group
    diagonal = (potential[group] - (centre + 1.5 * stencil_weights[0])) / half_width
    value = diagonal * source[padded, pl.ds(low_rows, window)]
    for reach in range(1, 7):
        value = value + (-0.5 / half_width * stencil_weights[reach]) * (
            source[padded, pl.ds(low_rows + reach, window)] + source[padded, pl.ds(low_rows - reach, window)]
        )
    at = part * window
    if not isinstance(part, int):
        at = pl.multiple_of(at, 32)
    return value + plane[pl.ds(at, window), half * lanes : (half + 1) * lanes]


def filter_kernel(
    depth, atoms, field, potential, tables, matrices, strengths, ping, pong,
    plane, high, low, shapes, listed, found,
):
    window = field.shape[1]
    slots = 8
    col = lax.axis_index("col")
    window_start = col * (depth - margin)
    inner = pl.ds(low_rows, window)

    def clear_rims(ref):
        ref[:low_groups] = jnp.zeros((low_groups,) + ref.shape[1:], jnp.float32)
        ref[low_groups + groups :] = jnp.zeros((low_groups,) + ref.shape[1:], jnp.float32)
        middle = pl.ds(low_groups, groups)
        ref[middle, :low_rows] = jnp.zeros((groups, low_rows, lanes), jnp.float32)
        ref[middle, low_rows + window :] = jnp.zeros((groups, low_rows, lanes), jnp.float32)

    clear_rims(ping)
    ping[pl.ds(low_groups, groups), inner] = field[...]

    lane_y = lax.broadcasted_iota(jnp.int32, (4 * box, lanes), 1) % side

    def find(block, count):
        for place in range(slots):
            local = atoms[block, 0, 2 * slots + place] - window_start
            live = atoms[block, 0, 4 * slots + place]
            listed[count] = block * slots + place
            count = count + jnp.where((local >= -5) & (local <= window + 4), live, 0)
        return count

    count = lax.fori_loop(0, atoms.shape[0], find, jnp.int32(0))
    for extra in range(unroll):
        listed[count + extra] = 0
    batches = jnp.maximum((count + unroll - 1) // unroll, 1)

    def shape_batch(index, carry):
        for extra in range(unroll):
            atom = index * unroll + extra
            slot = listed[atom]
            block, place = slot // slots, lax.rem(slot, slots)
            x, y, z, kind = (atoms[block, 0, word * slots + place] for word in range(4))
            found[0, atom] = (x + 3) // per_group
            found[1, atom] = jnp.clip(z - window_start, -5, window + 4) - 5 + low_rows
            found[2, atom] = jnp.where(atom < count, kind, strengths.shape[0] - 1)
            start = y - 5
            table = tables[kind * per_group + lax.rem(x + 3, per_group)]
            rolled = pltpu.roll(table, lax.rem(start + lanes, lanes), 1)
            shapes[atom] = jnp.where((lane_y >= start) & (lane_y <= start + 10), rolled, 0.0)
        return carry

    lax.fori_loop(0, batches, shape_batch, 0)

    def gather(source, index, scale):
        gains = []
        for extra in range(unroll):
            atom = index * unroll + extra
            group, at = found[0, atom], found[1, atom]
            total = jnp.zeros((box, lanes), jnp.float32)
            for part in range(4):
                total = total + source[group + part, pl.ds(at, box)] * shapes[atom, pl.ds(part * box, box)]
            summed = jnp.sum(jnp.sum(total, axis=0, keepdims=True), axis=1, keepdims=True)
            gains.append(summed * (strengths[found[2, atom]] * scale))
        return tuple(gains)

    def scatter(target, index, gains):
        for extra in range(unroll):
            atom = index * unroll + extra
            group, at = found[0, atom], found[1, atom]
            for part in range(4):
                target[group + part, pl.ds(at, box)] += gains[extra] * shapes[atom, pl.ds(part * box, box)]

    def project(source, target, scale):
        def batch(index, gains):
            later = gather(source, index, scale)
            scatter(target, index - 1, gains)
            return later

        gains = lax.fori_loop(1, batches, batch, gather(source, 0, scale))
        scatter(target, batches - 1, gains)

    def step(source, target, scale, keep):
        plane_part(source, matrices, plane, high, low, window)
        for part in range(groups // 2):
            for half in range(2):
                padded = low_groups + 2 * part + half
                value = local_part(source, potential, plane, part, half, window)
                if keep:
                    value = scale * value - target[padded, inner]
                target[padded, inner] = value
        project(source, target, scale)
        clear_rims(target)

    step(ping, pong, 1.0, False)
    step(pong, ping, 2.0, True)
    middle = pl.ds(low_groups, groups)
    pong[middle, inner] = -pong[middle, inner]
    project(ping, pong, 2.0)


def collect_kernel(
    shape, cells, source, rest, potential, matrices, block, gram,
    plane, high, low, turning, pieces, partial, sums, local_sem, send_sem, recv_sem, sum_send, sum_recv,
):
    slabs, rows, cols = shape
    bands, _, _, depth = block.shape
    window = potential.shape[1]
    devices = slabs * rows * cols
    slab, row, col = (lax.axis_index(name) for name in ("slab", "row", "col"))
    me = slab * rows + row
    mine = me * cols + col

    def partner(step):
        target = lax.rem(mine + step, devices)
        return (target // (rows * cols), lax.rem(target // cols, rows), lax.rem(target, cols))

    barrier = pltpu.get_barrier_semaphore()
    for step in range(1, devices):
        pl.semaphore_signal(barrier, inc=1, device_id=partner(step), device_id_type=MESH)
    plane_part(source, matrices, plane, high, low, window)
    begin = pl.multiple_of(col * margin, margin)
    copies = []
    for order, s in enumerate((1, 2, 3, 0)):
        part = lax.rem(slab + s, slabs)
        for half in range(2):
            padded = low_groups + 2 * part + half
            value = local_part(source, potential, plane, part, half, window)
            turning[half] = 2.0 * value + rest[padded, pl.ds(low_rows, window)]
            turned = turning[half, pl.ds(begin, depth), :].T
            for x in range(per_group):
                for r in range(rows):
                    at = (x * rows + r) * 8
                    pieces[part * rows + r, half * per_group + x] = turned[at : at + 8]
        if order == 0:
            pl.semaphore_wait(barrier, devices - 1)
        for r in range(rows):
            to_row = lax.rem(row + r, rows)
            target = part * rows + to_row
            if s == 0 and r == 0:
                copies.append(pltpu.make_async_copy(pieces.at[me], block.at[me], local_sem))
            else:
                copies.append(
                    pltpu.make_async_remote_copy(
                        src_ref=pieces.at[target],
                        dst_ref=block.at[me],
                        send_sem=send_sem.at[order * rows + r],
                        recv_sem=recv_sem.at[order * rows + r],
                        device_id=(part, to_row, col),
                        device_id_type=MESH,
                    )
                )
            copies[-1].start()
    for copy in copies:
        copy.wait()

    size_x, size_y = block.shape[1:3]
    flat = bands * size_y
    wide = jnp.concatenate([block[:, x].reshape(flat, lanes) for x in range(size_x)], axis=1)
    high = wide.astype(jnp.bfloat16)
    low = (wide - high.astype(jnp.float32)).astype(jnp.bfloat16)
    product = lax.dot_general(
        high,
        jnp.concatenate([high, low], axis=0),
        (((1,), (1,)), ((), ())),
        preferred_element_type=jnp.float32,
    )
    cross = product[:, flat:]
    product = product[:, :flat] + cross + cross.T
    one = lax.broadcasted_iota(jnp.int32, (flat, flat), 0)
    two = lax.broadcasted_iota(jnp.int32, (flat, flat), 1)
    product = jnp.where(one % size_y == two % size_y, product, 0.0)
    product = jnp.sum(product.reshape(bands, size_y, flat), axis=1)

    def times(value, picks):
        parts = jnp.concatenate(split_three(value), axis=0).astype(jnp.bfloat16)
        result = jnp.dot(parts, picks.astype(jnp.bfloat16), preferred_element_type=jnp.float32)
        return result[:bands] + result[bands : 2 * bands] + result[2 * bands :]

    folded = times(product, (one // size_y == two % bands).astype(jnp.float32))
    packed = (2, bands // 2, lanes)
    keep = lax.broadcasted_iota(jnp.int32, packed, 1) == lax.broadcasted_iota(jnp.int32, packed, 2) // bands
    partial[...] = jnp.sum(jnp.where(keep, folded.reshape(packed), 0.0), axis=1)
    sums[mine] = partial[...]
    copies = []
    for step in range(1, devices):
        copies.append(
            pltpu.make_async_remote_copy(
                src_ref=partial,
                dst_ref=sums.at[mine],
                send_sem=sum_send.at[step],
                recv_sem=sum_recv.at[step],
                device_id=partner(step),
                device_id_type=MESH,
            )
        )
    for copy in copies:
        copy.start()
    for copy in copies:
        copy.wait()
    total = jnp.sum(sums[...], axis=0) * (1.0 / cells)
    total = jnp.where(keep, jnp.broadcast_to(total[:, None, :], packed), 0.0).reshape(bands, lanes)
    gram[...] = times(total, (one % bands == two).astype(jnp.float32))[:, :bands]


def band_shards(shape, wave, potential, positions, species, counts, offsets, beta, coupling):
    slabs, rows, cols = shape
    bands, size_x, size_y, size_z = wave.shape
    slots = positions.shape[1]
    window = size_z + margin
    vmem = pl.BlockSpec(memory_space=pltpu.VMEM)
    smem = pl.BlockSpec(memory_space=pltpu.SMEM)
    hbm = pl.BlockSpec(memory_space=pltpu.HBM)
    dma = pltpu.SemaphoreType.DMA
    table_count = beta.shape[0] * per_group
    matrices_shape = jax.ShapeDtypeStruct((6, 2 * lanes, 2 * lanes), jnp.bfloat16)
    offsets = offsets.transpose(1, 0, 2)
    held = (wave, potential, positions, species, counts, offsets, beta, coupling)
    held = [a if a is counts else pltpu.with_memory_space_constraint(a, pltpu.HBM) for a in held]
    field, wide_potential, atoms, tables, matrices, strengths = pl.pallas_call(
        lambda *refs: spread_kernel(shape, *refs),
        out_shape=(
            jax.ShapeDtypeStruct((groups, window, lanes), jnp.float32),
            jax.ShapeDtypeStruct((groups, window, lanes), jnp.float32),
            jax.ShapeDtypeStruct((cols, bands, 1, lanes), jnp.int32),
            jax.ShapeDtypeStruct((table_count, 4 * box, lanes), jnp.float32),
            matrices_shape,
            jax.ShapeDtypeStruct((beta.shape[0] + 1, 1, lanes), jnp.float32),
        ),
        in_specs=[hbm] * 4 + [smem] + [hbm] * 3,
        out_specs=[vmem] * 6,
        scratch_shapes=[
            pltpu.VMEM(positions.shape, jnp.int32),
            pltpu.VMEM(species.shape, jnp.int32),
            pltpu.VMEM(offsets.shape, jnp.int32),
            pltpu.VMEM(beta.shape, jnp.float32),
            pltpu.SMEM(coupling.shape, jnp.float32),
            dma((5,)),
            pltpu.VMEM((2, bands, size_x, size_y, size_z), jnp.float32),
            pltpu.VMEM((1, lanes), jnp.int32),
            dma((3,)),
            dma((bands,)),
            dma((bands,)),
            dma((4, 4)),
            dma((4, 4)),
            dma((6,)),
            dma((6,)),
        ],
        compiler_params=pltpu.CompilerParams(
            collective_id=0, has_side_effects=True, vmem_limit_bytes=32 * 2**20
        ),
        name="spread",
    )(*held)

    most = bands * cols * slots + unroll
    padded = jax.ShapeDtypeStruct((groups + 2 * low_groups, window + 2 * low_rows, lanes), jnp.float32)
    plane_scratch = [
        pltpu.VMEM((groups // 2 * window, 2 * lanes), jnp.float32),
        pltpu.VMEM((groups // 2 * window, 2 * lanes), jnp.bfloat16),
        pltpu.VMEM((groups // 2 * window, 2 * lanes), jnp.bfloat16),
    ]
    second, rest = pl.pallas_call(
        lambda *refs: filter_kernel(size_z, *refs),
        out_shape=(padded, padded),
        in_specs=[smem] + [vmem] * 5,
        out_specs=[vmem] * 2,
        scratch_shapes=plane_scratch
        + [
            pltpu.VMEM((most, 4 * box, lanes), jnp.float32),
            pltpu.SMEM((most,), jnp.int32),
            pltpu.SMEM((3, most), jnp.int32),
        ],
        compiler_params=pltpu.CompilerParams(vmem_limit_bytes=40 * 2**20),
        name="chebyshev",
    )(atoms.reshape(cols * bands, 1, lanes), field, wide_potential, tables, matrices, strengths)

    devices = slabs * rows * cols
    cells = devices * size_x * size_y * size_z
    filtered, gram = pl.pallas_call(
        lambda *refs: collect_kernel(shape, cells, *refs),
        out_shape=(
            jax.ShapeDtypeStruct(wave.shape, jnp.float32),
            jax.ShapeDtypeStruct((bands, bands), jnp.float32),
        ),
        in_specs=[vmem] * 4,
        out_specs=[vmem] * 2,
        scratch_shapes=plane_scratch
        + [
            pltpu.VMEM((2, window, lanes), jnp.float32),
            pltpu.VMEM(wave.shape, jnp.float32),
            pltpu.VMEM((2, lanes), jnp.float32),
            pltpu.VMEM((devices, 2, lanes), jnp.float32),
            dma,
            dma((bands,)),
            dma((bands,)),
            dma((devices,)),
            dma((devices,)),
        ],
        compiler_params=pltpu.CompilerParams(
            collective_id=1, has_side_effects=True, vmem_limit_bytes=32 * 2**20
        ),
        name="collect",
    )(second, rest, wide_potential, matrices)
    return filtered, gram


def solution(mesh):
    in_specs = (
        P(None, "slab", "row", "col"),
        P("slab", "row", "col"),
        P(None, ("slab", "row", "col")),
        P(("slab", "row", "col")),
        P(("slab", "row", "col")),
        P(),
        P(),
        P(),
    )
    out_specs = (P(None, "slab", "row", "col"), P())
    shape = tuple(mesh.shape[name] for name in ("slab", "row", "col"))

    def run(*arrays):
        bands, size_x, size_y, size_z = arrays[0].shape
        one_band_a_chip = (
            shape[0] * shape[1] == bands
            and shape[2] == 2
            and (size_x, size_y, size_z) == (shape[0] * 8, shape[1] * 8, 2 * lanes)
            and (size_x, size_y) == (side, side)
            and arrays[2].shape[1] == 8 * mesh.size
        )
        body = (lambda *blocks: band_shards(shape, *blocks)) if one_band_a_chip else shards
        return jax.shard_map(
            body, mesh=mesh, in_specs=in_specs, out_specs=out_specs, check_vma=False
        )(*arrays)

    return run
```

```python
import jax
import jax.numpy as jnp
import ml_dtypes
import numpy as np
from jax import lax
from jax.experimental import pallas as pl
from jax.experimental.pallas import tpu as pltpu
from jax.sharding import PartitionSpec as P

stencil_weights = (
    -5369.0 / 1800.0,
    12.0 / 7.0,
    -15.0 / 56.0,
    10.0 / 189.0,
    -1.0 / 112.0,
    2.0 / 1925.0,
    -1.0 / 16632.0,
)
lower_edge = 3.0
upper_edge = 17.0


def padded_2(block, sides, width):
    for axis, dim in sides:
        count = lax.axis_size(axis)
        forward = [(i, i + 1) for i in range(count - 1)]
        backward = [(target, source) for source, target in forward]
        low = lax.ppermute(
            lax.slice_in_dim(block, block.shape[dim] - width, None, axis=dim), axis, forward
        )
        high = lax.ppermute(lax.slice_in_dim(block, 0, width, axis=dim), axis, backward)
        block = jnp.concatenate([low, block, high], axis=dim)
    return block


def stencil(padded, extent):
    size_x, size_y, size_z = extent

    def window(shift_x, shift_y, shift_z):
        return padded[
            :,
            6 + shift_x : 6 + shift_x + size_x,
            6 + shift_y : 6 + shift_y + size_y,
            6 + shift_z : 6 + shift_z + size_z,
        ]

    total = 3.0 * stencil_weights[0] * window(0, 0, 0)
    for reach in range(1, 7):
        paired = (
            window(reach, 0, 0)
            + window(-reach, 0, 0)
            + window(0, reach, 0)
            + window(0, -reach, 0)
            + window(0, 0, reach)
            + window(0, 0, -reach)
        )
        total = total + stencil_weights[reach] * paired
    return total


def atom_tables(species, offsets, beta, coupling):
    matches = species[:, None] == jnp.arange(beta.shape[0], dtype=jnp.int32)[None]
    onehot = matches.astype(jnp.float32)
    shapes = jnp.dot(onehot, beta, precision=lax.Precision.HIGHEST)
    gains = jnp.sum(onehot * coupling[None], axis=1)
    offset_rows = jnp.sum(jnp.where(matches[:, :, None, None], offsets[None], 0), axis=1)
    return (shapes, offset_rows, gains)


def add_rims(accumulated, received, axis_dim):
    length = accumulated.shape[axis_dim]
    inner = lax.slice_in_dim(accumulated, 6, length - 6, axis=axis_dim)
    lower_part = lax.slice_in_dim(received, 0, 6, axis=axis_dim)
    upper_part = lax.slice_in_dim(received, 18, 24, axis=axis_dim)
    leading = [slice(None)] * 4
    leading[axis_dim] = slice(0, 6)
    inner = inner.at[tuple(leading)].add(lower_part)
    trailing = [slice(None)] * 4
    trailing[axis_dim] = slice(length - 18, length - 12)
    return inner.at[tuple(trailing)].add(upper_part)


def shards(wave, potential, positions, species, counts, offsets, beta, coupling):
    bands, size_x, size_y, size_z = wave.shape
    extent = (size_x, size_y, size_z)
    wide_x, wide_y, wide_z = (size_x + 12, size_y + 12, size_z + 12)
    anchor = jnp.stack(
        [
            lax.axis_index("slab") * size_x,
            lax.axis_index("row") * size_y,
            lax.axis_index("col") * size_z,
        ]
    )
    slot_count = positions.shape[1]
    own_shapes, own_offsets, own_gains = atom_tables(species, offsets, beta, coupling)
    active = (jnp.arange(slot_count, dtype=jnp.int32) < counts[0]).astype(jnp.float32)
    own_weights = own_gains * active
    local = positions.T[:, :, None] - anchor[None, :, None] + own_offsets + 6
    ext_index = ((local[:, 0] * wide_y + local[:, 1]) * wide_z + local[:, 2]).reshape(-1)
    centre = 0.5 * (upper_edge + lower_edge)
    half_width = 0.5 * (upper_edge - lower_edge)

    def spread_rims(scaled):
        contributions = (scaled[:, :, None] * own_shapes[None]).reshape(bands, -1)
        accumulated = (
            jnp.zeros((bands, wide_x * wide_y * wide_z), jnp.float32)
            .at[:, ext_index]
            .add(contributions)
        )
        accumulated = accumulated.reshape(bands, wide_x, wide_y, wide_z)
        rims = jnp.concatenate([accumulated[:, :6], accumulated[:, -6:]], axis=1)
        received = padded_2(rims, (("slab", 1),), 6)
        accumulated = add_rims(accumulated, received, 1)
        rims = jnp.concatenate([accumulated[:, :, :6], accumulated[:, :, -6:]], axis=2)
        received = padded_2(rims, (("row", 2),), 6)
        accumulated = add_rims(accumulated, received, 2)
        rims = jnp.concatenate([accumulated[:, :, :, :6], accumulated[:, :, :, -6:]], axis=3)
        received = padded_2(rims, (("col", 3),), 6)
        return add_rims(accumulated, received, 3)

    def filter_step(field):
        padded = padded_2(field, (("slab", 1), ("row", 2), ("col", 3)), 6)
        picked = jnp.take(padded.reshape(bands, -1), ext_index, axis=1).reshape(
            bands, slot_count, -1
        )
        projected = jnp.sum(picked * own_shapes[None], axis=2)
        scaled = projected * own_weights[None]
        projector_part = spread_rims(scaled)
        applied = -0.5 * stencil(padded, extent) + potential[None] * field + projector_part
        return (applied - centre * field) / half_width

    first = filter_step(wave)
    second = 2.0 * filter_step(first) - wave
    third = 2.0 * filter_step(second) - first
    flattened = third.reshape(bands, -1)
    partial_gram = jnp.dot(flattened, flattened.T, precision=lax.Precision.HIGHEST)
    summed_gram = lax.psum(partial_gram, ("slab", "row", "col"))
    cells_total = (
        size_x
        * size_y
        * size_z
        * lax.axis_size("slab")
        * lax.axis_size("row")
        * lax.axis_size("col")
    )
    return (third, summed_gram / cells_total)


side = 32
lanes = 128
per_group = lanes // side
groups = side // per_group
margin = 32
low_groups = 2
low_rows = 16
box = 16
unroll = 8
centre = 0.5 * (upper_edge + lower_edge)
half_width = 0.5 * (upper_edge - lower_edge)
MESH = pl.DeviceIdType.MESH


def build_matrices(matrices):
    span = 2 * per_group
    size = span * side
    one = lax.broadcasted_iota(jnp.int32, (size, size), 0)
    two = lax.broadcasted_iota(jnp.int32, (size, size), 1)
    dy = jnp.abs(one % side - two % side)
    for which, shift in enumerate((0, span, -span)):
        dx = jnp.abs(one // side - two // side - shift)
        distance = jnp.where(dy == 0, dx, jnp.where(dx == 0, dy, 0))
        high = jnp.zeros((size, size), jnp.float32)
        low = jnp.zeros((size, size), jnp.float32)
        for reach in range(1, 7):
            weight = -0.5 / half_width * stencil_weights[reach]
            top = float(np.float32(ml_dtypes.bfloat16(weight)))
            high = jnp.where(distance == reach, top, high)
            low = jnp.where(distance == reach, weight - top, low)
        matrices[2 * which] = high.astype(jnp.bfloat16)
        matrices[2 * which + 1] = low.astype(jnp.bfloat16)


def split_three(value):
    first = value.astype(jnp.bfloat16).astype(jnp.float32)
    second = (value - first).astype(jnp.bfloat16).astype(jnp.float32)
    return (first, second, value - first - second)


def build_tables(offsets, beta, tables):
    points = beta.shape[1]
    for kind in range(beta.shape[0]):
        dx, dy, dz = (offsets[axis, kind : kind + 1, :] + 5 for axis in range(3))
        parts = split_three(beta[kind : kind + 1, :])
        for phase in range(per_group):
            moved = dx + phase
            place = (moved // per_group) * box + dz
            lane = (moved % per_group) * side + dy
            hit = lax.broadcasted_iota(jnp.int32, (4 * box, points), 0) == place
            left = jnp.concatenate([jnp.where(hit, part, 0.0) for part in parts], axis=0)
            right = (lax.broadcasted_iota(jnp.int32, (lanes, points), 0) == lane).astype(jnp.float32)
            dense = lax.dot_general(
                left.astype(jnp.bfloat16),
                right.astype(jnp.bfloat16),
                (((1,), (1,)), ((), ())),
                preferred_element_type=jnp.float32,
            )
            tables[kind * per_group + phase] = (
                dense[: 4 * box] + dense[4 * box : 8 * box] + dense[8 * box :]
            )


def spread_kernel(
    shape, wave, potential, positions_in, species_in, counts, offsets_in, beta_in, coupling_in,
    field_out, potential_out, atoms_out, tables, matrices, strengths,
    positions, species, offsets, beta, coupling, small_sem, got, info, local_sem, send_sem, recv_sem, part_send, part_recv, pair_send, pair_recv,
):
    slabs, rows, _ = shape
    depth = wave.shape[3]
    slab, row, col = (lax.axis_index(name) for name in ("slab", "row", "col"))
    me = slab * rows + row
    other = (slab, row, 1 - col)
    shifts = [(s, r) for s in (1, 2, 3, 0) for r in range(rows)]

    def partner(shift):
        return (lax.rem(slab + shift[0], slabs), lax.rem(row + shift[1], rows), col)

    small = (
        (positions_in, positions),
        (species_in, species),
        (offsets_in, offsets),
        (beta_in, beta),
        (coupling_in, coupling),
    )
    small = [pltpu.make_async_copy(*pair, small_sem.at[index]) for index, pair in enumerate(small)]
    for copy in small:
        copy.start()
    barrier = pltpu.get_barrier_semaphore()
    for shift in shifts:
        if shift != (0, 0):
            pl.semaphore_signal(barrier, inc=1, device_id=partner(shift), device_id_type=MESH)
    pl.semaphore_signal(barrier, inc=1, device_id=other, device_id_type=MESH)

    for copy in small:
        copy.wait()
    slots = positions.shape[1]
    live = (lax.broadcasted_iota(jnp.int32, (1, slots), 1) < counts[0]).astype(jnp.int32)
    words = [positions[0:1, :], positions[1:2, :], positions[2:3, :], species[...].reshape(1, slots), live]
    words.append(jnp.zeros((1, lanes - 5 * slots), jnp.int32))
    info[...] = jnp.concatenate(words, axis=1)
    pl.semaphore_wait(barrier, slabs * rows)

    def remote(source, place, send, recv, device):
        copy = pltpu.make_async_remote_copy(
            src_ref=source,
            dst_ref=place,
            send_sem=send,
            recv_sem=recv,
            device_id=device,
            device_id_type=MESH,
        )
        copy.start()
        return copy

    def local(source, place, sem):
        copy = pltpu.make_async_copy(source, place, sem)
        copy.start()
        return copy

    first = [
        local(potential, got.at[1, me], local_sem.at[1]),
        local(info, atoms_out.at[col, me], local_sem.at[2]),
    ]
    for r in range(1, rows):
        device = partner((0, r))
        first.append(remote(potential, got.at[1, me], part_send.at[0, r], part_recv.at[0, r], device))
        first.append(remote(info, atoms_out.at[col, me], part_send.at[1, r], part_recv.at[1, r], device))
    moves = {}
    for index, shift in enumerate(shifts):
        if shift == (0, 0):
            moves[shift] = local(wave.at[me], got.at[0, me], local_sem.at[0])
        else:
            device = partner(shift)
            target = device[0] * rows + device[1]
            moves[shift] = remote(wave.at[target], got.at[0, me], send_sem.at[index], recv_sem.at[index], device)
    for copy in first:
        copy.wait()
    run = pl.ds(slab * rows, rows)
    second = []
    for s in range(1, slabs):
        device = partner((s, 0))
        second.append(remote(got.at[1, run], got.at[1, run], part_send.at[2, s], part_recv.at[2, s], device))
        second.append(
            remote(atoms_out.at[col, run], atoms_out.at[col, run], part_send.at[3, s], part_recv.at[3, s], device)
        )
    build_tables(offsets, beta, tables)
    build_matrices(matrices)
    kinds = beta.shape[0]
    for kind in range(kinds):
        strengths[kind] = jnp.full((1, lanes), 1.0 / half_width, jnp.float32) * coupling[kind]
    strengths[kinds] = jnp.zeros((1, lanes), jnp.float32)
    for copy in second:
        copy.wait()

    own_at = pl.multiple_of(col * margin, margin)
    from_at = pl.multiple_of(col * margin + (1 - col) * (depth - margin), margin)
    to_at = pl.multiple_of(col * depth, margin)

    def turn(kind, out, part):
        for half in range(2):
            tiles = [
                got[kind, part * rows + r, half * per_group + x] for x in range(per_group) for r in range(rows)
            ]
            out[part * 2 + half, pl.ds(own_at, depth), :] = jnp.concatenate(tiles, axis=0).T

    def pass_on(out, part, size, index):
        source = out.at[pl.ds(part * 2, size), pl.ds(from_at, margin), :]
        place = out.at[pl.ds(part * 2, size), pl.ds(to_at, margin), :]
        return remote(source, place, pair_send.at[index], pair_recv.at[index], other)

    last = [remote(atoms_out.at[col], atoms_out.at[col], pair_send.at[0], pair_recv.at[0], other)]
    for part in range(slabs):
        turn(1, potential_out, part)
    last.append(pass_on(potential_out, 0, groups, 1))
    for order, s in enumerate((1, 2, 3, 0)):
        for r in range(rows):
            moves[(s, r)].wait()
        part = lax.rem(slab + (slabs - s), slabs)
        turn(0, field_out, part)
        last.append(pass_on(field_out, part, 2, 2 + order))
    for copy in last:
        copy.wait()


def plane_part(source, matrices, plane, high, low, window):
    inner = pl.ds(low_rows, window)
    for tile in range(groups // 2):
        wide = jnp.concatenate(
            [source[low_groups + 2 * tile, inner], source[low_groups + 2 * tile + 1, inner]], axis=1
        )
        big = wide.astype(jnp.bfloat16)
        high[pl.ds(tile * window, window)] = big
        low[pl.ds(tile * window, window)] = (wide - big.astype(jnp.float32)).astype(jnp.bfloat16)
    total = groups // 2 * window

    def product(part, which, begin, end):
        return jnp.dot(part[begin:end], matrices[which], preferred_element_type=jnp.float32)

    def triple(which, begin, end):
        return (
            product(high, which, begin, end)
            + product(low, which, begin, end)
            + product(high, which + 1, begin, end)
        )

    plane[...] = triple(0, 0, total)
    plane[window:] += triple(2, 0, total - window)
    plane[: total - window] += triple(4, window, total)


def local_part(source, potential, plane, part, half, window):
    group = 2 * part + half
    padded = low_groups + group
    diagonal = (potential[group] - (centre + 1.5 * stencil_weights[0])) / half_width
    value = diagonal * source[padded, pl.ds(low_rows, window)]
    for reach in range(1, 7):
        value = value + (-0.5 / half_width * stencil_weights[reach]) * (
            source[padded, pl.ds(low_rows + reach, window)] + source[padded, pl.ds(low_rows - reach, window)]
        )
    at = part * window
    if not isinstance(part, int):
        at = pl.multiple_of(at, 32)
    return value + plane[pl.ds(at, window), half * lanes : (half + 1) * lanes]


def filter_kernel(
    depth, atoms, field, potential, tables, matrices, strengths, ping, pong,
    plane, high, low, shapes, listed, found,
):
    window = field.shape[1]
    slots = 8
    col = lax.axis_index("col")
    window_start = col * (depth - margin)
    inner = pl.ds(low_rows, window)

    def clear_rims(ref):
        ref[:low_groups] = jnp.zeros((low_groups,) + ref.shape[1:], jnp.float32)
        ref[low_groups + groups :] = jnp.zeros((low_groups,) + ref.shape[1:], jnp.float32)
        middle = pl.ds(low_groups, groups)
        ref[middle, :low_rows] = jnp.zeros((groups, low_rows, lanes), jnp.float32)
        ref[middle, low_rows + window :] = jnp.zeros((groups, low_rows, lanes), jnp.float32)

    clear_rims(ping)
    ping[pl.ds(low_groups, groups), inner] = field[...]

    lane_y = lax.broadcasted_iota(jnp.int32, (4 * box, lanes), 1) % side

    def find(block, count):
        for place in range(slots):
            local = atoms[block, 0, 2 * slots + place] - window_start
            live = atoms[block, 0, 4 * slots + place]
            listed[count] = block * slots + place
            count = count + jnp.where((local >= -5) & (local <= window + 4), live, 0)
        return count

    def gather(source, index, scale):
        gains = []
        for extra in range(unroll):
            atom = index * unroll + extra
            group, at = found[0, atom], found[1, atom]
            total = jnp.zeros((box, lanes), jnp.float32)
            for part in range(4):
                total = total + source[group + part, pl.ds(at, box)] * shapes[atom, pl.ds(part * box, box)]
            summed = jnp.sum(jnp.sum(total, axis=0, keepdims=True), axis=1, keepdims=True)
            gains.append(summed * (strengths[found[2, atom]] * scale))
        return tuple(gains)

    def scatter(target, index, gains):
        for extra in range(unroll):
            atom = index * unroll + extra
            group, at = found[0, atom], found[1, atom]
            for part in range(4):
                target[group + part, pl.ds(at, box)] += gains[extra] * shapes[atom, pl.ds(part * box, box)]

    def project(source, target, scale):
        def batch(index, gains):
            later = gather(source, index, scale)
            scatter(target, index - 1, gains)
            return later

        gains = lax.fori_loop(1, batches, batch, gather(source, 0, scale))
        scatter(target, batches - 1, gains)

    def stencil_step(source, target, scale, keep, between=None):
        plane_part(source, matrices, plane, high, low, window)
        for part in range(groups // 2):
            for half in range(2):
                padded = low_groups + 2 * part + half
                value = local_part(source, potential, plane, part, half, window)
                if keep:
                    value = scale * value - target[padded, inner]
                target[padded, inner] = value
                if between is not None:
                    between(2 * part + half)

    counts = [jnp.int32(0)]
    share = atoms.shape[0] // groups

    def find_some(index):
        for block in range(index * share, (index + 1) * share):
            counts.append(find(block, counts[-1]))

    stencil_step(ping, pong, 1.0, False, find_some)
    count = counts[-1]
    for extra in range(unroll):
        listed[count + extra] = 0
    batches = jnp.maximum((count + unroll - 1) // unroll, 1)

    def shape_batch(index, carry):
        for extra in range(unroll):
            atom = index * unroll + extra
            slot = listed[atom]
            block, place = slot // slots, lax.rem(slot, slots)
            x, y, z, kind = (atoms[block, 0, word * slots + place] for word in range(4))
            found[0, atom] = (x + 3) // per_group
            found[1, atom] = jnp.clip(z - window_start, -5, window + 4) - 5 + low_rows
            found[2, atom] = jnp.where(atom < count, kind, strengths.shape[0] - 1)
            start = y - 5
            table = tables[kind * per_group + lax.rem(x + 3, per_group)]
            rolled = pltpu.roll(table, lax.rem(start + lanes, lanes), 1)
            shapes[atom] = jnp.where((lane_y >= start) & (lane_y <= start + 10), rolled, 0.0)
        return carry

    lax.fori_loop(0, batches, shape_batch, 0)

    project(ping, pong, 1.0)
    clear_rims(pong)
    stencil_step(pong, ping, 2.0, True)
    project(pong, ping, 2.0)
    clear_rims(ping)
    middle = pl.ds(low_groups, groups)
    pong[middle, inner] = -pong[middle, inner]
    project(ping, pong, 2.0)


def collect_kernel(
    shape, cells, source, rest, potential, matrices, block, gram,
    plane, high, low, turning, pieces, gram_high, gram_low, partial, sums, local_sem, send_sem, recv_sem, sum_send, sum_recv,
):
    slabs, rows, cols = shape
    bands, _, _, depth = block.shape
    window = potential.shape[1]
    devices = slabs * rows * cols
    slab, row, col = (lax.axis_index(name) for name in ("slab", "row", "col"))
    me = slab * rows + row
    mine = me * cols + col

    def partner(step):
        target = lax.rem(mine + step, devices)
        return (target // (rows * cols), lax.rem(target // cols, rows), lax.rem(target, cols))

    barrier = pltpu.get_barrier_semaphore()
    for step in range(1, devices):
        pl.semaphore_signal(barrier, inc=1, device_id=partner(step), device_id_type=MESH)
    plane_part(source, matrices, plane, high, low, window)
    begin = pl.multiple_of(col * margin, margin)
    copies = []
    for order, s in enumerate((1, 2, 3, 0)):
        part = lax.rem(slab + s, slabs)
        for half in range(2):
            padded = low_groups + 2 * part + half
            value = local_part(source, potential, plane, part, half, window)
            turning[half] = 2.0 * value + rest[padded, pl.ds(low_rows, window)]
            turned = turning[half, pl.ds(begin, depth), :].T
            for x in range(per_group):
                for r in range(rows):
                    at = (x * rows + r) * 8
                    pieces[part * rows + r, half * per_group + x] = turned[at : at + 8]
        if order == 0:
            pl.semaphore_wait(barrier, devices - 1)
        for r in range(rows):
            to_row = lax.rem(row + r, rows)
            target = part * rows + to_row
            if s == 0 and r == 0:
                copies.append(pltpu.make_async_copy(pieces.at[me], block.at[me], local_sem))
            else:
                copies.append(
                    pltpu.make_async_remote_copy(
                        src_ref=pieces.at[target],
                        dst_ref=block.at[me],
                        send_sem=send_sem.at[order * rows + r],
                        recv_sem=recv_sem.at[order * rows + r],
                        device_id=(part, to_row, col),
                        device_id_type=MESH,
                    )
                )
            copies[-1].start()
    size_x, size_y = block.shape[1:3]
    flat = bands * size_y
    some = rows * size_y
    for order, s in enumerate((1, 2, 3, 0)):
        for copy in copies[order * rows : (order + 1) * rows]:
            copy.wait()
        part = lax.rem(slab + (slabs - s), slabs)
        at = pl.ds(pl.multiple_of(part * some, some), some)
        for x in range(size_x):
            value = block[pl.ds(part * rows, rows), x].reshape(some, lanes)
            big = value.astype(jnp.bfloat16)
            gram_high[at, x * lanes : (x + 1) * lanes] = big
            gram_low[at, x * lanes : (x + 1) * lanes] = (value - big.astype(jnp.float32)).astype(jnp.bfloat16)
    product = lax.dot_general(
        gram_high[...],
        jnp.concatenate([gram_high[...], gram_low[...]], axis=0),
        (((1,), (1,)), ((), ())),
        preferred_element_type=jnp.float32,
    )
    cross = product[:, flat:]
    product = product[:, :flat] + cross + cross.T
    one = lax.broadcasted_iota(jnp.int32, (flat, flat), 0)
    two = lax.broadcasted_iota(jnp.int32, (flat, flat), 1)
    product = jnp.where(one % size_y == two % size_y, product, 0.0)
    product = jnp.sum(product.reshape(bands, size_y, flat), axis=1)

    def times(value, picks):
        parts = jnp.concatenate(split_three(value), axis=0).astype(jnp.bfloat16)
        result = jnp.dot(parts, picks.astype(jnp.bfloat16), preferred_element_type=jnp.float32)
        return result[:bands] + result[bands : 2 * bands] + result[2 * bands :]

    folded = times(product, (one // size_y == two % bands).astype(jnp.float32))
    packed = (2, bands // 2, lanes)
    keep = lax.broadcasted_iota(jnp.int32, packed, 1) == lax.broadcasted_iota(jnp.int32, packed, 2) // bands
    partial[...] = jnp.sum(jnp.where(keep, folded.reshape(packed), 0.0), axis=1)
    sums[mine] = partial[...]
    copies = []
    for step in range(1, devices):
        copies.append(
            pltpu.make_async_remote_copy(
                src_ref=partial,
                dst_ref=sums.at[mine],
                send_sem=sum_send.at[step],
                recv_sem=sum_recv.at[step],
                device_id=partner(step),
                device_id_type=MESH,
            )
        )
    for copy in copies:
        copy.start()
    for copy in copies:
        copy.wait()
    total = jnp.sum(sums[...], axis=0) * (1.0 / cells)
    total = jnp.where(keep, jnp.broadcast_to(total[:, None, :], packed), 0.0).reshape(bands, lanes)
    gram[...] = times(total, (one % bands == two).astype(jnp.float32))[:, :bands]


def band_shards(shape, wave, potential, positions, species, counts, offsets, beta, coupling):
    slabs, rows, cols = shape
    bands, size_x, size_y, size_z = wave.shape
    slots = positions.shape[1]
    window = size_z + margin
    vmem = pl.BlockSpec(memory_space=pltpu.VMEM)
    smem = pl.BlockSpec(memory_space=pltpu.SMEM)
    hbm = pl.BlockSpec(memory_space=pltpu.HBM)
    dma = pltpu.SemaphoreType.DMA
    table_count = beta.shape[0] * per_group
    matrices_shape = jax.ShapeDtypeStruct((6, 2 * lanes, 2 * lanes), jnp.bfloat16)
    offsets = offsets.transpose(1, 0, 2)
    held = (wave, potential, positions, species, counts, offsets, beta, coupling)
    held = [a if a is counts else pltpu.with_memory_space_constraint(a, pltpu.HBM) for a in held]
    field, wide_potential, atoms, tables, matrices, strengths = pl.pallas_call(
        lambda *refs: spread_kernel(shape, *refs),
        out_shape=(
            jax.ShapeDtypeStruct((groups, window, lanes), jnp.float32),
            jax.ShapeDtypeStruct((groups, window, lanes), jnp.float32),
            jax.ShapeDtypeStruct((cols, bands, 1, lanes), jnp.int32),
            jax.ShapeDtypeStruct((table_count, 4 * box, lanes), jnp.float32),
            matrices_shape,
            jax.ShapeDtypeStruct((beta.shape[0] + 1, 1, lanes), jnp.float32),
        ),
        in_specs=[hbm] * 4 + [smem] + [hbm] * 3,
        out_specs=[vmem] * 6,
        scratch_shapes=[
            pltpu.VMEM(positions.shape, jnp.int32),
            pltpu.VMEM(species.shape, jnp.int32),
            pltpu.VMEM(offsets.shape, jnp.int32),
            pltpu.VMEM(beta.shape, jnp.float32),
            pltpu.SMEM(coupling.shape, jnp.float32),
            dma((5,)),
            pltpu.VMEM((2, bands, size_x, size_y, size_z), jnp.float32),
            pltpu.VMEM((1, lanes), jnp.int32),
            dma((3,)),
            dma((bands,)),
            dma((bands,)),
            dma((4, 4)),
            dma((4, 4)),
            dma((6,)),
            dma((6,)),
        ],
        compiler_params=pltpu.CompilerParams(
            collective_id=0, has_side_effects=True, vmem_limit_bytes=32 * 2**20
        ),
        name="spread",
    )(*held)

    most = bands * cols * slots + unroll
    padded = jax.ShapeDtypeStruct((groups + 2 * low_groups, window + 2 * low_rows, lanes), jnp.float32)
    plane_scratch = [
        pltpu.VMEM((groups // 2 * window, 2 * lanes), jnp.float32),
        pltpu.VMEM((groups // 2 * window, 2 * lanes), jnp.bfloat16),
        pltpu.VMEM((groups // 2 * window, 2 * lanes), jnp.bfloat16),
    ]
    second, rest = pl.pallas_call(
        lambda *refs: filter_kernel(size_z, *refs),
        out_shape=(padded, padded),
        in_specs=[smem] + [vmem] * 5,
        out_specs=[vmem] * 2,
        scratch_shapes=plane_scratch
        + [
            pltpu.VMEM((most, 4 * box, lanes), jnp.float32),
            pltpu.SMEM((most,), jnp.int32),
            pltpu.SMEM((3, most), jnp.int32),
        ],
        compiler_params=pltpu.CompilerParams(vmem_limit_bytes=40 * 2**20),
        name="chebyshev",
    )(atoms.reshape(cols * bands, 1, lanes), field, wide_potential, tables, matrices, strengths)

    devices = slabs * rows * cols
    cells = devices * size_x * size_y * size_z
    filtered, gram = pl.pallas_call(
        lambda *refs: collect_kernel(shape, cells, *refs),
        out_shape=(
            jax.ShapeDtypeStruct(wave.shape, jnp.float32),
            jax.ShapeDtypeStruct((bands, bands), jnp.float32),
        ),
        in_specs=[vmem] * 4,
        out_specs=[vmem] * 2,
        scratch_shapes=plane_scratch
        + [
            pltpu.VMEM((2, window, lanes), jnp.float32),
            pltpu.VMEM(wave.shape, jnp.float32),
            pltpu.VMEM((bands * size_y, size_x * lanes), jnp.bfloat16),
            pltpu.VMEM((bands * size_y, size_x * lanes), jnp.bfloat16),
            pltpu.VMEM((2, lanes), jnp.float32),
            pltpu.VMEM((devices, 2, lanes), jnp.float32),
            dma,
            dma((bands,)),
            dma((bands,)),
            dma((devices,)),
            dma((devices,)),
        ],
        compiler_params=pltpu.CompilerParams(
            collective_id=1, has_side_effects=True, vmem_limit_bytes=32 * 2**20
        ),
        name="collect",
    )(second, rest, wide_potential, matrices)
    return filtered, gram


def solution(mesh):
    in_specs = (
        P(None, "slab", "row", "col"),
        P("slab", "row", "col"),
        P(None, ("slab", "row", "col")),
        P(("slab", "row", "col")),
        P(("slab", "row", "col")),
        P(),
        P(),
        P(),
    )
    out_specs = (P(None, "slab", "row", "col"), P())
    shape = tuple(mesh.shape[name] for name in ("slab", "row", "col"))

    def run(*arrays):
        bands, size_x, size_y, size_z = arrays[0].shape
        one_band_a_chip = (
            shape[0] * shape[1] == bands
            and shape[2] == 2
            and (size_x, size_y, size_z) == (shape[0] * 8, shape[1] * 8, 2 * lanes)
            and (size_x, size_y) == (side, side)
            and arrays[2].shape[1] == 8 * mesh.size
        )
        body = (lambda *blocks: band_shards(shape, *blocks)) if one_band_a_chip else shards
        return jax.shard_map(
            body, mesh=mesh, in_specs=in_specs, out_specs=out_specs, check_vma=False
        )(*arrays)

    return run
```

```python
import jax
import jax.numpy as jnp
import ml_dtypes
import numpy as np
from jax import lax
from jax.experimental import pallas as pl
from jax.experimental.pallas import tpu as pltpu
from jax.sharding import PartitionSpec as P

stencil_weights = (
    -5369.0 / 1800.0,
    12.0 / 7.0,
    -15.0 / 56.0,
    10.0 / 189.0,
    -1.0 / 112.0,
    2.0 / 1925.0,
    -1.0 / 16632.0,
)
lower_edge = 3.0
upper_edge = 17.0


def padded_2(block, sides, width):
    for axis, dim in sides:
        count = lax.axis_size(axis)
        forward = [(i, i + 1) for i in range(count - 1)]
        backward = [(target, source) for source, target in forward]
        low = lax.ppermute(
            lax.slice_in_dim(block, block.shape[dim] - width, None, axis=dim), axis, forward
        )
        high = lax.ppermute(lax.slice_in_dim(block, 0, width, axis=dim), axis, backward)
        block = jnp.concatenate([low, block, high], axis=dim)
    return block


def stencil(padded, extent):
    size_x, size_y, size_z = extent

    def window(shift_x, shift_y, shift_z):
        return padded[
            :,
            6 + shift_x : 6 + shift_x + size_x,
            6 + shift_y : 6 + shift_y + size_y,
            6 + shift_z : 6 + shift_z + size_z,
        ]

    total = 3.0 * stencil_weights[0] * window(0, 0, 0)
    for reach in range(1, 7):
        paired = (
            window(reach, 0, 0)
            + window(-reach, 0, 0)
            + window(0, reach, 0)
            + window(0, -reach, 0)
            + window(0, 0, reach)
            + window(0, 0, -reach)
        )
        total = total + stencil_weights[reach] * paired
    return total


def atom_tables(species, offsets, beta, coupling):
    matches = species[:, None] == jnp.arange(beta.shape[0], dtype=jnp.int32)[None]
    onehot = matches.astype(jnp.float32)
    shapes = jnp.dot(onehot, beta, precision=lax.Precision.HIGHEST)
    gains = jnp.sum(onehot * coupling[None], axis=1)
    offset_rows = jnp.sum(jnp.where(matches[:, :, None, None], offsets[None], 0), axis=1)
    return (shapes, offset_rows, gains)


def add_rims(accumulated, received, axis_dim):
    length = accumulated.shape[axis_dim]
    inner = lax.slice_in_dim(accumulated, 6, length - 6, axis=axis_dim)
    lower_part = lax.slice_in_dim(received, 0, 6, axis=axis_dim)
    upper_part = lax.slice_in_dim(received, 18, 24, axis=axis_dim)
    leading = [slice(None)] * 4
    leading[axis_dim] = slice(0, 6)
    inner = inner.at[tuple(leading)].add(lower_part)
    trailing = [slice(None)] * 4
    trailing[axis_dim] = slice(length - 18, length - 12)
    return inner.at[tuple(trailing)].add(upper_part)


def shards(wave, potential, positions, species, counts, offsets, beta, coupling):
    bands, size_x, size_y, size_z = wave.shape
    extent = (size_x, size_y, size_z)
    wide_x, wide_y, wide_z = (size_x + 12, size_y + 12, size_z + 12)
    anchor = jnp.stack(
        [
            lax.axis_index("slab") * size_x,
            lax.axis_index("row") * size_y,
            lax.axis_index("col") * size_z,
        ]
    )
    slot_count = positions.shape[1]
    own_shapes, own_offsets, own_gains = atom_tables(species, offsets, beta, coupling)
    active = (jnp.arange(slot_count, dtype=jnp.int32) < counts[0]).astype(jnp.float32)
    own_weights = own_gains * active
    local = positions.T[:, :, None] - anchor[None, :, None] + own_offsets + 6
    ext_index = ((local[:, 0] * wide_y + local[:, 1]) * wide_z + local[:, 2]).reshape(-1)
    centre = 0.5 * (upper_edge + lower_edge)
    half_width = 0.5 * (upper_edge - lower_edge)

    def spread_rims(scaled):
        contributions = (scaled[:, :, None] * own_shapes[None]).reshape(bands, -1)
        accumulated = (
            jnp.zeros((bands, wide_x * wide_y * wide_z), jnp.float32)
            .at[:, ext_index]
            .add(contributions)
        )
        accumulated = accumulated.reshape(bands, wide_x, wide_y, wide_z)
        rims = jnp.concatenate([accumulated[:, :6], accumulated[:, -6:]], axis=1)
        received = padded_2(rims, (("slab", 1),), 6)
        accumulated = add_rims(accumulated, received, 1)
        rims = jnp.concatenate([accumulated[:, :, :6], accumulated[:, :, -6:]], axis=2)
        received = padded_2(rims, (("row", 2),), 6)
        accumulated = add_rims(accumulated, received, 2)
        rims = jnp.concatenate([accumulated[:, :, :, :6], accumulated[:, :, :, -6:]], axis=3)
        received = padded_2(rims, (("col", 3),), 6)
        return add_rims(accumulated, received, 3)

    def filter_step(field):
        padded = padded_2(field, (("slab", 1), ("row", 2), ("col", 3)), 6)
        picked = jnp.take(padded.reshape(bands, -1), ext_index, axis=1).reshape(
            bands, slot_count, -1
        )
        projected = jnp.sum(picked * own_shapes[None], axis=2)
        scaled = projected * own_weights[None]
        projector_part = spread_rims(scaled)
        applied = -0.5 * stencil(padded, extent) + potential[None] * field + projector_part
        return (applied - centre * field) / half_width

    first = filter_step(wave)
    second = 2.0 * filter_step(first) - wave
    third = 2.0 * filter_step(second) - first
    flattened = third.reshape(bands, -1)
    partial_gram = jnp.dot(flattened, flattened.T, precision=lax.Precision.HIGHEST)
    summed_gram = lax.psum(partial_gram, ("slab", "row", "col"))
    cells_total = (
        size_x
        * size_y
        * size_z
        * lax.axis_size("slab")
        * lax.axis_size("row")
        * lax.axis_size("col")
    )
    return (third, summed_gram / cells_total)


side = 32
lanes = 128
per_group = lanes // side
groups = side // per_group
margin = 32
low_groups = 2
low_rows = 16
box = 16
unroll = 16
centre = 0.5 * (upper_edge + lower_edge)
half_width = 0.5 * (upper_edge - lower_edge)
MESH = pl.DeviceIdType.MESH


def build_matrices(matrices):
    span = 2 * per_group
    size = span * side
    one = lax.broadcasted_iota(jnp.int32, (size, size), 0)
    two = lax.broadcasted_iota(jnp.int32, (size, size), 1)
    dy = jnp.abs(one % side - two % side)
    for which, shift in enumerate((0, span, -span)):
        dx = jnp.abs(one // side - two // side - shift)
        distance = jnp.where(dy == 0, dx, jnp.where(dx == 0, dy, 0))
        high = jnp.zeros((size, size), jnp.float32)
        low = jnp.zeros((size, size), jnp.float32)
        for reach in range(1, 7):
            weight = -0.5 / half_width * stencil_weights[reach]
            top = float(np.float32(ml_dtypes.bfloat16(weight)))
            high = jnp.where(distance == reach, top, high)
            low = jnp.where(distance == reach, weight - top, low)
        matrices[2 * which] = high.astype(jnp.bfloat16)
        matrices[2 * which + 1] = low.astype(jnp.bfloat16)


def split_three(value):
    first = value.astype(jnp.bfloat16).astype(jnp.float32)
    second = (value - first).astype(jnp.bfloat16).astype(jnp.float32)
    return (first, second, value - first - second)


def build_tables(offsets, beta, tables):
    points = beta.shape[1]
    for kind in range(beta.shape[0]):
        dx, dy, dz = (offsets[axis, kind : kind + 1, :] + 5 for axis in range(3))
        parts = split_three(beta[kind : kind + 1, :])
        for phase in range(per_group):
            moved = dx + phase
            place = (moved // per_group) * box + dz
            lane = (moved % per_group) * side + dy
            hit = lax.broadcasted_iota(jnp.int32, (4 * box, points), 0) == place
            left = jnp.concatenate([jnp.where(hit, part, 0.0) for part in parts], axis=0)
            right = (lax.broadcasted_iota(jnp.int32, (lanes, points), 0) == lane).astype(jnp.float32)
            dense = lax.dot_general(
                left.astype(jnp.bfloat16),
                right.astype(jnp.bfloat16),
                (((1,), (1,)), ((), ())),
                preferred_element_type=jnp.float32,
            )
            tables[kind * per_group + phase] = (
                dense[: 4 * box] + dense[4 * box : 8 * box] + dense[8 * box :]
            )


def spread_kernel(
    shape, wave, potential, positions_in, species_in, counts, offsets_in, beta_in, coupling_in,
    field_out, potential_out, atoms_out, tables, matrices, strengths,
    positions, species, offsets, beta, coupling, small_sem, got, info, local_sem, send_sem, recv_sem, part_send, part_recv, pair_send, pair_recv,
):
    slabs, rows, _ = shape
    depth = wave.shape[3]
    slab, row, col = (lax.axis_index(name) for name in ("slab", "row", "col"))
    me = slab * rows + row
    other = (slab, row, 1 - col)
    shifts = [(s, r) for s in (1, 2, 3, 0) for r in range(rows)]

    def partner(shift):
        return (lax.rem(slab + shift[0], slabs), lax.rem(row + shift[1], rows), col)

    small = (
        (positions_in, positions),
        (species_in, species),
        (offsets_in, offsets),
        (beta_in, beta),
        (coupling_in, coupling),
    )
    small = [pltpu.make_async_copy(*pair, small_sem.at[index]) for index, pair in enumerate(small)]
    for copy in small:
        copy.start()
    barrier = pltpu.get_barrier_semaphore()
    for shift in shifts:
        if shift != (0, 0):
            pl.semaphore_signal(barrier, inc=1, device_id=partner(shift), device_id_type=MESH)
    pl.semaphore_signal(barrier, inc=1, device_id=other, device_id_type=MESH)

    for copy in small:
        copy.wait()
    slots = positions.shape[1]
    live = (lax.broadcasted_iota(jnp.int32, (1, slots), 1) < counts[0]).astype(jnp.int32)
    words = [positions[0:1, :], positions[1:2, :], positions[2:3, :], species[...].reshape(1, slots), live]
    words.append(jnp.zeros((1, lanes - 5 * slots), jnp.int32))
    info[...] = jnp.concatenate(words, axis=1)
    pl.semaphore_wait(barrier, slabs * rows)

    def remote(source, place, send, recv, device):
        copy = pltpu.make_async_remote_copy(
            src_ref=source,
            dst_ref=place,
            send_sem=send,
            recv_sem=recv,
            device_id=device,
            device_id_type=MESH,
        )
        copy.start()
        return copy

    def local(source, place, sem):
        copy = pltpu.make_async_copy(source, place, sem)
        copy.start()
        return copy

    first = [
        local(potential, got.at[1, me], local_sem.at[1]),
        local(info, atoms_out.at[col, me], local_sem.at[2]),
    ]
    for r in range(1, rows):
        device = partner((0, r))
        first.append(remote(potential, got.at[1, me], part_send.at[0, r], part_recv.at[0, r], device))
        first.append(remote(info, atoms_out.at[col, me], part_send.at[1, r], part_recv.at[1, r], device))
    moves = {}
    for index, shift in enumerate(shifts):
        if shift == (0, 0):
            moves[shift] = local(wave.at[me], got.at[0, me], local_sem.at[0])
        else:
            device = partner(shift)
            target = device[0] * rows + device[1]
            moves[shift] = remote(wave.at[target], got.at[0, me], send_sem.at[index], recv_sem.at[index], device)
    for copy in first:
        copy.wait()
    run = pl.ds(slab * rows, rows)
    second = []
    for s in range(1, slabs):
        device = partner((s, 0))
        second.append(remote(got.at[1, run], got.at[1, run], part_send.at[2, s], part_recv.at[2, s], device))
        second.append(
            remote(atoms_out.at[col, run], atoms_out.at[col, run], part_send.at[3, s], part_recv.at[3, s], device)
        )
    build_tables(offsets, beta, tables)
    build_matrices(matrices)
    kinds = beta.shape[0]
    for kind in range(kinds):
        strengths[kind] = jnp.full((1, lanes), 1.0 / half_width, jnp.float32) * coupling[kind]
    strengths[kinds] = jnp.zeros((1, lanes), jnp.float32)
    for copy in second:
        copy.wait()

    own_at = pl.multiple_of(col * margin, margin)
    from_at = pl.multiple_of(col * margin + (1 - col) * (depth - margin), margin)
    to_at = pl.multiple_of(col * depth, margin)

    def turn(kind, out, part):
        for half in range(2):
            tiles = [
                got[kind, part * rows + r, half * per_group + x] for x in range(per_group) for r in range(rows)
            ]
            out[part * 2 + half, pl.ds(own_at, depth), :] = jnp.concatenate(tiles, axis=0).T

    def pass_on(out, part, size, index):
        source = out.at[pl.ds(part * 2, size), pl.ds(from_at, margin), :]
        place = out.at[pl.ds(part * 2, size), pl.ds(to_at, margin), :]
        return remote(source, place, pair_send.at[index], pair_recv.at[index], other)

    last = [remote(atoms_out.at[col], atoms_out.at[col], pair_send.at[0], pair_recv.at[0], other)]
    for part in range(slabs):
        turn(1, potential_out, part)
    last.append(pass_on(potential_out, 0, groups, 1))
    for order, s in enumerate((1, 2, 3, 0)):
        for r in range(rows):
            moves[(s, r)].wait()
        part = lax.rem(slab + (slabs - s), slabs)
        turn(0, field_out, part)
        last.append(pass_on(field_out, part, 2, 2 + order))
    for copy in last:
        copy.wait()


def plane_part(source, matrices, plane, high, low, window):
    inner = pl.ds(low_rows, window)
    for tile in range(groups // 2):
        wide = jnp.concatenate(
            [source[low_groups + 2 * tile, inner], source[low_groups + 2 * tile + 1, inner]], axis=1
        )
        big = wide.astype(jnp.bfloat16)
        high[pl.ds(tile * window, window)] = big
        low[pl.ds(tile * window, window)] = (wide - big.astype(jnp.float32)).astype(jnp.bfloat16)
    total = groups // 2 * window

    def product(part, which, begin, end):
        return jnp.dot(part[begin:end], matrices[which], preferred_element_type=jnp.float32)

    def triple(which, begin, end):
        return (
            product(high, which, begin, end)
            + product(low, which, begin, end)
            + product(high, which + 1, begin, end)
        )

    plane[...] = triple(0, 0, total)
    plane[window:] += triple(2, 0, total - window)
    plane[: total - window] += triple(4, window, total)


def local_part(source, potential, plane, part, half, window):
    group = 2 * part + half
    padded = low_groups + group
    diagonal = (potential[group] - (centre + 1.5 * stencil_weights[0])) / half_width
    value = diagonal * source[padded, pl.ds(low_rows, window)]
    for reach in range(1, 7):
        value = value + (-0.5 / half_width * stencil_weights[reach]) * (
            source[padded, pl.ds(low_rows + reach, window)] + source[padded, pl.ds(low_rows - reach, window)]
        )
    at = part * window
    if not isinstance(part, int):
        at = pl.multiple_of(at, 32)
    return value + plane[pl.ds(at, window), half * lanes : (half + 1) * lanes]


def filter_kernel(
    depth, atoms, field, potential, tables, matrices, strengths, ping, pong,
    plane, high, low, shapes, listed, found,
):
    window = field.shape[1]
    slots = 8
    col = lax.axis_index("col")
    window_start = col * (depth - margin)
    inner = pl.ds(low_rows, window)

    def clear_rims(ref):
        ref[:low_groups] = jnp.zeros((low_groups,) + ref.shape[1:], jnp.float32)
        ref[low_groups + groups :] = jnp.zeros((low_groups,) + ref.shape[1:], jnp.float32)
        middle = pl.ds(low_groups, groups)
        ref[middle, :low_rows] = jnp.zeros((groups, low_rows, lanes), jnp.float32)
        ref[middle, low_rows + window :] = jnp.zeros((groups, low_rows, lanes), jnp.float32)

    clear_rims(ping)
    ping[pl.ds(low_groups, groups), inner] = field[...]

    lane_y = lax.broadcasted_iota(jnp.int32, (4 * box, lanes), 1) % side

    def find(block, count):
        for place in range(slots):
            local = atoms[block, 0, 2 * slots + place] - window_start
            live = atoms[block, 0, 4 * slots + place]
            listed[count] = block * slots + place
            count = count + jnp.where((local >= -5) & (local <= window + 4), live, 0)
        return count

    def gather(source, index, scale):
        gains = []
        for extra in range(unroll):
            atom = index * unroll + extra
            group, at = found[0, atom], found[1, atom]
            total = jnp.zeros((box, lanes), jnp.float32)
            for part in range(4):
                total = total + source[group + part, pl.ds(at, box)] * shapes[atom, pl.ds(part * box, box)]
            summed = jnp.sum(jnp.sum(total, axis=0, keepdims=True), axis=1, keepdims=True)
            gains.append(summed * (strengths[found[2, atom]] * scale))
        return tuple(gains)

    def scatter(target, index, gains):
        for extra in range(unroll):
            atom = index * unroll + extra
            group, at = found[0, atom], found[1, atom]
            for part in range(4):
                target[group + part, pl.ds(at, box)] += gains[extra] * shapes[atom, pl.ds(part * box, box)]

    def project(source, target, scale):
        def batch(index, gains):
            later = gather(source, index, scale)
            scatter(target, index - 1, gains)
            return later

        gains = lax.fori_loop(1, batches, batch, gather(source, 0, scale))
        scatter(target, batches - 1, gains)

    def stencil_step(source, target, scale, keep, between=None):
        plane_part(source, matrices, plane, high, low, window)
        for part in range(groups // 2):
            for half in range(2):
                padded = low_groups + 2 * part + half
                value = local_part(source, potential, plane, part, half, window)
                if keep:
                    value = scale * value - target[padded, inner]
                target[padded, inner] = value
                if between is not None:
                    between(2 * part + half)

    counts = [jnp.int32(0)]
    share = atoms.shape[0] // groups

    def find_some(index):
        for block in range(index * share, (index + 1) * share):
            counts.append(find(block, counts[-1]))

    stencil_step(ping, pong, 1.0, False, find_some)
    count = counts[-1]
    for extra in range(unroll):
        listed[count + extra] = 0
    batches = jnp.maximum((count + unroll - 1) // unroll, 1)

    def shape_batch(index, carry):
        for extra in range(unroll):
            atom = index * unroll + extra
            slot = listed[atom]
            block, place = slot // slots, lax.rem(slot, slots)
            x, y, z, kind = (atoms[block, 0, word * slots + place] for word in range(4))
            found[0, atom] = (x + 3) // per_group
            found[1, atom] = jnp.clip(z - window_start, -5, window + 4) - 5 + low_rows
            found[2, atom] = jnp.where(atom < count, kind, strengths.shape[0] - 1)
            start = y - 5
            table = tables[kind * per_group + lax.rem(x + 3, per_group)]
            rolled = pltpu.roll(table, lax.rem(start + lanes, lanes), 1)
            shapes[atom] = jnp.where((lane_y >= start) & (lane_y <= start + 10), rolled, 0.0)
        return carry

    lax.fori_loop(0, batches, shape_batch, 0)

    project(ping, pong, 1.0)
    clear_rims(pong)
    stencil_step(pong, ping, 2.0, True)
    project(pong, ping, 2.0)
    clear_rims(ping)
    middle = pl.ds(low_groups, groups)
    pong[middle, inner] = -pong[middle, inner]
    project(ping, pong, 2.0)


def collect_kernel(
    shape, cells, source, rest, potential, matrices, block, gram,
    plane, high, low, turning, pieces, gram_high, gram_low, partial, sums, local_sem, send_sem, recv_sem, sum_send, sum_recv,
):
    slabs, rows, cols = shape
    bands, _, _, depth = block.shape
    window = potential.shape[1]
    devices = slabs * rows * cols
    slab, row, col = (lax.axis_index(name) for name in ("slab", "row", "col"))
    me = slab * rows + row
    mine = me * cols + col

    def partner(step):
        target = lax.rem(mine + step, devices)
        return (target // (rows * cols), lax.rem(target // cols, rows), lax.rem(target, cols))

    barrier = pltpu.get_barrier_semaphore()
    for step in range(1, devices):
        pl.semaphore_signal(barrier, inc=1, device_id=partner(step), device_id_type=MESH)
    plane_part(source, matrices, plane, high, low, window)
    begin = pl.multiple_of(col * margin, margin)
    copies = []
    for order, s in enumerate((1, 2, 3, 0)):
        part = lax.rem(slab + s, slabs)
        for half in range(2):
            padded = low_groups + 2 * part + half
            value = local_part(source, potential, plane, part, half, window)
            turning[half] = 2.0 * value + rest[padded, pl.ds(low_rows, window)]
            turned = turning[half, pl.ds(begin, depth), :].T
            for x in range(per_group):
                for r in range(rows):
                    at = (x * rows + r) * 8
                    pieces[part * rows + r, half * per_group + x] = turned[at : at + 8]
        if order == 0:
            pl.semaphore_wait(barrier, devices - 1)
        for r in range(rows):
            to_row = lax.rem(row + r, rows)
            target = part * rows + to_row
            if s == 0 and r == 0:
                copies.append(pltpu.make_async_copy(pieces.at[me], block.at[me], local_sem))
            else:
                copies.append(
                    pltpu.make_async_remote_copy(
                        src_ref=pieces.at[target],
                        dst_ref=block.at[me],
                        send_sem=send_sem.at[order * rows + r],
                        recv_sem=recv_sem.at[order * rows + r],
                        device_id=(part, to_row, col),
                        device_id_type=MESH,
                    )
                )
            copies[-1].start()
    size_x, size_y = block.shape[1:3]
    flat = bands * size_y
    some = rows * size_y
    for order, s in enumerate((1, 2, 3, 0)):
        for copy in copies[order * rows : (order + 1) * rows]:
            copy.wait()
        part = lax.rem(slab + (slabs - s), slabs)
        at = pl.ds(pl.multiple_of(part * some, some), some)
        for x in range(size_x):
            value = block[pl.ds(part * rows, rows), x].reshape(some, lanes)
            big = value.astype(jnp.bfloat16)
            gram_high[at, x * lanes : (x + 1) * lanes] = big
            gram_low[at, x * lanes : (x + 1) * lanes] = (value - big.astype(jnp.float32)).astype(jnp.bfloat16)
    product = lax.dot_general(
        gram_high[...],
        jnp.concatenate([gram_high[...], gram_low[...]], axis=0),
        (((1,), (1,)), ((), ())),
        preferred_element_type=jnp.float32,
    )
    cross = product[:, flat:]
    product = product[:, :flat] + cross + cross.T
    one = lax.broadcasted_iota(jnp.int32, (flat, flat), 0)
    two = lax.broadcasted_iota(jnp.int32, (flat, flat), 1)
    product = jnp.where(one % size_y == two % size_y, product, 0.0)
    product = jnp.sum(product.reshape(bands, size_y, flat), axis=1)

    def times(value, picks):
        parts = jnp.concatenate(split_three(value), axis=0).astype(jnp.bfloat16)
        result = jnp.dot(parts, picks.astype(jnp.bfloat16), preferred_element_type=jnp.float32)
        return result[:bands] + result[bands : 2 * bands] + result[2 * bands :]

    folded = times(product, (one // size_y == two % bands).astype(jnp.float32))
    packed = (2, bands // 2, lanes)
    keep = lax.broadcasted_iota(jnp.int32, packed, 1) == lax.broadcasted_iota(jnp.int32, packed, 2) // bands
    partial[...] = jnp.sum(jnp.where(keep, folded.reshape(packed), 0.0), axis=1)
    sums[mine] = partial[...]
    copies = []
    for step in range(1, devices):
        copies.append(
            pltpu.make_async_remote_copy(
                src_ref=partial,
                dst_ref=sums.at[mine],
                send_sem=sum_send.at[step],
                recv_sem=sum_recv.at[step],
                device_id=partner(step),
                device_id_type=MESH,
            )
        )
    for copy in copies:
        copy.start()
    for copy in copies:
        copy.wait()
    total = jnp.sum(sums[...], axis=0) * (1.0 / cells)
    total = jnp.where(keep, jnp.broadcast_to(total[:, None, :], packed), 0.0).reshape(bands, lanes)
    gram[...] = times(total, (one % bands == two).astype(jnp.float32))[:, :bands]


def band_shards(shape, wave, potential, positions, species, counts, offsets, beta, coupling):
    slabs, rows, cols = shape
    bands, size_x, size_y, size_z = wave.shape
    slots = positions.shape[1]
    window = size_z + margin
    vmem = pl.BlockSpec(memory_space=pltpu.VMEM)
    smem = pl.BlockSpec(memory_space=pltpu.SMEM)
    hbm = pl.BlockSpec(memory_space=pltpu.HBM)
    dma = pltpu.SemaphoreType.DMA
    table_count = beta.shape[0] * per_group
    matrices_shape = jax.ShapeDtypeStruct((6, 2 * lanes, 2 * lanes), jnp.bfloat16)
    offsets = offsets.transpose(1, 0, 2)
    held = (wave, potential, positions, species, counts, offsets, beta, coupling)
    held = [a if a is counts else pltpu.with_memory_space_constraint(a, pltpu.HBM) for a in held]
    field, wide_potential, atoms, tables, matrices, strengths = pl.pallas_call(
        lambda *refs: spread_kernel(shape, *refs),
        out_shape=(
            jax.ShapeDtypeStruct((groups, window, lanes), jnp.float32),
            jax.ShapeDtypeStruct((groups, window, lanes), jnp.float32),
            jax.ShapeDtypeStruct((cols, bands, 1, lanes), jnp.int32),
            jax.ShapeDtypeStruct((table_count, 4 * box, lanes), jnp.float32),
            matrices_shape,
            jax.ShapeDtypeStruct((beta.shape[0] + 1, 1, lanes), jnp.float32),
        ),
        in_specs=[hbm] * 4 + [smem] + [hbm] * 3,
        out_specs=[vmem] * 6,
        scratch_shapes=[
            pltpu.VMEM(positions.shape, jnp.int32),
            pltpu.VMEM(species.shape, jnp.int32),
            pltpu.VMEM(offsets.shape, jnp.int32),
            pltpu.VMEM(beta.shape, jnp.float32),
            pltpu.SMEM(coupling.shape, jnp.float32),
            dma((5,)),
            pltpu.VMEM((2, bands, size_x, size_y, size_z), jnp.float32),
            pltpu.VMEM((1, lanes), jnp.int32),
            dma((3,)),
            dma((bands,)),
            dma((bands,)),
            dma((4, 4)),
            dma((4, 4)),
            dma((6,)),
            dma((6,)),
        ],
        compiler_params=pltpu.CompilerParams(
            collective_id=0, has_side_effects=True, vmem_limit_bytes=32 * 2**20
        ),
        name="spread",
    )(*held)

    most = bands * cols * slots + unroll
    padded = jax.ShapeDtypeStruct((groups + 2 * low_groups, window + 2 * low_rows, lanes), jnp.float32)
    plane_scratch = [
        pltpu.VMEM((groups // 2 * window, 2 * lanes), jnp.float32),
        pltpu.VMEM((groups // 2 * window, 2 * lanes), jnp.bfloat16),
        pltpu.VMEM((groups // 2 * window, 2 * lanes), jnp.bfloat16),
    ]
    second, rest = pl.pallas_call(
        lambda *refs: filter_kernel(size_z, *refs),
        out_shape=(padded, padded),
        in_specs=[smem] + [vmem] * 5,
        out_specs=[vmem] * 2,
        scratch_shapes=plane_scratch
        + [
            pltpu.VMEM((most, 4 * box, lanes), jnp.float32),
            pltpu.SMEM((most,), jnp.int32),
            pltpu.SMEM((3, most), jnp.int32),
        ],
        compiler_params=pltpu.CompilerParams(vmem_limit_bytes=40 * 2**20),
        name="chebyshev",
    )(atoms.reshape(cols * bands, 1, lanes), field, wide_potential, tables, matrices, strengths)

    devices = slabs * rows * cols
    cells = devices * size_x * size_y * size_z
    filtered, gram = pl.pallas_call(
        lambda *refs: collect_kernel(shape, cells, *refs),
        out_shape=(
            jax.ShapeDtypeStruct(wave.shape, jnp.float32),
            jax.ShapeDtypeStruct((bands, bands), jnp.float32),
        ),
        in_specs=[vmem] * 4,
        out_specs=[vmem] * 2,
        scratch_shapes=plane_scratch
        + [
            pltpu.VMEM((2, window, lanes), jnp.float32),
            pltpu.VMEM(wave.shape, jnp.float32),
            pltpu.VMEM((bands * size_y, size_x * lanes), jnp.bfloat16),
            pltpu.VMEM((bands * size_y, size_x * lanes), jnp.bfloat16),
            pltpu.VMEM((2, lanes), jnp.float32),
            pltpu.VMEM((devices, 2, lanes), jnp.float32),
            dma,
            dma((bands,)),
            dma((bands,)),
            dma((devices,)),
            dma((devices,)),
        ],
        compiler_params=pltpu.CompilerParams(
            collective_id=1, has_side_effects=True, vmem_limit_bytes=32 * 2**20
        ),
        name="collect",
    )(second, rest, wide_potential, matrices)
    return filtered, gram


def solution(mesh):
    in_specs = (
        P(None, "slab", "row", "col"),
        P("slab", "row", "col"),
        P(None, ("slab", "row", "col")),
        P(("slab", "row", "col")),
        P(("slab", "row", "col")),
        P(),
        P(),
        P(),
    )
    out_specs = (P(None, "slab", "row", "col"), P())
    shape = tuple(mesh.shape[name] for name in ("slab", "row", "col"))

    def run(*arrays):
        bands, size_x, size_y, size_z = arrays[0].shape
        one_band_a_chip = (
            shape[0] * shape[1] == bands
            and shape[2] == 2
            and (size_x, size_y, size_z) == (shape[0] * 8, shape[1] * 8, 2 * lanes)
            and (size_x, size_y) == (side, side)
            and arrays[2].shape[1] == 8 * mesh.size
        )
        body = (lambda *blocks: band_shards(shape, *blocks)) if one_band_a_chip else shards
        return jax.shard_map(
            body, mesh=mesh, in_specs=in_specs, out_specs=out_specs, check_vma=False
        )(*arrays)

    return run
```
